256 devices in a mesh: morton: 64 (over x, z, core), sib: 4 (over y).
Axes of the slice: x: 4, y: 4, z: 8, core: 2. Of those that a mesh axis runs over, the one named last changes fastest.
Arguments:
- velocity: bfloat16 [32768, 3, 512], P(('morton', 'sib')), may hold values from -6 to 6
- pressure: bfloat16 [32768, 512], P(('morton', 'sib')), may hold values from -96 to 96
- viscosity: float32 [32768, 512], P(('morton', 'sib')), may hold values from 0.25 to 8
- levels: int32 [32768], P(('morton', 'sib')), may hold values from 3 to 7
- morton_keys: int32 [32768], P(('morton', 'sib')), may hold values from 0 to 2097151, as said below
- counts: int32 [256], replicated, may hold values from 32 to 128, as said below
- neighbors: int32 [32768, 6], P(('morton', 'sib')), may hold values from -1 to 32767, as said below
Outputs:
- stokes_force: float32 [32768, 3, 512], P(('morton', 'sib'))
- continuity: float32 [32768, 512], P(('morton', 'sib'))
- box_multipoles: float32 [64, 3, 216], P('morton')
- root_multipole: float32 [64, 3, 216], P('morton')
The draws below stay inside these ranges and needn't reach their ends.
Inputs may be any that keep to these rules, and one draw needn't show every extreme that they name: counts[r] live leaves occupy slots 0 to counts[r] - 1 of range r; some range is full in every draw. `morton_keys`: the key of a leaf of range r lies in that range's key block. `neighbors`: -1 marks the domain's boundary and every face of a padded slot. Otherwise the entry is a live leaf of the same Morton index m (any range), or one of the last 32 live leaves of a range of Morton index m - 1, or one of the first 32 leaves of a range of Morton index m + 1; in every draw the outermost leaf of both bands is referenced for every m that has such a neighbour.
All inputs are finite; a program needn't handle non-finite values.
Results may differ from the reference program's by a relative error of at most 0.0068.
Values may be sent and summed in bfloat16 or wider, within the bound.
A program may use at most 64 MiB of HBM per device.

```python
import math
import jax
import jax.numpy as jnp
import numpy as np
from jax import lax

LEAF_DEV = 128
NODES = 512
DEG = 5
LMAX = 7
LMIN = 3
MOMENTS = 216
TOTAL = 32768
N_MORTON = 64
N_SIB = 4


def range_loads(key):
    ranges = TOTAL // LEAF_DEV
    quarter = LEAF_DEV // 4
    draw_ticks = jax.random.randint(key, (ranges,), 0, 65)
    leaf_loads = quarter + 3 * quarter * draw_ticks * draw_ticks // 4096
    fullest = jax.random.randint(jax.random.fold_in(key, 99), (), 0, ranges)
    return jnp.where(jnp.arange(ranges) == fullest, LEAF_DEV, leaf_loads).astype(jnp.int32)


def draw_counts(key, part):
    leaf_loads = range_loads(key)
    return leaf_loads


def draw_morton_keys(key, part):
    key = jax.random.fold_in(key, 7)
    ranges = TOTAL // LEAF_DEV
    key_range = (1 << 3 * LMAX) // ranges
    leaf_ids = jnp.arange(TOTAL, dtype=jnp.int32)
    offsets = jax.random.randint(key, (TOTAL,), 0, key_range)
    return (leaf_ids // LEAF_DEV * key_range + offsets).astype(jnp.int32)


def draw_neighbors(key, part):
    leaf_loads = range_loads(key)
    key = jax.random.fold_in(key, 5)
    ranges = TOTAL // LEAF_DEV
    mortons = ranges // N_SIB
    edge_rows = LEAF_DEV // 4
    leaf_ids = jnp.arange(TOTAL, dtype=jnp.int32)
    own_range = leaf_ids // LEAF_DEV
    slot_ids = leaf_ids % LEAF_DEV
    live_leaf = slot_ids < leaf_loads[own_range]
    keys_split = jax.random.split(key, 3)
    face_kinds = jax.random.randint(keys_split[0], (TOTAL, 6), 0, 6)
    target_sib = jax.random.randint(keys_split[1], (TOTAL, 6), 0, N_SIB)
    raw_slot = jax.random.randint(keys_split[2], (TOTAL, 6), 0, 1 << 20)
    morton_col = (own_range // N_SIB)[:, None]
    lower_ok = morton_col >= 1
    upper_ok = morton_col <= mortons - 2
    go_lower = (face_kinds == 3) & lower_ok
    go_upper = (face_kinds == 4) & upper_ok
    go_same = face_kinds <= 2
    target_morton = jnp.where(go_lower, morton_col - 1, jnp.where(go_upper, morton_col + 1, morton_col))
    target_range = target_morton * N_SIB + target_sib
    target_load = leaf_loads[target_range]
    target_slot = jnp.where(go_lower, target_load - edge_rows + raw_slot % edge_rows, jnp.where(go_upper, raw_slot % edge_rows, raw_slot % target_load))
    chosen = jnp.where(go_same | go_lower | go_upper, target_range * LEAF_DEV + target_slot, -1)
    first_leaf = (slot_ids == 0) & (own_range % N_SIB == 0)
    face_ids = jnp.arange(6)[None, :]
    force_low = first_leaf[:, None] & (face_ids == 0) & lower_ok
    force_up = first_leaf[:, None] & (face_ids == 1) & upper_ok
    low_range = jnp.clip((morton_col - 1) * N_SIB + (N_SIB - 1), 0, ranges - 1)
    low_target = low_range * LEAF_DEV + leaf_loads[low_range] - edge_rows
    up_target = (morton_col + 1) * N_SIB * LEAF_DEV + edge_rows - 1
    chosen = jnp.where(force_low, low_target, jnp.where(force_up, up_target, chosen))
    return jnp.where(live_leaf[:, None], chosen, -1).astype(jnp.int32)


def set_ends(entries, stream_key, smallest, top_value):
    dims = entries.shape
    spot = [jax.random.randint(jax.random.fold_in(stream_key, axis), (), 0, dims[axis]) for axis in range(len(dims))]
    entries = entries.at[tuple(spot)].set(smallest)
    longest = dims.index(max(dims))
    spot[longest] = (spot[longest] + 1) % dims[longest]
    return entries.at[tuple(spot)].set(top_value)


def shard_levels(key, dims, cuts, least, largest):
    def one(axis_at, blocks):
        steps = jax.random.uniform(jax.random.fold_in(jax.random.fold_in(key, 6), axis_at), (blocks,), jnp.float32, least / len(cuts), largest / len(cuts))
        return jnp.repeat(jnp.exp(steps), dims[axis_at] // blocks).reshape((-1,) + (1,) * (len(dims) - axis_at - 1))

    gain = one(*cuts[0])
    for cut in cuts[1:]:
        gain = gain * one(*cut)
    return gain


def gaussian(rng, dims, deviation, limit, cuts=(), held_as=jnp.bfloat16):
    factor_of = shard_levels(rng, dims, cuts, -0.22, 0.18) if cuts else 1.0
    values = jax.random.normal(rng, dims, jnp.float32) * deviation * factor_of
    return jnp.minimum(jnp.maximum(values, -limit), limit).astype(held_as)


def setup_inputs(seed: int = 0) -> dict:
    keys = jax.random.split(jax.random.key(seed), 8)
    return {
        "velocity": gaussian(keys[0], (TOTAL, 3, NODES), 1.0, 6.0, ((0, 256),)),
        "pressure": gaussian(keys[1], (TOTAL, NODES), 16.0, 96.0, ((0, 256),)),
        "viscosity": jnp.clip(jnp.exp(math.log(8.0) - 3.465736 * jax.random.uniform(keys[2], (TOTAL, NODES), jnp.float32) ** shard_levels(keys[2], (TOTAL, NODES), ((0, 256),), -0.2, 0.2)), 0.25, 8.0),
        "levels": set_ends(jax.random.randint(keys[3], (TOTAL,), LMIN, LMAX + 1), jax.random.fold_in(keys[3], 1), LMIN, LMAX).astype(jnp.int32),
        "morton_keys": draw_morton_keys(jax.random.fold_in(keys[7], 71), 0),
        "counts": draw_counts(jax.random.fold_in(keys[7], 71), 0),
        "neighbors": draw_neighbors(jax.random.fold_in(keys[7], 71), 0),
    }


penalty = 256.0
out_scale = 1.0 / 1024.0
mass_scale = 1.0 / 32.0
highest = lax.Precision.HIGHEST


def cheb_matrix():
    points = -np.cos(np.pi * np.arange(8) / 7.0)
    bary_weights = np.array([(-1.0) ** node_idx for node_idx in range(8)])
    bary_weights[0] = bary_weights[0] * 0.5
    bary_weights[7] = bary_weights[7] * 0.5
    derivative = np.zeros((8, 8))
    for row_idx in range(8):
        for col_idx in range(8):
            if row_idx != col_idx:
                derivative[row_idx, col_idx] = (bary_weights[col_idx] / bary_weights[row_idx]) / (points[row_idx] - points[col_idx])
        derivative[row_idx, row_idx] = -np.sum(derivative[row_idx])
    return points, derivative


def face_nodes():
    node_list = []
    for face_idx in range(6):
        face_dim = face_idx // 2
        face_side = face_idx % 2
        for first_idx in range(8):
            for second_idx in range(8):
                coords = [first_idx, second_idx]
                coords.insert(face_dim, 7 * face_side)
                node_list.append(64 * coords[0] + 8 * coords[1] + coords[2])
    return np.array(node_list, dtype=np.int32)


def derivative_along(nodal_field, diff_matrix, dim_idx):
    forms = ['...abc,Aa->...Abc', '...abc,Bb->...aBc', '...abc,Cc->...abC']
    return jnp.einsum(forms[dim_idx], nodal_field, diff_matrix, precision=highest)


def power_table(values):
    power_terms = [jnp.ones_like(values)]
    for power_idx in range(DEG):
        power_terms.append(power_terms[-1] * values)
    return jnp.stack(power_terms, axis=-1)


def leaf_geometry(morton_keys, levels):
    shift_bits = 3 * (LMAX - levels)
    anchor = jnp.left_shift(jnp.right_shift(morton_keys, shift_bits), shift_bits)
    leaf_span = jnp.left_shift(jnp.ones_like(levels), LMAX - levels).astype(jnp.float32)
    finest = 1.0 / float(2 ** LMAX)
    cell_coords = []
    for offset in (2, 1, 0):
        coordinate = jnp.zeros_like(anchor)
        for bit_idx in range(LMAX):
            coordinate = coordinate + jnp.left_shift(jnp.bitwise_and(jnp.right_shift(anchor, 3 * bit_idx + offset), 1), bit_idx)
        cell_coords.append((coordinate.astype(jnp.float32) + 0.5 * leaf_span) * finest)
    return jnp.stack(cell_coords, axis=-1), 0.5 * leaf_span * finest


def box_geometry(base_key, key_bits):
    finest = 1.0 / float(2 ** LMAX)
    centers = []
    side_lengths = []
    for offset in (2, 1, 0):
        free_bits = max(0, min(LMAX, (key_bits - offset + 2) // 3))
        coordinate = jnp.zeros_like(base_key)
        for bit_idx in range(LMAX):
            coordinate = coordinate + jnp.left_shift(jnp.bitwise_and(jnp.right_shift(base_key, 3 * bit_idx + offset), 1), bit_idx)
        side_len = float(2 ** free_bits) * finest
        centers.append(coordinate.astype(jnp.float32) * finest + 0.5 * side_len)
        side_lengths.append(side_len)
    return jnp.stack(centers), 0.5 * max(side_lengths)


def moments(forces, centers, radius, box_center, box_scale, points):
    leaf_count = forces.shape[0]
    nodal_field = forces.reshape(leaf_count, 3, 8, 8, 8)
    tables = []
    for dim_idx in range(3):
        position = centers[:, dim_idx][:, None] + radius[:, None] * points[None, :]
        tables.append(power_table((position - box_center[dim_idx]) / box_scale))
    step_one = jnp.einsum('liabc,lcz->liabz', nodal_field, tables[2], precision=highest)
    step_two = jnp.einsum('liabz,lby->liayz', step_one, tables[1], precision=highest)
    moment_sum = jnp.einsum('liayz,lax->ixyz', step_two, tables[0], precision=highest)
    return (moment_sum / 512.0).reshape(3, MOMENTS)


def leaf_forces(vel_rows, press_rows, visc_rows, nbr_faces, live_rows, diff_matrix, node_list):
    leaf_count = vel_rows.shape[0]
    nodal_field = vel_rows.astype(jnp.float32).reshape(leaf_count, 3, 8, 8, 8)
    gradient = jnp.stack([derivative_along(nodal_field, diff_matrix, dim_idx) for dim_idx in range(3)], axis=2).reshape(leaf_count, 3, 3, 512)
    press_field = press_rows.astype(jnp.float32).reshape(leaf_count, 8, 8, 8)
    press_grad = jnp.stack([derivative_along(press_field, diff_matrix, dim_idx) for dim_idx in range(3)], axis=1).reshape(leaf_count, 3, 512)
    stress = (visc_rows[:, None, None, :] * (gradient + jnp.swapaxes(gradient, 1, 2))).astype(jnp.bfloat16)
    stress_field = stress.astype(jnp.float32).reshape(leaf_count, 3, 3, 8, 8, 8)
    divergence = derivative_along(stress_field[:, :, 0], diff_matrix, 0) + derivative_along(stress_field[:, :, 1], diff_matrix, 1) + derivative_along(stress_field[:, :, 2], diff_matrix, 2)
    divergence = divergence.reshape(leaf_count, 3, 512)
    own_faces = vel_rows.astype(jnp.float32)[:, :, node_list]
    face_jump = jnp.zeros((leaf_count, 3, 512), jnp.float32).at[:, :, node_list].add(own_faces - nbr_faces)
    momentum = (penalty * visc_rows[:, None, :] * face_jump - divergence + press_grad) * out_scale
    mass_rows = -(gradient[:, 0, 0] + gradient[:, 1, 1] + gradient[:, 2, 2]) * mass_scale
    return jnp.where(live_rows[:, None, None], momentum, 0.0), jnp.where(live_rows[:, None], mass_rows, 0.0)


def reference(velocity, pressure, viscosity, levels, morton_keys, counts, neighbors):
    points_np, derivative_np = cheb_matrix()
    points = jnp.asarray(points_np.astype(np.float32)).astype(jnp.float32)
    rounded = lax.optimization_barrier(jnp.asarray(derivative_np.astype(np.float32)).astype(jnp.bfloat16))
    diff_matrix = rounded.astype(jnp.float32)
    node_list = face_nodes()
    opposite = velocity[:, :, node_list].reshape(TOTAL, 3, 6, 64).transpose(2, 0, 1, 3)
    key_range = 2 ** (3 * LMAX) // (N_MORTON * N_SIB)
    box_bits = 3 * LMAX - (N_MORTON.bit_length() - 1)
    group_leaves = N_SIB * LEAF_DEV
    root_center = jnp.full((3,), 0.5, jnp.float32)

    def per_box(morton_idx):
        first_leaf = morton_idx * group_leaves
        vel_rows = lax.dynamic_slice_in_dim(velocity, first_leaf, group_leaves, 0)
        press_rows = lax.dynamic_slice_in_dim(pressure, first_leaf, group_leaves, 0)
        visc_rows = lax.dynamic_slice_in_dim(viscosity, first_leaf, group_leaves, 0)
        level_rows = lax.dynamic_slice_in_dim(levels, first_leaf, group_leaves, 0)
        key_rows = lax.dynamic_slice_in_dim(morton_keys, first_leaf, group_leaves, 0)
        nbr_rows = lax.dynamic_slice_in_dim(neighbors, first_leaf, group_leaves, 0)
        leaf_ids = first_leaf + jnp.arange(group_leaves, dtype=jnp.int32)
        live_rows = (leaf_ids % LEAF_DEV) < jnp.take(counts, leaf_ids // LEAF_DEV)
        fetched = []
        for face_idx in range(6):
            target = nbr_rows[:, face_idx]
            rows_got = jnp.take(opposite[face_idx ^ 1], jnp.clip(target, 0, TOTAL - 1), axis=0)
            fetched.append(jnp.where((target >= 0)[:, None, None], rows_got, jnp.zeros_like(rows_got)))
        nbr_faces = jnp.stack(fetched, axis=2).reshape(group_leaves, 3, 384).astype(jnp.float32)
        forces, masses = leaf_forces(vel_rows, press_rows, visc_rows, nbr_faces, live_rows, diff_matrix, node_list)
        centers, radius = leaf_geometry(key_rows, level_rows)
        box_center, box_scale = box_geometry(morton_idx * (N_SIB * key_range), box_bits)
        box_part = moments(forces, centers, radius, box_center, box_scale, points)
        root_part = moments(forces, centers, radius, root_center, 0.5, points)
        return forces, masses, box_part, root_part

    forces, masses, box_parts, root_parts = lax.map(per_box, jnp.arange(N_MORTON, dtype=jnp.int32))
    root_total = jnp.sum(root_parts, axis=0)
    root_copies = jnp.broadcast_to(root_total[None], (N_MORTON, 3, MOMENTS))
    return forces.reshape(TOTAL, 3, NODES), masses.reshape(TOTAL, NODES), box_parts, root_copies
```

```python
import functools
import math

import jax
import jax.numpy as jnp
import numpy as np
from jax import lax
from jax.experimental import pallas as pl
from jax.experimental.pallas import tpu as pltpu
from jax.sharding import PartitionSpec as P

DEG = 5
LMAX = 7
MOMENTS = 216
LEAVES = 128
NODES = 512
LANES = 896
BAND = 32
TILE = 128
MESH = pl.DeviceIdType.MESH
F32 = jnp.float32
BF16 = jnp.bfloat16

penalty = 256.0
out_scale = 1.0 / 1024.0
mass_scale = 1.0 / 32.0

X_SIZE, Z_SIZE, CORES, SIBS = 4, 8, 2, 4
ZC = Z_SIZE * CORES
MORTONS = X_SIZE * ZC


def cheb():
    points = -np.cos(np.pi * np.arange(8) / 7.0)
    weights = np.array([(-1.0) ** k for k in range(8)])
    weights[0] *= 0.5
    weights[7] *= 0.5
    derivative = np.zeros((8, 8))
    for row in range(8):
        for col in range(8):
            if row != col:
                derivative[row, col] = weights[col] / weights[row] / (points[row] - points[col])
        derivative[row, row] = -np.sum(derivative[row])
    return points, derivative


def node_of(coords):
    return 64 * coords[0] + 8 * coords[1] + coords[2]


def coords_of(node):
    return [node // 64, node // 8 % 8, node % 8]


def surface_lists():
    x_nodes = [node_of([7 * side, b, c]) for side in range(2) for b in range(8) for c in range(8)]
    rest = []
    for node in range(NODES):
        a, b, c = coords_of(node)
        if a not in (0, 7) and (b in (0, 7) or c in (0, 7)):
            rest.append(node)
    return x_nodes, rest


def tables():
    points, derivative = cheb()
    eye = np.eye(8)
    directional = [
        np.kron(np.kron(derivative, eye), eye),
        np.kron(np.kron(eye, derivative), eye),
        np.kron(np.kron(eye, eye), derivative),
    ]
    diff = np.stack([m.T for m in directional])
    x_nodes, rest = surface_lists()
    tail = len(rest) - TILE
    pick = np.zeros((NODES, 2 * TILE))
    for k, node in enumerate(rest):
        pick[node, k] = 1.0
    tiles = [list(x_nodes), list(rest[:TILE]), [-1] * TILE]
    for comp in range(3):
        for k in range(tail):
            tiles[2][tail * comp + k] = rest[TILE + k]
    spread = np.zeros((7 * TILE, NODES))
    masks = np.zeros((7, TILE))
    slot = 0
    for dim in range(3):
        for tile in range(3):
            if dim == 0 and tile > 0:
                continue
            for lane, node in enumerate(tiles[tile]):
                if node < 0:
                    continue
                coords = coords_of(node)
                if coords[dim] in (0, 7):
                    other = list(coords)
                    other[dim] = 7 - coords[dim]
                    spread[slot * TILE + lane, node_of(other)] = 1.0
                    masks[slot, lane] = 1.0 if coords[dim] == 7 else 0.0
            slot += 1
    mult = np.zeros((NODES,))
    for node in range(NODES):
        mult[node] = sum(1 for c in coords_of(node) if c in (0, 7))
    vander = np.zeros((288, NODES))
    for jx in range(6):
        for jy in range(6):
            for jz in range(6):
                for node in range(NODES):
                    a, b, c = coords_of(node)
                    vander[jx * 48 + jy * 8 + jz, node] = (
                        points[a] ** jx * points[b] ** jy * points[c] ** jz / 512.0
                    )
    small = np.zeros((26, 8, TILE))
    for k in range(6):
        for a in range(6):
            if a >= k:
                small[k, a, :] = math.comb(a, k)
        for lane in range(108):
            ay, az = lane // 6 % 6, lane % 6
            if ay >= k:
                small[6 + k, :, lane] = math.comb(ay, k)
            if az >= k:
                small[12 + k, :, lane] = math.comb(az, k)
    for ax in range(6):
        for lane in range(108):
            small[18, ax, lane] = BOX_IN_ROOT ** (ax + lane // 6 % 6 + lane % 6)
    for slot in range(7):
        small[19 + slot, :, :] = masks[slot][None, :]
    return diff, pick, spread, mult, vander, small, tail


BOX_CELLS = 2 ** ((3 * LMAX - 6) // 3)
FINEST = 1.0 / 2**LMAX
BOX_SIDE = BOX_CELLS * FINEST
BOX_SCALE = 0.5 * BOX_SIDE
BOX_IN_ROOT = BOX_SCALE / 0.5

VEL_IN, PRESS_IN, VISC_IN, PICK_IN, DIFF_IN, SPREAD_IN, VAND_IN, SMALL_IN = range(8)
QUARTER = LEAVES // 4


def dot(a, b):
    return jnp.dot(a, b, preferred_element_type=F32)


def dot_nt(a, b):
    return lax.dot_general(a, b, (((1,), (1,)), ((), ())), preferred_element_type=F32)


def split(value):
    high = value.astype(BF16)
    return high, (value - high.astype(F32)).astype(BF16)


def kernel(
    tail,
    counts_ref,
    levels_ref,
    keys_ref,
    nbr_ref,
    mult_ref,
    vel_hbm,
    press_hbm,
    visc_hbm,
    pick_hbm,
    diff_hbm,
    spread_hbm,
    vand_hbm,
    small_hbm,
    force_hbm,
    mass_hbm,
    box_ref,
    root_ref,
    field,
    visc,
    pick,
    diff,
    spread,
    vand,
    small,
    tab,
    high_band,
    low_band,
    band_out,
    grads,
    local,
    picked,
    force,
    mass,
    pos_sq,
    mcat,
    part,
    recv_a,
    recv_b,
    sum_a,
    in_sem,
    out_sem,
    ring_send,
    ring_recv,
    fwd_send,
    fwd_recv,
    high_send,
    high_recv,
    low_send,
    low_recv,
    a_send,
    a_recv,
    b_send,
    b_recv,
):
    m = lax.axis_index("morton")
    s = lax.axis_index("sib")
    x_at = lax.div(m, ZC)
    zc_at = lax.rem(m, ZC)
    up = {"sib": lax.rem(s + 1, SIBS)}
    down = {"sib": lax.rem(s + SIBS - 1, SIBS)}
    after = {"morton": lax.rem(m + 1, MORTONS)}
    before = {"morton": lax.rem(m + MORTONS - 1, MORTONS)}

    def place(device):
        return (device.get("morton", m), device.get("sib", s))

    def group_a(dx, dy):
        return (lax.rem(x_at + dx, X_SIZE) * ZC + zc_at, lax.rem(s + dy, SIBS))

    def group_b(dz):
        return (x_at * ZC + lax.rem(zc_at + dz, ZC), s)

    a_steps = [(dx, dy) for dx in range(X_SIZE) for dy in range(SIBS) if dx or dy]
    b_steps = list(range(1, ZC))

    barrier = pltpu.get_barrier_semaphore()
    for step in a_steps:
        pl.semaphore_signal(barrier, inc=1, device_id=group_a(*step), device_id_type=MESH)
    for step in b_steps:
        pl.semaphore_signal(barrier, inc=1, device_id=group_b(step), device_id_type=MESH)
    for device in (after, before):
        pl.semaphore_signal(barrier, inc=1, device_id=place(device), device_id_type=MESH)

    loads = [
        pltpu.make_async_copy(vel_hbm, field.at[pl.ds(0, 3)], in_sem.at[VEL_IN]),
        pltpu.make_async_copy(press_hbm, field.at[3], in_sem.at[PRESS_IN]),
        pltpu.make_async_copy(visc_hbm, visc, in_sem.at[VISC_IN]),
        pltpu.make_async_copy(pick_hbm, pick, in_sem.at[PICK_IN]),
        pltpu.make_async_copy(diff_hbm, diff, in_sem.at[DIFF_IN]),
        pltpu.make_async_copy(spread_hbm, spread, in_sem.at[SPREAD_IN]),
        pltpu.make_async_copy(vand_hbm, vand, in_sem.at[VAND_IN]),
        pltpu.make_async_copy(small_hbm, small, in_sem.at[SMALL_IN]),
    ]
    for which in (VEL_IN, PICK_IN, PRESS_IN, DIFF_IN, VISC_IN, SPREAD_IN, VAND_IN, SMALL_IN):
        loads[which].start()

    loads[VEL_IN].wait()
    loads[PICK_IN].wait()
    lane = lax.broadcasted_iota(jnp.int32, (LEAVES, TILE), 1)
    rest = dot(field[0:3].reshape(3 * LEAVES, NODES), pick[...])
    shared = jnp.zeros((LEAVES, TILE), F32)
    for comp in range(3):
        near = field[comp, :, 0:TILE].astype(F32)
        far = field[comp, :, NODES - TILE : NODES].astype(F32)
        tab[0, :, TILE * comp : TILE * (comp + 1)] = jnp.where(lane < 64, near, far).astype(BF16)
        rows = rest[LEAVES * comp : LEAVES * (comp + 1)]
        tab[0, :, TILE * (3 + comp) : TILE * (4 + comp)] = rows[:, 0:TILE].astype(BF16)
        piece = rows[:, TILE : 2 * TILE]
        if comp:
            piece = pltpu.roll(piece, tail * comp, 1)
        shared = shared + piece
    tab[0, :, TILE * 6 : TILE * 7] = shared.astype(BF16)

    pl.semaphore_wait(barrier, len(a_steps) + len(b_steps) + 2)

    def quarter(block, q):
        return tab.at[block, pl.ds(QUARTER * q, QUARTER)]

    def send(src, dst, send_sem, recv_sem, device):
        return pltpu.make_async_remote_copy(
            src_ref=src,
            dst_ref=dst,
            send_sem=send_sem,
            recv_sem=recv_sem,
            device_id=device,
            device_id_type=MESH,
        )

    ups = [
        send(quarter(0, q), quarter(2, q), ring_send.at[0, q], ring_recv.at[0, q], place(up))
        for q in range(4)
    ]
    downs = [
        send(quarter(0, q), quarter(1, q), ring_send.at[1, q], ring_recv.at[1, q], place(down))
        for q in range(4)
    ]
    for q_up, q_down in ((0, 2), (1, 3), (2, 0), (3, 1)):
        ups[q_up].start()
        downs[q_down].start()
    forwards = {
        0: send(quarter(2, 0), quarter(3, 0), fwd_send.at[0], fwd_recv.at[0], place(up)),
        1: send(quarter(2, 1), quarter(3, 1), fwd_send.at[1], fwd_recv.at[1], place(up)),
        2: send(quarter(1, 2), quarter(3, 2), fwd_send.at[2], fwd_recv.at[2], place(down)),
        3: send(quarter(1, 3), quarter(3, 3), fwd_send.at[3], fwd_recv.at[3], place(down)),
    }
    highs = [
        send(quarter(b, 0), high_band.at[b], high_send.at[b], high_recv.at[b], place(before))
        for b in range(4)
    ]
    lows = [
        send(band_out.at[b], low_band.at[b], low_send.at[b], low_recv.at[b], place(after))
        for b in range(4)
    ]
    turn = [0, 1, 3, 2]
    band_row = lax.broadcasted_iota(jnp.int32, (BAND, LEAVES), 0)
    band_col = lax.broadcasted_iota(jnp.int32, (BAND, LEAVES), 1)

    def send_bands(b):
        highs[b].start()
        live = counts_ref[m * SIBS + lax.rem(s + turn[b], SIBS)]
        chosen = jnp.where(band_col == band_row + (live - BAND), 1.0, 0.0).astype(BF16)
        band_out[b] = dot(chosen, tab[b]).astype(BF16)
        lows[b].start()

    send_bands(0)

    nbr = nbr_ref[...]
    owner_sib = jnp.bitwise_and(jnp.right_shift(nbr, 7), 3)
    slot = jnp.bitwise_and(nbr, LEAVES - 1)
    step = jnp.right_shift(nbr, 9) - m
    offset = jnp.bitwise_and(owner_sib - s + SIBS, 3)
    block = jnp.where(offset == 2, 3, jnp.where(offset == 3, 2, offset))
    prior = lax.rem(m + MORTONS - 1, MORTONS) * SIBS
    prior_live = jnp.zeros_like(nbr)
    for k in range(SIBS):
        prior_live = jnp.where(owner_sib == k, counts_ref[prior + k], prior_live)
    row = jnp.where(
        step == 0,
        block * LEAVES + slot,
        jnp.where(
            step == 1,
            4 * LEAVES + block * BAND + slot,
            4 * LEAVES + 4 * BAND + block * BAND + slot - (prior_live - BAND),
        ),
    )
    row = jnp.where(nbr < 0, -1, row).astype(F32)
    pos_sq[...] = jnp.zeros_like(pos_sq)
    pos_sq[0:6, :] = row
    pos_sq[...] = pos_sq[...].T

    def gather(first, rows, source, fresh):
        col = lax.broadcasted_iota(jnp.int32, (LEAVES, rows), 1).astype(F32) + float(first)
        for dim in range(3):
            pair = []
            for face in (2 * dim, 2 * dim + 1):
                at = pos_sq[:, face : face + 1]
                pair.append(jnp.where(col == at, 1.0, 0.0))
            chosen = jnp.concatenate(pair, axis=0).astype(BF16)
            width = 3 * TILE if dim == 0 else LANES
            got = dot(chosen, source[:, 0:width])
            if fresh:
                picked[dim, :, 0:width] = got
            else:
                picked[dim, :, 0:width] += got

    gather(0, LEAVES, tab[0], True)

    loads[PRESS_IN].wait()
    loads[DIFF_IN].wait()
    stacked = field[...].reshape(4 * LEAVES, NODES)
    for dim in range(3):
        grads[dim] = dot(stacked, diff[dim])

    own_live = counts_ref[m * SIBS + s]
    leaf_row = lax.broadcasted_iota(jnp.int32, (LEAVES, NODES), 0)
    live_rows = leaf_row < own_live

    def grad(comp, dim):
        return grads[dim, LEAVES * comp : LEAVES * (comp + 1), :]

    mass[...] = jnp.where(
        live_rows, -(grad(0, 0) + grad(1, 1) + grad(2, 2)) * mass_scale, 0.0
    )
    mass_out = pltpu.make_async_copy(mass, mass_hbm, out_sem.at[0])
    mass_out.start()

    ups[0].wait_recv()
    forwards[0].start()
    downs[2].wait_recv()
    forwards[2].start()

    loads[VISC_IN].wait()
    stress = {}
    for i in range(3):
        for j in range(i, 3):
            stress[i, j] = (visc[...] * (grad(i, j) + grad(j, i))).astype(BF16)
    ups[1].wait_recv()
    forwards[1].start()
    downs[3].wait_recv()
    forwards[3].start()
    total = None
    for j in range(3):
        rows = jnp.concatenate([stress[min(i, j), max(i, j)] for i in range(3)], axis=0)
        term = dot(rows, diff[j])
        total = term if total is None else total + term
    for comp in range(3):
        jump = field[comp].astype(F32) * mult_ref[...]
        local[comp] = (
            penalty * visc[...] * jump
            - total[LEAVES * comp : LEAVES * (comp + 1)]
            + grad(3, comp)
        ) * out_scale

    level = levels_ref[...]
    shift_bits = 3 * (LMAX - level)
    anchor = jnp.left_shift(jnp.right_shift(keys_ref[...], shift_bits), shift_bits)
    span = jnp.left_shift(jnp.ones_like(level), LMAX - level).astype(F32)
    at_box = []
    box_center = []
    for dim, bit0 in enumerate((2, 1, 0)):
        cell = jnp.zeros_like(anchor)
        corner = 0
        for bit in range(LMAX):
            cell = cell + jnp.left_shift(
                jnp.bitwise_and(jnp.right_shift(anchor, 3 * bit + bit0), 1), bit
            )
            up_bit = 3 * bit + bit0 - (3 * LMAX - 6)
            if up_bit >= 0:
                corner = corner + lax.rem(lax.div(m, 2**up_bit), 2) * 2**bit
        center = corner.astype(F32) * FINEST + 0.5 * BOX_SIDE
        box_center.append(center)
        at_box.append(((cell.astype(F32) + 0.5 * span) * FINEST - center) / BOX_SCALE)
    half = 0.5 * span * FINEST / BOX_SCALE
    sub = lax.broadcasted_iota(jnp.int32, (8, TILE), 0)

    def power_rows(value):
        value = jnp.broadcast_to(value, (8, TILE))
        power = jnp.ones((8, TILE), F32)
        rows = power
        for k in range(1, DEG + 1):
            power = power * value
            rows = jnp.where(sub == k, power, rows)
        return rows

    loads[SMALL_IN].wait()
    half_rows = power_rows(half)
    half_wide = jnp.broadcast_to(half, (8, TILE))
    scales = [half_rows]
    for _ in range(DEG):
        scales.append(scales[-1] * half_wide)
    x_rows = power_rows(at_box[0])
    x_tiles = []
    half_power = jnp.ones((8, TILE), F32)
    for k in range(DEG + 1):
        turned = x_rows if k == 0 else pltpu.roll(x_rows, k, 0)
        x_tiles.append(small[k] * turned * half_power)
        half_power = half_power * half_wide
    x_table = jnp.concatenate(x_tiles, axis=1)
    x_high, x_low = split(x_table)
    y_wide = jnp.broadcast_to(at_box[1], (8, TILE))
    z_wide = jnp.broadcast_to(at_box[2], (8, TILE))
    z_coef = []
    z_power = jnp.ones((8, TILE), F32)
    for k in range(DEG + 1):
        z_coef.append(small[k] * z_power)
        z_power = z_power * z_wide

    downs[0].wait_recv()
    downs[1].wait_recv()
    send_bands(1)
    ups[2].wait_recv()
    ups[3].wait_recv()
    send_bands(2)
    gather(LEAVES, LEAVES, tab[1], False)
    gather(2 * LEAVES, LEAVES, tab[2], False)
    for q in range(4):
        forwards[q].wait_recv()
    send_bands(3)
    gather(3 * LEAVES, LEAVES, tab[3], False)
    loads[SPREAD_IN].wait()
    loads[VAND_IN].wait()
    for b in range(4):
        highs[b].wait_recv()
    gather(4 * LEAVES, 4 * BAND, high_band[...].reshape(4 * BAND, LANES), False)
    for b in range(4):
        lows[b].wait_recv()
    gather(4 * LEAVES + 4 * BAND, 4 * BAND, low_band[...].reshape(4 * BAND, LANES), False)

    rows = []
    for comp in range(3):
        parts = []
        slot_at = 0
        for dim in range(3):
            for part_at, tile in enumerate((comp, 3 + comp, 6)):
                if dim == 0 and part_at > 0:
                    continue
                lanes = slice(TILE * tile, TILE * (tile + 1))
                low_side = picked[dim, 0:LEAVES, lanes]
                high_side = picked[dim, LEAVES : 2 * LEAVES, lanes]
                value = jnp.where(small[19 + slot_at, 0:1, :] > 0.5, low_side, high_side)
                if part_at == 2:
                    mine = (lane >= tail * comp) & (lane < tail * (comp + 1))
                    value = jnp.where(mine, value, 0.0)
                parts.append(value.astype(BF16))
                slot_at += 1
        rows.append(jnp.concatenate(parts, axis=1))
    across = dot(jnp.concatenate(rows, axis=0), spread[...])
    for comp in range(3):
        there = across[LEAVES * comp : LEAVES * (comp + 1)]
        value = local[comp] - (penalty * out_scale) * visc[...] * there
        force[comp] = jnp.where(live_rows, value, 0.0)
    force_out = pltpu.make_async_copy(force, force_hbm, out_sem.at[1])
    force_out.start()

    f_high, f_low = split(force[...].reshape(3 * LEAVES, NODES))
    leaf_moments = (
        dot_nt(vand[0], f_high) + dot_nt(vand[0], f_low) + dot_nt(vand[1], f_high)
    )
    for comp in range(3):
        for jx in range(6):
            columns = []
            for jy in range(6):
                first = jx * 48 + jy * 8
                base = leaf_moments[first : first + 8, TILE * comp : TILE * (comp + 1)] * scales[jy]
                moved = base * z_coef[0]
                for k in range(1, DEG + 1):
                    moved = moved + z_coef[k] * pltpu.roll(base, k, 0)
                columns.append(moved)
            for low in range(1, DEG + 1):
                for at in range(DEG, low - 1, -1):
                    columns[at] = columns[at] + y_wide * columns[at - 1]
            for jy in range(6):
                first = 36 * comp + 6 * jy
                mcat[first : first + 6, TILE * jx : TILE * (jx + 1)] = columns[jy][0:6]
    mcat[108:TILE, :] = jnp.zeros((TILE - 108, 6 * TILE), F32)
    c_high, c_low = split(mcat[...])
    own_box = dot_nt(x_high, c_high) + dot_nt(x_low, c_high) + dot_nt(x_high, c_low)

    shifted = own_box * small[18]
    shift_by = [(center - 0.5) / 0.5 for center in box_center]
    for dim, (axis, stride, base) in enumerate(((0, 1, 0), (1, 6, 6), (1, 1, 12))):
        moved = shifted
        power = 1.0
        for k in range(1, DEG + 1):
            power = power * shift_by[dim]
            moved = moved + small[base + k] * power * pltpu.roll(shifted, stride * k, axis)
        shifted = moved

    part[0] = own_box
    part[1] = shifted
    at_a = x_at * SIBS + s
    recv_a[at_a, 0] = own_box
    recv_a[at_a, 1] = shifted
    a_copies = []
    for k, (dx, dy) in enumerate(a_steps):
        if dx == 0:
            src, dst = part, recv_a.at[at_a]
        else:
            src, dst = part.at[1], recv_a.at[at_a, 1]
        copy = send(src, dst, a_send.at[k], a_recv.at[k], group_a(dx, dy))
        copy.start()
        a_copies.append(copy)
    for copy in a_copies:
        copy.wait_recv()
    box = None
    root = None
    for x in range(X_SIZE):
        for y in range(SIBS):
            term = recv_a[x * SIBS + y, 1]
            root = term if root is None else root + term
    for y in range(SIBS):
        term = recv_a[x_at * SIBS + y, 0]
        box = term if box is None else box + term
    box_ref[...] = box
    sum_a[...] = root
    recv_b[zc_at] = root
    b_copies = []
    for k, dz in enumerate(b_steps):
        copy = send(sum_a, recv_b.at[zc_at], b_send.at[k], b_recv.at[k], group_b(dz))
        copy.start()
        b_copies.append(copy)
    for copy in b_copies:
        copy.wait_recv()
    root = recv_b[0]
    for k in range(1, ZC):
        root = root + recv_b[k]
    root_ref[...] = root

    for copy in ups + downs + list(forwards.values()) + highs + lows + a_copies + b_copies:
        copy.wait_send()
    mass_out.wait()
    force_out.wait()


def on_device(velocity, pressure, viscosity, levels, morton_keys, counts, neighbors):
    diff, pick, spread, mult, vander, small, tail = tables()
    as_bf16 = lambda a: jnp.asarray(a.astype(np.float32)).astype(BF16)
    vander32 = vander.astype(np.float32)
    v_high = vander32.astype(jnp.bfloat16)
    v_low = (vander32 - v_high.astype(np.float32)).astype(jnp.bfloat16)
    vand = np.stack([v_high, v_low])
    dma = pltpu.SemaphoreType.DMA
    any_space = pl.BlockSpec(memory_space=pl.ANY)
    vmem = pl.BlockSpec(memory_space=pltpu.VMEM)
    smem = pl.BlockSpec(memory_space=pltpu.SMEM)
    force, mass, box, root = pl.pallas_call(
        functools.partial(kernel, tail),
        out_shape=(
            jax.ShapeDtypeStruct((3, LEAVES, NODES), F32),
            jax.ShapeDtypeStruct((LEAVES, NODES), F32),
            jax.ShapeDtypeStruct((8, TILE), F32),
            jax.ShapeDtypeStruct((8, TILE), F32),
        ),
        in_specs=[smem, vmem, vmem, vmem, vmem] + [any_space] * 8,
        out_specs=(any_space, any_space, vmem, vmem),
        scratch_shapes=[
            pltpu.VMEM((4, LEAVES, NODES), BF16),
            pltpu.VMEM((LEAVES, NODES), F32),
            pltpu.VMEM((NODES, 2 * TILE), BF16),
            pltpu.VMEM((3, NODES, NODES), BF16),
            pltpu.VMEM((7 * TILE, NODES), BF16),
            pltpu.VMEM((2, 288, NODES), BF16),
            pltpu.VMEM((26, 8, TILE), F32),
            pltpu.VMEM((4, LEAVES, LANES), BF16),
            pltpu.VMEM((4, BAND, LANES), BF16),
            pltpu.VMEM((4, BAND, LANES), BF16),
            pltpu.VMEM((4, BAND, LANES), BF16),
            pltpu.VMEM((3, 4 * LEAVES, NODES), F32),
            pltpu.VMEM((3, LEAVES, NODES), F32),
            pltpu.VMEM((3, 2 * LEAVES, LANES), F32),
            pltpu.VMEM((3, LEAVES, NODES), F32),
            pltpu.VMEM((LEAVES, NODES), F32),
            pltpu.VMEM((LEAVES, LEAVES), F32),
            pltpu.VMEM((TILE, 6 * TILE), F32),
            pltpu.VMEM((2, 8, TILE), F32),
            pltpu.VMEM((X_SIZE * SIBS, 2, 8, TILE), F32),
            pltpu.VMEM((ZC, 8, TILE), F32),
            pltpu.VMEM((8, TILE), F32),
            dma((8,)),
            dma((2,)),
            dma((2, 4)),
            dma((2, 4)),
            dma((4,)),
            dma((4,)),
            dma((4,)),
            dma((4,)),
            dma((4,)),
            dma((4,)),
            dma((15,)),
            dma((15,)),
            dma((15,)),
            dma((15,)),
        ],
        compiler_params=pltpu.CompilerParams(
            collective_id=0, has_side_effects=True, vmem_limit_bytes=48 * 2**20
        ),
    )(
        counts,
        levels.reshape(1, LEAVES),
        morton_keys.reshape(1, LEAVES),
        neighbors.T,
        jnp.asarray(mult.astype(np.float32)).reshape(1, NODES),
        velocity.transpose(1, 0, 2),
        pressure,
        viscosity,
        as_bf16(pick),
        as_bf16(diff),
        as_bf16(spread),
        jnp.asarray(vand),
        jnp.asarray(small.astype(np.float32)),
    )

    def moment_rows(packed):
        return (
            packed[:6, :108].reshape(6, 3, 36).transpose(1, 0, 2).reshape(1, 3, MOMENTS)
        )

    return (force.transpose(1, 0, 2), mass, moment_rows(box), moment_rows(root))


def solution(mesh):
    in_specs = (
        P(("morton", "sib"), None, None),
        P(("morton", "sib"), None),
        P(("morton", "sib"), None),
        P(("morton", "sib")),
        P(("morton", "sib")),
        P(),
        P(("morton", "sib"), None),
    )
    out_specs = (
        P(("morton", "sib"), None, None),
        P(("morton", "sib"), None),
        P("morton", None, None),
        P("morton", None, None),
    )
    return jax.shard_map(
        on_device, mesh=mesh, in_specs=in_specs, out_specs=out_specs, check_vma=False
    )
```

```python
import functools
import math

import jax
import jax.numpy as jnp
import numpy as np
from jax import lax
from jax.experimental import pallas as pl
from jax.experimental.pallas import tpu as pltpu
from jax.sharding import PartitionSpec as P

DEG = 5
LMAX = 7
MOMENTS = 216
LEAVES = 128
NODES = 512
LANES = 896
BAND = 32
TILE = 128
MESH = pl.DeviceIdType.MESH
F32 = jnp.float32
BF16 = jnp.bfloat16

penalty = 256.0
out_scale = 1.0 / 1024.0
mass_scale = 1.0 / 32.0

X_SIZE, Z_SIZE, CORES, SIBS = 4, 8, 2, 4
ZC = Z_SIZE * CORES
MORTONS = X_SIZE * ZC


def cheb():
    points = -np.cos(np.pi * np.arange(8) / 7.0)
    weights = np.array([(-1.0) ** k for k in range(8)])
    weights[0] *= 0.5
    weights[7] *= 0.5
    derivative = np.zeros((8, 8))
    for row in range(8):
        for col in range(8):
            if row != col:
                derivative[row, col] = weights[col] / weights[row] / (points[row] - points[col])
        derivative[row, row] = -np.sum(derivative[row])
    return points, derivative


def node_of(coords):
    return 64 * coords[0] + 8 * coords[1] + coords[2]


def coords_of(node):
    return [node // 64, node // 8 % 8, node % 8]


def surface_lists():
    x_nodes = [node_of([7 * side, b, c]) for side in range(2) for b in range(8) for c in range(8)]
    inner = [n for n in range(NODES) if coords_of(n)[0] not in (0, 7)]
    on_y = [n for n in inner if coords_of(n)[1] in (0, 7)]
    only_z = [n for n in inner if n not in on_y and coords_of(n)[2] in (0, 7)]
    return x_nodes, on_y + only_z


FACE_TILES = ((0,), (0, 1), (0, 1, 2))
MULT_AT, MASK_AT = 19, 23


def tables():
    points, derivative = cheb()
    eye = np.eye(8)
    directional = [
        np.kron(np.kron(derivative, eye), eye),
        np.kron(np.kron(eye, derivative), eye),
        np.kron(np.kron(eye, eye), derivative),
    ]
    diff = np.stack([m.T for m in directional])
    x_nodes, rest = surface_lists()
    tail = len(rest) - TILE
    pick = np.zeros((NODES, 2 * TILE))
    for k, node in enumerate(rest):
        pick[node, k] = 1.0
    tiles = [list(x_nodes), list(rest[:TILE]), [-1] * TILE]
    for comp in range(3):
        for k in range(tail):
            tiles[2][tail * comp + k] = rest[TILE + k]
    spread = np.zeros((6 * TILE, NODES))
    small = np.zeros((MASK_AT + 21, 8, TILE))
    slot = 0
    for dim in range(3):
        for tile in FACE_TILES[dim]:
            for lane, node in enumerate(tiles[tile]):
                if node < 0:
                    continue
                coords = coords_of(node)
                if coords[dim] in (0, 7):
                    other = list(coords)
                    other[dim] = 7 - coords[dim]
                    spread[slot * TILE + lane, node_of(other)] = 1.0
                    if coords[dim] == 7:
                        for at in ((6,) if tile == 2 else range(3 * tile, 3 * tile + 3)):
                            small[MASK_AT + 7 * dim + at, :, lane] = 1.0
            slot += 1
    for node in range(NODES):
        count = sum(1 for c in coords_of(node) if c in (0, 7))
        small[MULT_AT + node // TILE, :, node % TILE] = count
    vander = np.zeros((288, NODES))
    for jx in range(6):
        for jy in range(6):
            for jz in range(6):
                for node in range(NODES):
                    a, b, c = coords_of(node)
                    vander[jx * 48 + jy * 8 + jz, node] = (
                        points[a] ** jx * points[b] ** jy * points[c] ** jz / 512.0
                    )
    for k in range(6):
        for a in range(6):
            if a >= k:
                small[k, a, :] = math.comb(a, k)
        for lane in range(108):
            ay, az = lane // 6 % 6, lane % 6
            if ay >= k:
                small[6 + k, :, lane] = math.comb(ay, k)
            if az >= k:
                small[12 + k, :, lane] = math.comb(az, k)
    for ax in range(6):
        for lane in range(108):
            small[18, ax, lane] = BOX_IN_ROOT ** (ax + lane // 6 % 6 + lane % 6)
    return diff, pick, spread, vander, small, tail


BOX_CELLS = 2 ** ((3 * LMAX - 6) // 3)
FINEST = 1.0 / 2**LMAX
BOX_SIDE = BOX_CELLS * FINEST
BOX_SCALE = 0.5 * BOX_SIDE
BOX_IN_ROOT = BOX_SCALE / 0.5

(
    VEL_IN,
    PICK_IN,
    COUNTS_IN,
    NBR_IN,
    PRESS_IN,
    DIFF_IN,
    VISC_IN,
    SMALL_IN,
    LEVELS_IN,
    KEYS_IN,
    SPREAD_IN,
    VAND_IN,
) = range(12)
QUARTER = LEAVES // 4
HALF_BAND = BAND // 2
ROUNDS = 3
LINK_AT, CHIP_AT, ROWS = 4 * LEAVES, 4 * LEAVES + 4 * BAND, 4 * LEAVES + 8 * BAND


def dot(a, b):
    return jnp.dot(a, b, preferred_element_type=F32)


def dot_nt(a, b):
    return lax.dot_general(a, b, (((1,), (1,)), ((), ())), preferred_element_type=F32)


def split(value):
    high = value.astype(BF16)
    return high, (value - high.astype(F32)).astype(BF16)


def flat_rows(packed, out_ref):
    lane = lax.broadcasted_iota(jnp.int32, (8, TILE), 1)
    sub = lax.broadcasted_iota(jnp.int32, (8, TILE), 0)
    first_tile = (sub < 3) | ((sub == 3) & (lane >= 108))
    valid = jnp.bitwise_and(lane - 36 * sub, TILE - 1) < 36
    turned = {0: packed}
    for by in range(-2, DEG + 1):
        if by:
            turned[by] = pltpu.roll(packed, 36 * by % TILE, 1)
    for comp in range(3):
        rows = turned[-comp]
        for ax in range(1, DEG + 1):
            rows = jnp.where(sub == ax, turned[ax - comp], rows)
        rows = jnp.where(valid & (sub < 6), rows, 0.0)
        near = jnp.sum(jnp.where(first_tile, rows, 0.0), axis=0, keepdims=True)
        far = jnp.sum(jnp.where(first_tile, 0.0, rows), axis=0, keepdims=True)
        out_ref[comp, :, 0:TILE] = near
        out_ref[comp, :, TILE:MOMENTS] = far[:, : MOMENTS - TILE]


def kernel(
    tail,
    vel_hbm,
    pick_hbm,
    counts_hbm,
    nbr_hbm,
    press_hbm,
    diff_hbm,
    visc_hbm,
    small_hbm,
    levels_hbm,
    keys_hbm,
    spread_hbm,
    vand_hbm,
    force_out_ref,
    mass_out_ref,
    box_out_ref,
    root_out_ref,
    field,
    pick,
    counts,
    nbr_in,
    diff,
    visc,
    small,
    levels,
    keys,
    spread,
    vand,
    tab,
    link_band,
    chip_band,
    grads,
    local,
    picked,
    force,
    mass,
    pos_sq,
    mcat,
    part,
    recv_a,
    recv_b,
    sum_a,
    flat,
    in_sem,
    out_sem,
    ring_send,
    ring_recv,
    fwd_send,
    fwd_recv,
    link_send,
    link_recv,
    relay_send,
    relay_recv,
    chip_send,
    chip_recv,
    a_send,
    a_recv,
    b_send,
    b_recv,
    known,
):
    m = lax.axis_index("morton")
    s = lax.axis_index("sib")
    x_at = lax.div(m, ZC)
    zc_at = lax.rem(m, ZC)
    core = lax.rem(m, CORES)
    above = lax.rem(s + 1, SIBS)
    below = lax.rem(s + SIBS - 1, SIBS)
    m_chip = m + 1 - 2 * core
    m_link = lax.rem(m + MORTONS - 1 + 2 * core, MORTONS)

    def group_a(dx, dy):
        return (lax.rem(x_at + dx, X_SIZE) * ZC + zc_at, lax.rem(s + dy, SIBS))

    def group_b(dz):
        return (x_at * ZC + lax.rem(zc_at + dz, ZC), s)

    a_steps = [(dx, dy) for dx in range(X_SIZE) for dy in range(SIBS) if dx or dy]
    b_steps = list(range(1, ZC))

    loads = [
        pltpu.make_async_copy(vel_hbm, field.at[pl.ds(0, 3)], in_sem.at[VEL_IN]),
        pltpu.make_async_copy(pick_hbm, pick, in_sem.at[PICK_IN]),
        pltpu.make_async_copy(counts_hbm, counts, in_sem.at[COUNTS_IN]),
        pltpu.make_async_copy(nbr_hbm, nbr_in, in_sem.at[NBR_IN]),
        pltpu.make_async_copy(press_hbm, field.at[3], in_sem.at[PRESS_IN]),
        pltpu.make_async_copy(diff_hbm, diff, in_sem.at[DIFF_IN]),
        pltpu.make_async_copy(visc_hbm, visc, in_sem.at[VISC_IN]),
        pltpu.make_async_copy(small_hbm, small, in_sem.at[SMALL_IN]),
        pltpu.make_async_copy(levels_hbm, levels, in_sem.at[LEVELS_IN]),
        pltpu.make_async_copy(keys_hbm, keys, in_sem.at[KEYS_IN]),
        pltpu.make_async_copy(spread_hbm, spread, in_sem.at[SPREAD_IN]),
        pltpu.make_async_copy(vand_hbm, vand, in_sem.at[VAND_IN]),
    ]
    for which in (VEL_IN, PICK_IN, COUNTS_IN, NBR_IN):
        loads[which].start()

    near_groups = [group_a(1, 0), group_a(X_SIZE - 1, 0), group_b(1), group_b(ZC - 1)]
    near = [(m, above), (m, below), (m_link, s), (m_link, above), (m_link, below)] + near_groups
    barrier = pltpu.get_barrier_semaphore()
    for device in near:
        pl.semaphore_signal(barrier, inc=1, device_id=device, device_id_type=MESH)

    loads[VEL_IN].wait()
    loads[PICK_IN].wait()
    for which in range(PRESS_IN, len(loads)):
        loads[which].start()
    lane = lax.broadcasted_iota(jnp.int32, (LEAVES, TILE), 1)
    rest = dot(field[0:3].reshape(3 * LEAVES, NODES), pick[...])
    shared = jnp.zeros((LEAVES, TILE), F32)
    for comp in range(3):
        first = field[comp, :, 0:TILE].astype(F32)
        last = field[comp, :, NODES - TILE : NODES].astype(F32)
        tab[0:LEAVES, TILE * comp : TILE * (comp + 1)] = jnp.where(lane < 64, first, last).astype(BF16)
        rows = rest[LEAVES * comp : LEAVES * (comp + 1)]
        tab[0:LEAVES, TILE * (3 + comp) : TILE * (4 + comp)] = rows[:, 0:TILE].astype(BF16)
        piece = rows[:, TILE : 2 * TILE]
        if comp:
            piece = pltpu.roll(piece, tail * comp, 1)
        shared = shared + piece
    tab[0:LEAVES, TILE * 6 : TILE * 7] = shared.astype(BF16)

    pl.semaphore_wait(barrier, len(near))

    def send(src, dst, send_sem, recv_sem, device):
        return pltpu.make_async_remote_copy(
            src_ref=src,
            dst_ref=dst,
            send_sem=send_sem,
            recv_sem=recv_sem,
            device_id=device,
            device_id_type=MESH,
        )

    def quarters(block, q, count=1):
        return tab.at[pl.ds(LEAVES * block + QUARTER * q, QUARTER * count)]

    def link_rows(b, first=0, rows=BAND):
        return tab.at[pl.ds(LINK_AT + BAND * b + first, rows)]

    def chip_rows(b):
        return tab.at[pl.ds(CHIP_AT + BAND * b, BAND)]

    ups, downs = [], []
    for k, (q_up, q_down, count) in enumerate(((0, 2, 1), (1, 3, 1), (2, 0, 2))):
        ups.append(
            send(
                quarters(0, q_up, count),
                quarters(2, q_up, count),
                ring_send.at[0, k],
                ring_recv.at[0, k],
                (m, above),
            )
        )
        downs.append(
            send(
                quarters(0, q_down, count),
                quarters(1, q_down, count),
                ring_send.at[1, k],
                ring_recv.at[1, k],
                (m, below),
            )
        )
    forwards = [
        send(quarters(2, 0), quarters(3, 0), fwd_send.at[0], fwd_recv.at[0], (m, above)),
        send(quarters(1, 2), quarters(3, 2), fwd_send.at[1], fwd_recv.at[1], (m, below)),
        send(quarters(2, 1), quarters(3, 1), fwd_send.at[2], fwd_recv.at[2], (m, above)),
        send(quarters(1, 3), quarters(3, 3), fwd_send.at[3], fwd_recv.at[3], (m, below)),
    ]
    links = [
        send(link_band, link_rows(0), link_send.at[0], link_recv.at[0], (m_link, s)),
        send(link_band, link_rows(2), link_send.at[1], link_recv.at[1], (m_link, above)),
        send(link_band, link_rows(1), link_send.at[2], link_recv.at[2], (m_link, below)),
    ]
    relays = [
        send(
            link_rows(2, 0, HALF_BAND),
            link_rows(3, 0, HALF_BAND),
            relay_send.at[0],
            relay_recv.at[0],
            (m, above),
        ),
        send(
            link_rows(1, HALF_BAND, HALF_BAND),
            link_rows(3, HALF_BAND, HALF_BAND),
            relay_send.at[1],
            relay_recv.at[1],
            (m, below),
        ),
    ]
    chips = [
        send(chip_band.at[b], chip_rows(b), chip_send.at[b], chip_recv.at[b], (m_chip, s))
        for b in range(4)
    ]
    turn = [0, 1, 3, 2]
    band_row = lax.broadcasted_iota(jnp.int32, (BAND, LEAVES), 0)
    band_col = lax.broadcasted_iota(jnp.int32, (BAND, LEAVES), 1)

    def band(b, last):
        live = counts[m * SIBS + lax.rem(s + turn[b], SIBS)]
        chosen = jnp.where(band_col == band_row + last * (live - BAND), 1.0, 0.0).astype(BF16)
        return dot(chosen, tab[LEAVES * b : LEAVES * (b + 1)]).astype(BF16)

    def send_chip(b):
        chip_band[b] = band(b, 1 - core)
        chips[b].start()

    round_peers = []
    for k in range(ROUNDS):
        round_peers.append(
            [group_a(1, 0), group_a(X_SIZE - 1, 0), (m, above), (m, below)]
            + [group_b(2**k), group_b(ZC - 2**k)]
        )

    def tell(k):
        for device in round_peers[k]:
            pl.semaphore_signal(known.at[k], inc=1, device_id=device, device_id_type=MESH)

    def hear(k):
        pl.semaphore_wait(known.at[k], len(round_peers[k]))

    ups[0].start()
    downs[0].start()
    loads[COUNTS_IN].wait()
    link_band[...] = band(0, core)
    links[0].start()
    ups[1].start()
    downs[1].start()
    loads[NBR_IN].wait()
    nbr = nbr_in[...]
    owner_sib = jnp.bitwise_and(jnp.right_shift(nbr, 7), 3)
    slot = jnp.bitwise_and(nbr, LEAVES - 1)
    step = jnp.right_shift(nbr, 9) - m
    offset = jnp.bitwise_and(owner_sib - s + SIBS, 3)
    block = jnp.where(offset == 2, 3, jnp.where(offset == 3, 2, offset))
    prior = lax.rem(m + MORTONS - 1, MORTONS) * SIBS
    prior_live = jnp.zeros_like(nbr)
    for k in range(SIBS):
        prior_live = jnp.where(owner_sib == k, counts[prior + k], prior_live)
    halo_row = 4 * LEAVES + block * BAND + slot
    row = jnp.where(
        step == 0,
        block * LEAVES + slot,
        jnp.where(
            step == 1,
            halo_row + (1 - core) * (4 * BAND),
            halo_row + core * (4 * BAND) - (prior_live - BAND),
        ),
    )
    row = jnp.where(nbr < 0, -1, row).astype(F32)
    pos_sq[...] = jnp.zeros_like(pos_sq)
    pos_sq[0:6, :] = row
    pos_sq[...] = pos_sq[...].T

    def gather(first, rows, fresh=False):
        col = lax.broadcasted_iota(jnp.int32, (LEAVES, rows), 1).astype(F32) + float(first)
        for dim in range(3):
            pair = []
            for face in (2 * dim, 2 * dim + 1):
                at = pos_sq[:, face : face + 1]
                pair.append(jnp.where(col == at, 1.0, 0.0))
            chosen = jnp.concatenate(pair, axis=0).astype(BF16)
            width = TILE * (3, 6, 7)[dim]
            got = dot(chosen, tab[first : first + rows, 0:width])
            for tile in range(width // TILE):
                lanes = slice(TILE * tile, TILE * (tile + 1))
                mask = small[MASK_AT + 7 * dim + tile, 0:1, :] > 0.5
                one = jnp.where(mask, got[0:LEAVES, lanes], got[LEAVES:, lanes]).astype(BF16)
                if fresh:
                    picked[dim, :, lanes] = one
                else:
                    picked[dim, :, lanes] += one

    links[1].start()
    links[2].start()
    tell(0)
    send_chip(0)
    loads[SMALL_IN].wait()
    gather(0, LEAVES, True)
    ups[2].start()
    downs[2].start()

    loads[PRESS_IN].wait()
    loads[DIFF_IN].wait()
    stacked = field[...].reshape(4 * LEAVES, NODES)
    for dim in range(3):
        grads[dim] = dot(stacked, diff[dim])

    own_live = counts[m * SIBS + s]
    leaf_row = lax.broadcasted_iota(jnp.int32, (LEAVES, NODES), 0)
    live_rows = leaf_row < own_live

    def grad(comp, dim):
        return grads[dim, LEAVES * comp : LEAVES * (comp + 1), :]

    mass[...] = jnp.where(
        live_rows, -(grad(0, 0) + grad(1, 1) + grad(2, 2)) * mass_scale, 0.0
    )
    mass_out = pltpu.make_async_copy(mass, mass_out_ref, out_sem.at[0])
    mass_out.start()

    loads[VISC_IN].wait()
    stress = {}
    for i in range(3):
        for j in range(i, 3):
            stress[i, j] = (visc[...] * (grad(i, j) + grad(j, i))).astype(BF16)
    total = None
    for j in range(3):
        rows = jnp.concatenate([stress[min(i, j), max(i, j)] for i in range(3)], axis=0)
        term = dot(rows, diff[j])
        total = term if total is None else total + term
    mult = jnp.concatenate([small[MULT_AT + t, 0:1, :] for t in range(4)], axis=1)
    for comp in range(3):
        jump = field[comp].astype(F32) * mult
        local[comp] = (
            penalty * visc[...] * jump
            - total[LEAVES * comp : LEAVES * (comp + 1)]
            + grad(3, comp)
        ) * out_scale
    ups[0].wait_recv()
    forwards[0].start()
    downs[0].wait_recv()
    forwards[1].start()
    hear(0)
    tell(1)
    ups[1].wait_recv()
    forwards[2].start()
    downs[1].wait_recv()
    forwards[3].start()
    links[1].wait_recv()
    relays[0].start()
    links[2].wait_recv()
    relays[1].start()
    hear(1)
    tell(2)

    loads[LEVELS_IN].wait()
    loads[KEYS_IN].wait()
    level = levels[...]
    shift_bits = 3 * (LMAX - level)
    anchor = jnp.left_shift(jnp.right_shift(keys[...], shift_bits), shift_bits)
    span = jnp.left_shift(jnp.ones_like(level), LMAX - level).astype(F32)
    at_box = []
    box_center = []
    for dim, bit0 in enumerate((2, 1, 0)):
        cell = jnp.zeros_like(anchor)
        corner = 0
        for bit in range(LMAX):
            cell = cell + jnp.left_shift(
                jnp.bitwise_and(jnp.right_shift(anchor, 3 * bit + bit0), 1), bit
            )
            up_bit = 3 * bit + bit0 - (3 * LMAX - 6)
            if up_bit >= 0:
                corner = corner + lax.rem(lax.div(m, 2**up_bit), 2) * 2**bit
        center = corner.astype(F32) * FINEST + 0.5 * BOX_SIDE
        box_center.append(center)
        at_box.append(((cell.astype(F32) + 0.5 * span) * FINEST - center) / BOX_SCALE)
    half = 0.5 * span * FINEST / BOX_SCALE
    sub = lax.broadcasted_iota(jnp.int32, (8, TILE), 0)

    def power_rows(value):
        value = jnp.broadcast_to(value, (8, TILE))
        power = jnp.ones((8, TILE), F32)
        rows = power
        for k in range(1, DEG + 1):
            power = power * value
            rows = jnp.where(sub == k, power, rows)
        return rows

    half_rows = power_rows(half)
    half_wide = jnp.broadcast_to(half, (8, TILE))
    scales = [half_rows]
    for _ in range(DEG):
        scales.append(scales[-1] * half_wide)
    x_rows = power_rows(at_box[0])
    x_tiles = []
    half_power = jnp.ones((8, TILE), F32)
    for k in range(DEG + 1):
        turned = x_rows if k == 0 else pltpu.roll(x_rows, k, 0)
        x_tiles.append(small[k] * turned * half_power)
        half_power = half_power * half_wide
    x_table = jnp.concatenate(x_tiles, axis=1)
    x_high, x_low = split(x_table)
    y_wide = jnp.broadcast_to(at_box[1], (8, TILE))
    z_wide = jnp.broadcast_to(at_box[2], (8, TILE))
    z_coef = []
    z_power = jnp.ones((8, TILE), F32)
    for k in range(DEG + 1):
        z_coef.append(small[k] * z_power)
        z_power = z_power * z_wide

    downs[2].wait_recv()
    send_chip(1)
    ups[2].wait_recv()
    send_chip(2)
    gather(LEAVES, 2 * LEAVES)
    loads[SPREAD_IN].wait()
    loads[VAND_IN].wait()
    hear(2)
    links[0].wait_recv()
    for k in range(2):
        relays[k].wait_recv()
    for b in range(3):
        chips[b].wait_recv()
    gather(LINK_AT, 7 * BAND)
    for k in range(4):
        forwards[k].wait_recv()
    send_chip(3)
    gather(3 * LEAVES, LEAVES)
    chips[3].wait_recv()
    gather(CHIP_AT + 3 * BAND, BAND)

    rows = []
    for comp in range(3):
        parts = []
        for dim in range(3):
            for tile in FACE_TILES[dim]:
                at = 6 if tile == 2 else 3 * tile + comp
                value = picked[dim, :, TILE * at : TILE * (at + 1)]
                if tile == 2:
                    mine = (lane >= tail * comp) & (lane < tail * (comp + 1))
                    value = jnp.where(mine, value.astype(F32), 0.0).astype(BF16)
                parts.append(value)
        rows.append(jnp.concatenate(parts, axis=1))
    across = dot(jnp.concatenate(rows, axis=0), spread[...])
    for comp in range(3):
        there = across[LEAVES * comp : LEAVES * (comp + 1)]
        value = local[comp] - (penalty * out_scale) * visc[...] * there
        force[comp] = jnp.where(live_rows, value, 0.0)
    force_out = pltpu.make_async_copy(force, force_out_ref, out_sem.at[1])
    force_out.start()

    f_high, f_low = split(force[...].reshape(3 * LEAVES, NODES))
    leaf_moments = (
        dot_nt(vand[0], f_high) + dot_nt(vand[0], f_low) + dot_nt(vand[1], f_high)
    )
    for comp in range(3):
        for jx in range(6):
            columns = []
            for jy in range(6):
                first = jx * 48 + jy * 8
                base = leaf_moments[first : first + 8, TILE * comp : TILE * (comp + 1)] * scales[jy]
                moved = base * z_coef[0]
                for k in range(1, DEG + 1):
                    moved = moved + z_coef[k] * pltpu.roll(base, k, 0)
                columns.append(moved)
            for low in range(1, DEG + 1):
                for at in range(DEG, low - 1, -1):
                    columns[at] = columns[at] + y_wide * columns[at - 1]
            for jy in range(6):
                first = 36 * comp + 6 * jy
                mcat[first : first + 6, TILE * jx : TILE * (jx + 1)] = columns[jy][0:6]
    mcat[108:TILE, :] = jnp.zeros((TILE - 108, 6 * TILE), F32)
    c_high, c_low = split(mcat[...])
    own_box = dot_nt(x_high, c_high) + dot_nt(x_low, c_high) + dot_nt(x_high, c_low)

    shifted = own_box * small[18]
    shift_by = [(center - 0.5) / 0.5 for center in box_center]
    for dim, (axis, stride, base) in enumerate(((0, 1, 0), (1, 6, 6), (1, 1, 12))):
        moved = shifted
        power = 1.0
        for k in range(1, DEG + 1):
            power = power * shift_by[dim]
            moved = moved + small[base + k] * power * pltpu.roll(shifted, stride * k, axis)
        shifted = moved

    part[0] = own_box
    part[1] = shifted
    at_a = x_at * SIBS + s
    recv_a[at_a, 0] = own_box
    recv_a[at_a, 1] = shifted
    a_copies = []
    for k, (dx, dy) in enumerate(a_steps):
        if dx == 0:
            src, dst = part, recv_a.at[at_a]
        else:
            src, dst = part.at[1], recv_a.at[at_a, 1]
        copy = send(src, dst, a_send.at[k], a_recv.at[k], group_a(dx, dy))
        copy.start()
        a_copies.append(copy)
    for copy in a_copies:
        copy.wait_recv()
    box = None
    root = None
    for x in range(X_SIZE):
        for y in range(SIBS):
            term = recv_a[x * SIBS + y, 1]
            root = term if root is None else root + term
    for y in range(SIBS):
        term = recv_a[x_at * SIBS + y, 0]
        box = term if box is None else box + term
    flat_rows(box, flat.at[0])
    box_out = pltpu.make_async_copy(flat.at[0], box_out_ref, out_sem.at[2])
    box_out.start()
    sum_a[...] = root
    recv_b[zc_at] = root
    b_copies = []
    for k, dz in enumerate(b_steps):
        copy = send(sum_a, recv_b.at[zc_at], b_send.at[k], b_recv.at[k], group_b(dz))
        copy.start()
        b_copies.append(copy)
    for copy in b_copies:
        copy.wait_recv()
    root = recv_b[0]
    for k in range(1, ZC):
        root = root + recv_b[k]
    flat_rows(root, flat.at[1])
    root_out = pltpu.make_async_copy(flat.at[1], root_out_ref, out_sem.at[3])
    root_out.start()

    for copy in ups + downs + links + forwards + relays + chips + a_copies + b_copies:
        copy.wait_send()
    mass_out.wait()
    force_out.wait()
    box_out.wait()
    root_out.wait()


def finish(force, mass, box, root, force_out, mass_out, box_out, root_out, *scratch):
    held, sem = scratch[:4], scratch[4]
    parts = []
    for k, (src, dst) in enumerate(((force, force_out), (mass, mass_out), (box, box_out), (root, root_out))):
        pieces = 3 if k != 1 else 1
        for piece in range(pieces):
            at = (src, held[k], dst) if pieces == 1 else (src.at[piece], held[k].at[piece], dst.at[piece])
            parts.append(at)
    copies = []
    for k, (src, mid, dst) in enumerate(parts):
        copies.append(
            (
                pltpu.make_async_copy(src, mid, sem.at[0, k]),
                pltpu.make_async_copy(mid, dst, sem.at[1, k]),
            )
        )
    for copy, _ in copies:
        copy.start()
    for copy, then in copies:
        copy.wait()
        then.start()
    for _, then in copies:
        then.wait()


def on_device(velocity, pressure, viscosity, levels, morton_keys, counts, neighbors):
    diff, pick, spread, vander, small, tail = tables()
    as_bf16 = lambda a: jnp.asarray(a.astype(np.float32)).astype(BF16)
    vander32 = vander.astype(np.float32)
    v_high = vander32.astype(jnp.bfloat16)
    v_low = (vander32 - v_high.astype(np.float32)).astype(jnp.bfloat16)
    vand = np.stack([v_high, v_low])
    dma = pltpu.SemaphoreType.DMA
    any_space = pl.BlockSpec(memory_space=pl.ANY)
    hbm = pl.BlockSpec(memory_space=pltpu.HBM)
    results = (
        jax.ShapeDtypeStruct((3, LEAVES, NODES), F32),
        jax.ShapeDtypeStruct((LEAVES, NODES), F32),
        jax.ShapeDtypeStruct((3, 1, MOMENTS), F32),
        jax.ShapeDtypeStruct((3, 1, MOMENTS), F32),
    )
    raw = pl.pallas_call(
        functools.partial(kernel, tail),
        out_shape=results,
        in_specs=[hbm] * 12,
        out_specs=(any_space,) * 4,
        scratch_shapes=[
            pltpu.VMEM((4, LEAVES, NODES), BF16),
            pltpu.VMEM((NODES, 2 * TILE), BF16),
            pltpu.SMEM((MORTONS * SIBS,), jnp.int32),
            pltpu.VMEM((6, LEAVES), jnp.int32),
            pltpu.VMEM((3, NODES, NODES), BF16),
            pltpu.VMEM((LEAVES, NODES), F32),
            pltpu.VMEM((MASK_AT + 21, 8, TILE), F32),
            pltpu.VMEM((1, LEAVES), jnp.int32),
            pltpu.VMEM((1, LEAVES), jnp.int32),
            pltpu.VMEM((6 * TILE, NODES), BF16),
            pltpu.VMEM((2, 288, NODES), BF16),
            pltpu.VMEM((ROWS, LANES), BF16),
            pltpu.VMEM((BAND, LANES), BF16),
            pltpu.VMEM((4, BAND, LANES), BF16),
            pltpu.VMEM((3, 4 * LEAVES, NODES), F32),
            pltpu.VMEM((3, LEAVES, NODES), F32),
            pltpu.VMEM((3, LEAVES, LANES), BF16),
            pltpu.VMEM((3, LEAVES, NODES), F32),
            pltpu.VMEM((LEAVES, NODES), F32),
            pltpu.VMEM((LEAVES, LEAVES), F32),
            pltpu.VMEM((TILE, 6 * TILE), F32),
            pltpu.VMEM((2, 8, TILE), F32),
            pltpu.VMEM((X_SIZE * SIBS, 2, 8, TILE), F32),
            pltpu.VMEM((ZC, 8, TILE), F32),
            pltpu.VMEM((8, TILE), F32),
            pltpu.VMEM((2, 3, 1, MOMENTS), F32),
            dma((12,)),
            dma((4,)),
            dma((2, 3)),
            dma((2, 3)),
            dma((4,)),
            dma((4,)),
            dma((3,)),
            dma((3,)),
            dma((2,)),
            dma((2,)),
            dma((4,)),
            dma((4,)),
            dma((15,)),
            dma((15,)),
            dma((15,)),
            dma((15,)),
            pltpu.SemaphoreType.REGULAR((ROUNDS,)),
        ],
        compiler_params=pltpu.CompilerParams(
            collective_id=0, has_side_effects=True, vmem_limit_bytes=60 * 2**20
        ),
    )(
        velocity.transpose(1, 0, 2),
        as_bf16(pick),
        counts,
        neighbors.T,
        pressure,
        as_bf16(diff),
        viscosity,
        jnp.asarray(small.astype(np.float32)),
        levels.reshape(1, LEAVES),
        morton_keys.reshape(1, LEAVES),
        as_bf16(spread),
        jnp.asarray(vand),
    )
    force, mass, box, root = pl.pallas_call(
        finish,
        out_shape=results,
        in_specs=[any_space] * 4,
        out_specs=(any_space,) * 4,
        scratch_shapes=[pltpu.VMEM(r.shape, r.dtype) for r in results] + [dma((2, 10))],
        compiler_params=pltpu.CompilerParams(vmem_limit_bytes=60 * 2**20),
    )(*raw)
    return (
        force.transpose(1, 0, 2),
        mass,
        box.transpose(1, 0, 2),
        root.transpose(1, 0, 2),
    )


def solution(mesh):
    in_specs = (
        P(("morton", "sib"), None, None),
        P(("morton", "sib"), None),
        P(("morton", "sib"), None),
        P(("morton", "sib")),
        P(("morton", "sib")),
        P(),
        P(("morton", "sib"), None),
    )
    out_specs = (
        P(("morton", "sib"), None, None),
        P(("morton", "sib"), None),
        P("morton", None, None),
        P("morton", None, None),
    )
    return jax.shard_map(
        on_device, mesh=mesh, in_specs=in_specs, out_specs=out_specs, check_vma=False
    )
```

```python
import functools
import math

import jax
import jax.numpy as jnp
import numpy as np
from jax import lax
from jax.experimental import pallas as pl
from jax.experimental.pallas import tpu as pltpu
from jax.sharding import PartitionSpec as P

DEG = 5
LMAX = 7
MOMENTS = 216
LEAVES = 128
NODES = 512
LANES = 896
BAND = 32
TILE = 128
MESH = pl.DeviceIdType.MESH
F32 = jnp.float32
BF16 = jnp.bfloat16

penalty = 256.0
out_scale = 1.0 / 1024.0
mass_scale = 1.0 / 32.0

X_SIZE, Z_SIZE, CORES, SIBS = 4, 8, 2, 4
ZC = Z_SIZE * CORES
MORTONS = X_SIZE * ZC


def cheb():
    points = -np.cos(np.pi * np.arange(8) / 7.0)
    weights = np.array([(-1.0) ** k for k in range(8)])
    weights[0] *= 0.5
    weights[7] *= 0.5
    derivative = np.zeros((8, 8))
    for row in range(8):
        for col in range(8):
            if row != col:
                derivative[row, col] = weights[col] / weights[row] / (points[row] - points[col])
        derivative[row, row] = -np.sum(derivative[row])
    return points, derivative


def node_of(coords):
    return 64 * coords[0] + 8 * coords[1] + coords[2]


def coords_of(node):
    return [node // 64, node // 8 % 8, node % 8]


def surface_lists():
    x_nodes = [node_of([7 * side, b, c]) for side in range(2) for b in range(8) for c in range(8)]
    inner = [n for n in range(NODES) if coords_of(n)[0] not in (0, 7)]
    on_y = [n for n in inner if coords_of(n)[1] in (0, 7)]
    only_z = [n for n in inner if n not in on_y and coords_of(n)[2] in (0, 7)]
    return x_nodes, on_y + only_z


FACE_TILES = ((0,), (0, 1), (0, 1, 2))
MULT_AT, MASK_AT = 19, 23


def tables():
    points, derivative = cheb()
    eye = np.eye(8)
    directional = [
        np.kron(np.kron(derivative, eye), eye),
        np.kron(np.kron(eye, derivative), eye),
        np.kron(np.kron(eye, eye), derivative),
    ]
    diff = np.stack([m.T for m in directional])
    x_nodes, rest = surface_lists()
    tail = len(rest) - TILE
    pick = np.zeros((NODES, 2 * TILE))
    for k, node in enumerate(rest):
        pick[node, k] = 1.0
    tiles = [list(x_nodes), list(rest[:TILE]), [-1] * TILE]
    for comp in range(3):
        for k in range(tail):
            tiles[2][tail * comp + k] = rest[TILE + k]
    spread = np.zeros((6 * TILE, NODES))
    small = np.zeros((MASK_AT + 21, 8, TILE))
    slot = 0
    for dim in range(3):
        for tile in FACE_TILES[dim]:
            for lane, node in enumerate(tiles[tile]):
                if node < 0:
                    continue
                coords = coords_of(node)
                if coords[dim] in (0, 7):
                    other = list(coords)
                    other[dim] = 7 - coords[dim]
                    spread[slot * TILE + lane, node_of(other)] = 1.0
                    if coords[dim] == 7:
                        for at in ((6,) if tile == 2 else range(3 * tile, 3 * tile + 3)):
                            small[MASK_AT + 7 * dim + at, :, lane] = 1.0
            slot += 1
    for node in range(NODES):
        count = sum(1 for c in coords_of(node) if c in (0, 7))
        small[MULT_AT + node // TILE, :, node % TILE] = count
    vander = np.zeros((288, NODES))
    for jx in range(6):
        for jy in range(6):
            for jz in range(6):
                for node in range(NODES):
                    a, b, c = coords_of(node)
                    vander[jx * 48 + jy * 8 + jz, node] = (
                        points[a] ** jx * points[b] ** jy * points[c] ** jz / 512.0
                    )
    for k in range(6):
        for a in range(6):
            if a >= k:
                small[k, a, :] = math.comb(a, k)
        for lane in range(108):
            ay, az = lane // 6 % 6, lane % 6
            if ay >= k:
                small[6 + k, :, lane] = math.comb(ay, k)
            if az >= k:
                small[12 + k, :, lane] = math.comb(az, k)
    for ax in range(6):
        for lane in range(108):
            small[18, ax, lane] = BOX_IN_ROOT ** (ax + lane // 6 % 6 + lane % 6)
    return diff, pick, spread, vander, small, tail


BOX_CELLS = 2 ** ((3 * LMAX - 6) // 3)
FINEST = 1.0 / 2**LMAX
BOX_SIDE = BOX_CELLS * FINEST
BOX_SCALE = 0.5 * BOX_SIDE
BOX_IN_ROOT = BOX_SCALE / 0.5

(
    VEL_IN,
    PICK_IN,
    COUNTS_IN,
    NBR_IN,
    PRESS_IN,
    DIFF_IN,
    VISC_IN,
    SMALL_IN,
    LEVELS_IN,
    KEYS_IN,
    SPREAD_IN,
    VAND_IN,
) = range(12)
QUARTER = LEAVES // 4
HALF_BAND = BAND // 2
ROUNDS = 3
LINK_AT, CHIP_AT, ROWS = 4 * LEAVES, 4 * LEAVES + 4 * BAND, 4 * LEAVES + 8 * BAND


def dot(a, b):
    return jnp.dot(a, b, preferred_element_type=F32)


def dot_nt(a, b):
    return lax.dot_general(a, b, (((1,), (1,)), ((), ())), preferred_element_type=F32)


def split(value):
    high = value.astype(BF16)
    return high, (value - high.astype(F32)).astype(BF16)


def flat_rows(packed, out_ref):
    lane = lax.broadcasted_iota(jnp.int32, (8, TILE), 1)
    sub = lax.broadcasted_iota(jnp.int32, (8, TILE), 0)
    first_tile = (sub < 3) | ((sub == 3) & (lane >= 108))
    valid = jnp.bitwise_and(lane - 36 * sub, TILE - 1) < 36
    turned = {0: packed}
    for by in range(-2, DEG + 1):
        if by:
            turned[by] = pltpu.roll(packed, 36 * by % TILE, 1)
    for comp in range(3):
        rows = turned[-comp]
        for ax in range(1, DEG + 1):
            rows = jnp.where(sub == ax, turned[ax - comp], rows)
        rows = jnp.where(valid & (sub < 6), rows, 0.0)
        near = jnp.sum(jnp.where(first_tile, rows, 0.0), axis=0, keepdims=True)
        far = jnp.sum(jnp.where(first_tile, 0.0, rows), axis=0, keepdims=True)
        out_ref[comp, :, 0:TILE] = near
        out_ref[comp, :, TILE:MOMENTS] = far[:, : MOMENTS - TILE]


def kernel(
    tail,
    vel_hbm,
    pick_hbm,
    counts_hbm,
    nbr_hbm,
    press_hbm,
    diff_hbm,
    visc_hbm,
    small_hbm,
    levels_hbm,
    keys_hbm,
    spread_hbm,
    vand_hbm,
    force_out_ref,
    mass_out_ref,
    box_out_ref,
    root_out_ref,
    field,
    pick,
    counts,
    nbr_in,
    diff,
    visc,
    small,
    levels,
    keys,
    spread,
    vand,
    tab,
    link_band,
    chip_band,
    grads,
    local,
    picked,
    force,
    mass,
    pos_sq,
    mcat,
    part,
    recv_box,
    other_core,
    recv_a,
    recv_b,
    sum_a,
    sum_b,
    whole,
    flat,
    in_sem,
    out_sem,
    ring_send,
    ring_recv,
    fwd_send,
    fwd_recv,
    link_send,
    link_recv,
    relay_send,
    relay_recv,
    chip_send,
    chip_recv,
    box_send,
    box_recv,
    core_send,
    core_recv,
    a_send,
    a_recv,
    b_send,
    b_recv,
    known,
):
    m = lax.axis_index("morton")
    s = lax.axis_index("sib")
    x_at = lax.div(m, ZC)
    zc_at = lax.rem(m, ZC)
    core = lax.rem(m, CORES)
    above = lax.rem(s + 1, SIBS)
    below = lax.rem(s + SIBS - 1, SIBS)
    m_chip = m + 1 - 2 * core
    m_link = lax.rem(m + MORTONS - 1 + 2 * core, MORTONS)

    def group_a(dx, dy):
        return (lax.rem(x_at + dx, X_SIZE) * ZC + zc_at, lax.rem(s + dy, SIBS))

    def group_b(dz):
        return (x_at * ZC + lax.rem(zc_at + dz, ZC), s)

    a_steps = [(dx, dy) for dx in range(X_SIZE) for dy in range(SIBS) if dx or dy]

    loads = [
        pltpu.make_async_copy(vel_hbm.at[0], field.at[0], in_sem.at[VEL_IN]),
        pltpu.make_async_copy(pick_hbm, pick, in_sem.at[PICK_IN]),
        pltpu.make_async_copy(counts_hbm, counts, in_sem.at[COUNTS_IN]),
        pltpu.make_async_copy(nbr_hbm, nbr_in, in_sem.at[NBR_IN]),
        pltpu.make_async_copy(press_hbm, field.at[3], in_sem.at[PRESS_IN]),
        pltpu.make_async_copy(diff_hbm, diff, in_sem.at[DIFF_IN]),
        pltpu.make_async_copy(visc_hbm, visc, in_sem.at[VISC_IN]),
        pltpu.make_async_copy(small_hbm, small, in_sem.at[SMALL_IN]),
        pltpu.make_async_copy(levels_hbm, levels, in_sem.at[LEVELS_IN]),
        pltpu.make_async_copy(keys_hbm, keys, in_sem.at[KEYS_IN]),
        pltpu.make_async_copy(spread_hbm, spread, in_sem.at[SPREAD_IN]),
        pltpu.make_async_copy(vand_hbm, vand, in_sem.at[VAND_IN]),
    ]
    more_velocity = [
        pltpu.make_async_copy(vel_hbm.at[k], field.at[k], in_sem.at[VAND_IN + k])
        for k in (1, 2)
    ]
    for copy in [loads[VEL_IN], loads[PICK_IN]] + more_velocity:
        copy.start()
    for which in (COUNTS_IN, NBR_IN):
        loads[which].start()

    near_groups = [group_a(1, 0), group_a(X_SIZE - 1, 0), group_b(1), group_b(ZC - 1)]
    near = [(m, above), (m, below), (m_link, s), (m_link, above), (m_link, below)] + near_groups
    barrier = pltpu.get_barrier_semaphore()
    for device in near:
        pl.semaphore_signal(barrier, inc=1, device_id=device, device_id_type=MESH)

    loads[VEL_IN].wait()
    for copy in more_velocity:
        copy.wait()
    loads[PICK_IN].wait()
    for which in range(PRESS_IN, len(loads)):
        loads[which].start()
    lane = lax.broadcasted_iota(jnp.int32, (LEAVES, TILE), 1)
    rest = dot(field[0:3].reshape(3 * LEAVES, NODES), pick[...])
    shared = jnp.zeros((LEAVES, TILE), F32)
    for comp in range(3):
        first = field[comp, :, 0:TILE].astype(F32)
        last = field[comp, :, NODES - TILE : NODES].astype(F32)
        tab[0:LEAVES, TILE * comp : TILE * (comp + 1)] = jnp.where(lane < 64, first, last).astype(BF16)
        rows = rest[LEAVES * comp : LEAVES * (comp + 1)]
        tab[0:LEAVES, TILE * (3 + comp) : TILE * (4 + comp)] = rows[:, 0:TILE].astype(BF16)
        piece = rows[:, TILE : 2 * TILE]
        if comp:
            piece = pltpu.roll(piece, tail * comp, 1)
        shared = shared + piece
    tab[0:LEAVES, TILE * 6 : TILE * 7] = shared.astype(BF16)

    pl.semaphore_wait(barrier, len(near))

    def send(src, dst, send_sem, recv_sem, device):
        return pltpu.make_async_remote_copy(
            src_ref=src,
            dst_ref=dst,
            send_sem=send_sem,
            recv_sem=recv_sem,
            device_id=device,
            device_id_type=MESH,
        )

    def quarters(block, q, count=1):
        return tab.at[pl.ds(LEAVES * block + QUARTER * q, QUARTER * count)]

    def link_rows(b, first=0, rows=BAND):
        return tab.at[pl.ds(LINK_AT + BAND * b + first, rows)]

    def chip_rows(b):
        return tab.at[pl.ds(CHIP_AT + BAND * b, BAND)]

    ups, downs = [], []
    for k, (q_up, q_down, count) in enumerate(((0, 2, 1), (1, 3, 1), (2, 0, 2))):
        ups.append(
            send(
                quarters(0, q_up, count),
                quarters(2, q_up, count),
                ring_send.at[0, k],
                ring_recv.at[0, k],
                (m, above),
            )
        )
        downs.append(
            send(
                quarters(0, q_down, count),
                quarters(1, q_down, count),
                ring_send.at[1, k],
                ring_recv.at[1, k],
                (m, below),
            )
        )
    forwards = [
        send(quarters(2, 0), quarters(3, 0), fwd_send.at[0], fwd_recv.at[0], (m, above)),
        send(quarters(1, 2), quarters(3, 2), fwd_send.at[1], fwd_recv.at[1], (m, below)),
        send(quarters(2, 1), quarters(3, 1), fwd_send.at[2], fwd_recv.at[2], (m, above)),
        send(quarters(1, 3), quarters(3, 3), fwd_send.at[3], fwd_recv.at[3], (m, below)),
    ]
    links = [
        send(link_band, link_rows(0), link_send.at[0], link_recv.at[0], (m_link, s)),
        send(link_band, link_rows(2), link_send.at[1], link_recv.at[1], (m_link, above)),
        send(link_band, link_rows(1), link_send.at[2], link_recv.at[2], (m_link, below)),
    ]
    relays = [
        send(
            link_rows(2, 0, HALF_BAND),
            link_rows(3, 0, HALF_BAND),
            relay_send.at[0],
            relay_recv.at[0],
            (m, above),
        ),
        send(
            link_rows(1, HALF_BAND, HALF_BAND),
            link_rows(3, HALF_BAND, HALF_BAND),
            relay_send.at[1],
            relay_recv.at[1],
            (m, below),
        ),
    ]
    chips = [
        send(chip_band.at[b], chip_rows(b), chip_send.at[b], chip_recv.at[b], (m_chip, s))
        for b in range(4)
    ]
    turn = [0, 1, 3, 2]
    band_row = lax.broadcasted_iota(jnp.int32, (BAND, LEAVES), 0)
    band_col = lax.broadcasted_iota(jnp.int32, (BAND, LEAVES), 1)

    def band(b, last):
        live = counts[m * SIBS + lax.rem(s + turn[b], SIBS)]
        chosen = jnp.where(band_col == band_row + last * (live - BAND), 1.0, 0.0).astype(BF16)
        return dot(chosen, tab[LEAVES * b : LEAVES * (b + 1)]).astype(BF16)

    def send_chip(b):
        chip_band[b] = band(b, 1 - core)
        chips[b].start()

    round_peers = []
    for k in range(ROUNDS):
        round_peers.append(
            [group_a(1, 0), group_a(X_SIZE - 1, 0), (m, above), (m, below)]
            + [group_b(2**k), group_b(ZC - 2**k)]
        )

    def tell(k):
        for device in round_peers[k]:
            pl.semaphore_signal(known.at[k], inc=1, device_id=device, device_id_type=MESH)

    def hear(k):
        pl.semaphore_wait(known.at[k], len(round_peers[k]))

    ups[0].start()
    downs[0].start()
    loads[COUNTS_IN].wait()
    link_band[...] = band(0, core)
    links[0].start()
    loads[NBR_IN].wait()
    nbr = nbr_in[...]
    owner_sib = jnp.bitwise_and(jnp.right_shift(nbr, 7), 3)
    slot = jnp.bitwise_and(nbr, LEAVES - 1)
    step = jnp.right_shift(nbr, 9) - m
    offset = jnp.bitwise_and(owner_sib - s + SIBS, 3)
    block = jnp.where(offset == 2, 3, jnp.where(offset == 3, 2, offset))
    prior = lax.rem(m + MORTONS - 1, MORTONS) * SIBS
    prior_live = jnp.zeros_like(nbr)
    for k in range(SIBS):
        prior_live = jnp.where(owner_sib == k, counts[prior + k], prior_live)
    halo_row = 4 * LEAVES + block * BAND + slot
    row = jnp.where(
        step == 0,
        block * LEAVES + slot,
        jnp.where(
            step == 1,
            halo_row + (1 - core) * (4 * BAND),
            halo_row + core * (4 * BAND) - (prior_live - BAND),
        ),
    )
    row = jnp.where(nbr < 0, -1, row).astype(F32)
    pos_sq[...] = jnp.zeros_like(pos_sq)
    pos_sq[0:6, :] = row
    pos_sq[...] = pos_sq[...].T

    def gather(first, rows, fresh=False):
        col = lax.broadcasted_iota(jnp.int32, (LEAVES, rows), 1).astype(F32) + float(first)
        for dim in range(3):
            pair = []
            for face in (2 * dim, 2 * dim + 1):
                at = pos_sq[:, face : face + 1]
                pair.append(jnp.where(col == at, 1.0, 0.0))
            chosen = jnp.concatenate(pair, axis=0).astype(BF16)
            width = TILE * (3, 6, 7)[dim]
            got = dot(chosen, tab[first : first + rows, 0:width])
            for tile in range(width // TILE):
                lanes = slice(TILE * tile, TILE * (tile + 1))
                mask = small[MASK_AT + 7 * dim + tile, 0:1, :] > 0.5
                one = jnp.where(mask, got[0:LEAVES, lanes], got[LEAVES:, lanes]).astype(BF16)
                if fresh:
                    picked[dim, :, lanes] = one
                else:
                    picked[dim, :, lanes] += one

    send_chip(0)
    loads[SMALL_IN].wait()
    ups[1].start()
    downs[1].start()
    tell(0)
    gather(0, LEAVES, True)
    links[1].start()
    links[2].start()

    loads[PRESS_IN].wait()
    loads[DIFF_IN].wait()
    stacked = field[...].reshape(4 * LEAVES, NODES)
    for dim in range(3):
        grads[dim] = dot(stacked, diff[dim])
        if dim == 1:
            ups[2].start()
            downs[2].start()

    own_live = counts[m * SIBS + s]
    leaf_row = lax.broadcasted_iota(jnp.int32, (LEAVES, NODES), 0)
    live_rows = leaf_row < own_live

    def grad(comp, dim):
        return grads[dim, LEAVES * comp : LEAVES * (comp + 1), :]

    mass[...] = jnp.where(
        live_rows, -(grad(0, 0) + grad(1, 1) + grad(2, 2)) * mass_scale, 0.0
    )
    mass_out = pltpu.make_async_copy(mass, mass_out_ref, out_sem.at[0])
    mass_out.start()

    loads[VISC_IN].wait()
    stress = {}
    for i in range(3):
        for j in range(i, 3):
            stress[i, j] = (visc[...] * (grad(i, j) + grad(j, i))).astype(BF16)
    total = None
    for j in range(3):
        rows = jnp.concatenate([stress[min(i, j), max(i, j)] for i in range(3)], axis=0)
        term = dot(rows, diff[j])
        total = term if total is None else total + term
    mult = jnp.concatenate([small[MULT_AT + t, 0:1, :] for t in range(4)], axis=1)
    for comp in range(3):
        jump = field[comp].astype(F32) * mult
        local[comp] = (
            penalty * visc[...] * jump
            - total[LEAVES * comp : LEAVES * (comp + 1)]
            + grad(3, comp)
        ) * out_scale
    ups[0].wait_recv()
    forwards[0].start()
    downs[0].wait_recv()
    forwards[1].start()
    hear(0)
    tell(1)
    ups[1].wait_recv()
    forwards[2].start()
    downs[1].wait_recv()
    forwards[3].start()
    links[1].wait_recv()
    relays[0].start()
    links[2].wait_recv()
    relays[1].start()
    hear(1)
    tell(2)

    loads[LEVELS_IN].wait()
    loads[KEYS_IN].wait()
    level = levels[...]
    shift_bits = 3 * (LMAX - level)
    anchor = jnp.left_shift(jnp.right_shift(keys[...], shift_bits), shift_bits)
    span = jnp.left_shift(jnp.ones_like(level), LMAX - level).astype(F32)
    at_box = []
    box_center = []
    for dim, bit0 in enumerate((2, 1, 0)):
        cell = jnp.zeros_like(anchor)
        corner = 0
        for bit in range(LMAX):
            cell = cell + jnp.left_shift(
                jnp.bitwise_and(jnp.right_shift(anchor, 3 * bit + bit0), 1), bit
            )
            up_bit = 3 * bit + bit0 - (3 * LMAX - 6)
            if up_bit >= 0:
                corner = corner + lax.rem(lax.div(m, 2**up_bit), 2) * 2**bit
        center = corner.astype(F32) * FINEST + 0.5 * BOX_SIDE
        box_center.append(center)
        at_box.append(((cell.astype(F32) + 0.5 * span) * FINEST - center) / BOX_SCALE)
    half = 0.5 * span * FINEST / BOX_SCALE
    sub = lax.broadcasted_iota(jnp.int32, (8, TILE), 0)

    def power_rows(value):
        value = jnp.broadcast_to(value, (8, TILE))
        power = jnp.ones((8, TILE), F32)
        rows = power
        for k in range(1, DEG + 1):
            power = power * value
            rows = jnp.where(sub == k, power, rows)
        return rows

    half_rows = power_rows(half)
    half_wide = jnp.broadcast_to(half, (8, TILE))
    scales = [half_rows]
    for _ in range(DEG):
        scales.append(scales[-1] * half_wide)
    x_rows = power_rows(at_box[0])
    x_tiles = []
    half_power = jnp.ones((8, TILE), F32)
    for k in range(DEG + 1):
        turned = x_rows if k == 0 else pltpu.roll(x_rows, k, 0)
        x_tiles.append(small[k] * turned * half_power)
        half_power = half_power * half_wide
    x_table = jnp.concatenate(x_tiles, axis=1)
    x_high, x_low = split(x_table)
    y_wide = jnp.broadcast_to(at_box[1], (8, TILE))
    z_wide = jnp.broadcast_to(at_box[2], (8, TILE))
    z_coef = []
    z_power = jnp.ones((8, TILE), F32)
    for k in range(DEG + 1):
        z_coef.append(small[k] * z_power)
        z_power = z_power * z_wide

    downs[2].wait_recv()
    send_chip(1)
    ups[2].wait_recv()
    send_chip(2)
    gather(LEAVES, 2 * LEAVES)
    for k in range(4):
        forwards[k].wait_recv()
    send_chip(3)
    gather(3 * LEAVES, LEAVES)
    loads[SPREAD_IN].wait()
    loads[VAND_IN].wait()
    hear(2)
    links[0].wait_recv()
    for k in range(2):
        relays[k].wait_recv()
    for b in range(4):
        chips[b].wait_recv()
    gather(LINK_AT, 8 * BAND)

    rows = []
    for comp in range(3):
        parts = []
        for dim in range(3):
            for tile in FACE_TILES[dim]:
                at = 6 if tile == 2 else 3 * tile + comp
                value = picked[dim, :, TILE * at : TILE * (at + 1)]
                if tile == 2:
                    mine = (lane >= tail * comp) & (lane < tail * (comp + 1))
                    value = jnp.where(mine, value.astype(F32), 0.0).astype(BF16)
                parts.append(value)
        rows.append(jnp.concatenate(parts, axis=1))
    across = dot(jnp.concatenate(rows, axis=0), spread[...])
    for comp in range(3):
        there = across[LEAVES * comp : LEAVES * (comp + 1)]
        value = local[comp] - (penalty * out_scale) * visc[...] * there
        force[comp] = jnp.where(live_rows, value, 0.0)
    force_out = pltpu.make_async_copy(force, force_out_ref, out_sem.at[1])
    force_out.start()

    f_high, f_low = split(force[...].reshape(3 * LEAVES, NODES))
    leaf_moments = (
        dot_nt(vand[0], f_high) + dot_nt(vand[0], f_low) + dot_nt(vand[1], f_high)
    )
    for comp in range(3):
        for jx in range(6):
            columns = []
            for jy in range(6):
                first = jx * 48 + jy * 8
                base = leaf_moments[first : first + 8, TILE * comp : TILE * (comp + 1)] * scales[jy]
                moved = base * z_coef[0]
                for k in range(1, DEG + 1):
                    moved = moved + z_coef[k] * pltpu.roll(base, k, 0)
                columns.append(moved)
            for low in range(1, DEG + 1):
                for at in range(DEG, low - 1, -1):
                    columns[at] = columns[at] + y_wide * columns[at - 1]
            for jy in range(6):
                first = 36 * comp + 6 * jy
                mcat[first : first + 6, TILE * jx : TILE * (jx + 1)] = columns[jy][0:6]
    mcat[108:TILE, :] = jnp.zeros((TILE - 108, 6 * TILE), F32)
    c_high, c_low = split(mcat[...])
    own_box = dot_nt(x_high, c_high) + dot_nt(x_low, c_high) + dot_nt(x_high, c_low)

    shifted = own_box * small[18]
    shift_by = [(center - 0.5) / 0.5 for center in box_center]
    for dim, (axis, stride, base) in enumerate(((0, 1, 0), (1, 6, 6), (1, 1, 12))):
        moved = shifted
        power = 1.0
        for k in range(1, DEG + 1):
            power = power * shift_by[dim]
            moved = moved + small[base + k] * power * pltpu.roll(shifted, stride * k, axis)
        shifted = moved

    part[0] = own_box
    part[1] = shifted
    recv_box[s] = own_box
    box_copies = [
        send(
            part.at[0],
            recv_box.at[s],
            box_send.at[k],
            box_recv.at[k],
            (m, lax.rem(s + 1 + k, SIBS)),
        )
        for k in range(SIBS - 1)
    ]
    give = send(part.at[1], other_core, core_send.at[0], core_recv.at[0], (m_chip, s))
    back = send(whole, whole, core_send.at[1], core_recv.at[1], (m_chip, s))
    at_a = x_at * SIBS + s
    z_at = lax.div(zc_at, CORES)
    a_copies = [
        send(sum_a, recv_a.at[at_a], a_send.at[k], a_recv.at[k], group_a(*step))
        for k, step in enumerate(a_steps)
    ]
    b_copies = [
        send(sum_b, recv_b.at[z_at], b_send.at[k], b_recv.at[k], group_b(CORES * (k + 1)))
        for k in range(Z_SIZE - 1)
    ]

    @pl.when(core == 0)
    def _():
        give.start()

    for copy in box_copies:
        copy.start()

    @pl.when(core == 1)
    def _():
        give.wait_recv()
        chip_sum = part[1] + other_core[...]
        sum_a[...] = chip_sum
        recv_a[at_a] = chip_sum
        for copy in a_copies:
            copy.start()

    for copy in box_copies:
        copy.wait_recv()
    box = recv_box[0]
    for k in range(1, SIBS):
        box = box + recv_box[k]
    flat_rows(box, flat.at[0])
    box_out = pltpu.make_async_copy(flat.at[0], box_out_ref, out_sem.at[2])
    box_out.start()

    @pl.when(core == 1)
    def _():
        for copy in a_copies:
            copy.wait_recv()
        plane = recv_a[0]
        for k in range(1, X_SIZE * SIBS):
            plane = plane + recv_a[k]
        sum_b[...] = plane
        recv_b[z_at] = plane
        for copy in b_copies:
            copy.start()
        for copy in b_copies:
            copy.wait_recv()
        total = recv_b[0]
        for k in range(1, Z_SIZE):
            total = total + recv_b[k]
        whole[...] = total
        back.start()

    @pl.when(core == 0)
    def _():
        back.wait_recv()

    flat_rows(whole[...], flat.at[1])
    root_out = pltpu.make_async_copy(flat.at[1], root_out_ref, out_sem.at[3])
    root_out.start()

    for copy in ups + downs + links + forwards + relays + chips + box_copies:
        copy.wait_send()

    @pl.when(core == 0)
    def _():
        give.wait_send()

    @pl.when(core == 1)
    def _():
        for copy in a_copies + b_copies + [back]:
            copy.wait_send()

    mass_out.wait()
    force_out.wait()
    box_out.wait()
    root_out.wait()


def finish(force, mass, box, root, force_out, mass_out, box_out, root_out, sem):
    pairs = [(force.at[k], force_out.at[k]) for k in range(3)]
    pairs += [(mass, mass_out), (box, box_out), (root, root_out)]
    copies = [pltpu.make_async_copy(a, b, sem.at[k]) for k, (a, b) in enumerate(pairs)]
    for copy in copies:
        copy.start()
    for copy in copies:
        copy.wait()


def on_device(velocity, pressure, viscosity, levels, morton_keys, counts, neighbors):
    diff, pick, spread, vander, small, tail = tables()
    as_bf16 = lambda a: jnp.asarray(a.astype(np.float32)).astype(BF16)
    vander32 = vander.astype(np.float32)
    v_high = vander32.astype(jnp.bfloat16)
    v_low = (vander32 - v_high.astype(np.float32)).astype(jnp.bfloat16)
    vand = np.stack([v_high, v_low])
    dma = pltpu.SemaphoreType.DMA
    any_space = pl.BlockSpec(memory_space=pl.ANY)
    hbm = pl.BlockSpec(memory_space=pltpu.HBM)
    results = (
        jax.ShapeDtypeStruct((3, LEAVES, NODES), F32),
        jax.ShapeDtypeStruct((LEAVES, NODES), F32),
        jax.ShapeDtypeStruct((3, 1, MOMENTS), F32),
        jax.ShapeDtypeStruct((3, 1, MOMENTS), F32),
    )
    raw = pl.pallas_call(
        functools.partial(kernel, tail),
        out_shape=tuple(pltpu.VMEM(r.shape, r.dtype) for r in results),
        in_specs=[hbm] * 12,
        out_specs=(any_space,) * 4,
        scratch_shapes=[
            pltpu.VMEM((4, LEAVES, NODES), BF16),
            pltpu.VMEM((NODES, 2 * TILE), BF16),
            pltpu.SMEM((MORTONS * SIBS,), jnp.int32),
            pltpu.VMEM((6, LEAVES), jnp.int32),
            pltpu.VMEM((3, NODES, NODES), BF16),
            pltpu.VMEM((LEAVES, NODES), F32),
            pltpu.VMEM((MASK_AT + 21, 8, TILE), F32),
            pltpu.VMEM((1, LEAVES), jnp.int32),
            pltpu.VMEM((1, LEAVES), jnp.int32),
            pltpu.VMEM((6 * TILE, NODES), BF16),
            pltpu.VMEM((2, 288, NODES), BF16),
            pltpu.VMEM((ROWS, LANES), BF16),
            pltpu.VMEM((BAND, LANES), BF16),
            pltpu.VMEM((4, BAND, LANES), BF16),
            pltpu.VMEM((3, 4 * LEAVES, NODES), F32),
            pltpu.VMEM((3, LEAVES, NODES), F32),
            pltpu.VMEM((3, LEAVES, LANES), BF16),
            pltpu.VMEM((3, LEAVES, NODES), F32),
            pltpu.VMEM((LEAVES, NODES), F32),
            pltpu.VMEM((LEAVES, LEAVES), F32),
            pltpu.VMEM((TILE, 6 * TILE), F32),
            pltpu.VMEM((2, 8, TILE), F32),
            pltpu.VMEM((SIBS, 8, TILE), F32),
            pltpu.VMEM((8, TILE), F32),
            pltpu.VMEM((X_SIZE * SIBS, 8, TILE), F32),
            pltpu.VMEM((Z_SIZE, 8, TILE), F32),
            pltpu.VMEM((8, TILE), F32),
            pltpu.VMEM((8, TILE), F32),
            pltpu.VMEM((8, TILE), F32),
            pltpu.VMEM((2, 3, 1, MOMENTS), F32),
            dma((14,)),
            dma((4,)),
            dma((2, 3)),
            dma((2, 3)),
            dma((4,)),
            dma((4,)),
            dma((3,)),
            dma((3,)),
            dma((2,)),
            dma((2,)),
            dma((4,)),
            dma((4,)),
            dma((3,)),
            dma((3,)),
            dma((2,)),
            dma((2,)),
            dma((15,)),
            dma((15,)),
            dma((7,)),
            dma((7,)),
            pltpu.SemaphoreType.REGULAR((ROUNDS,)),
        ],
        compiler_params=pltpu.CompilerParams(
            collective_id=0, has_side_effects=True, vmem_limit_bytes=60 * 2**20
        ),
    )(
        velocity.transpose(1, 0, 2),
        as_bf16(pick),
        counts,
        neighbors.T,
        pressure,
        as_bf16(diff),
        viscosity,
        jnp.asarray(small.astype(np.float32)),
        levels.reshape(1, LEAVES),
        morton_keys.reshape(1, LEAVES),
        as_bf16(spread),
        jnp.asarray(vand),
    )
    force, mass, box, root = pl.pallas_call(
        finish,
        out_shape=results,
        in_specs=[any_space] * 4,
        out_specs=(any_space,) * 4,
        scratch_shapes=[dma((6,))],
    )(*[pltpu.with_memory_space_constraint(r, pltpu.VMEM) for r in raw])
    return (
        force.transpose(1, 0, 2),
        mass,
        box.transpose(1, 0, 2),
        root.transpose(1, 0, 2),
    )


def solution(mesh):
    in_specs = (
        P(("morton", "sib"), None, None),
        P(("morton", "sib"), None),
        P(("morton", "sib"), None),
        P(("morton", "sib")),
        P(("morton", "sib")),
        P(),
        P(("morton", "sib"), None),
    )
    out_specs = (
        P(("morton", "sib"), None, None),
        P(("morton", "sib"), None),
        P("morton", None, None),
        P("morton", None, None),
    )
    return jax.shard_map(
        on_device, mesh=mesh, in_specs=in_specs, out_specs=out_specs, check_vma=False
    )
```

```python
import functools
import math

import jax
import jax.numpy as jnp
import numpy as np
from jax import lax
from jax.experimental import pallas as pl
from jax.experimental.pallas import tpu as pltpu
from jax.sharding import PartitionSpec as P

DEG = 5
LMAX = 7
MOMENTS = 216
LEAVES = 128
NODES = 512
LANES = 896
BAND = 32
TILE = 128
MESH = pl.DeviceIdType.MESH
F32 = jnp.float32
BF16 = jnp.bfloat16

penalty = 256.0
out_scale = 1.0 / 1024.0
mass_scale = 1.0 / 32.0

X_SIZE, Z_SIZE, CORES, SIBS = 4, 8, 2, 4
ZC = Z_SIZE * CORES
MORTONS = X_SIZE * ZC


def cheb():
    points = -np.cos(np.pi * np.arange(8) / 7.0)
    weights = np.array([(-1.0) ** k for k in range(8)])
    weights[0] *= 0.5
    weights[7] *= 0.5
    derivative = np.zeros((8, 8))
    for row in range(8):
        for col in range(8):
            if row != col:
                derivative[row, col] = weights[col] / weights[row] / (points[row] - points[col])
        derivative[row, row] = -np.sum(derivative[row])
    return points, derivative


def node_of(coords):
    return 64 * coords[0] + 8 * coords[1] + coords[2]


def coords_of(node):
    return [node // 64, node // 8 % 8, node % 8]


def surface_lists():
    x_nodes = [node_of([7 * side, b, c]) for side in range(2) for b in range(8) for c in range(8)]
    inner = [n for n in range(NODES) if coords_of(n)[0] not in (0, 7)]
    on_y = [n for n in inner if coords_of(n)[1] in (0, 7)]
    only_z = [n for n in inner if n not in on_y and coords_of(n)[2] in (0, 7)]
    return x_nodes, on_y + only_z


FACE_TILES = ((0,), (0, 1), (0, 1, 2))
MULT_AT, MASK_AT = 19, 23


def tables():
    points, derivative = cheb()
    eye = np.eye(8)
    directional = [
        np.kron(np.kron(derivative, eye), eye),
        np.kron(np.kron(eye, derivative), eye),
        np.kron(np.kron(eye, eye), derivative),
    ]
    diff = np.stack([m.T for m in directional])
    x_nodes, rest = surface_lists()
    tail = len(rest) - TILE
    pick = np.zeros((NODES, 2 * TILE))
    for k, node in enumerate(rest):
        pick[node, k] = 1.0
    tiles = [list(x_nodes), list(rest[:TILE]), [-1] * TILE]
    for comp in range(3):
        for k in range(tail):
            tiles[2][tail * comp + k] = rest[TILE + k]
    spread = np.zeros((6 * TILE, NODES))
    small = np.zeros((MASK_AT + 21, 8, TILE))
    sides = np.zeros((6, 16, LANES))
    slot = 0
    for dim in range(3):
        for tile in FACE_TILES[dim]:
            for lane, node in enumerate(tiles[tile]):
                if node < 0:
                    continue
                coords = coords_of(node)
                if coords[dim] in (0, 7):
                    other = list(coords)
                    other[dim] = 7 - coords[dim]
                    spread[slot * TILE + lane, node_of(other)] = 1.0
                    for at in (6,) if tile == 2 else range(3 * tile, 3 * tile + 3):
                        sides[2 * dim + (coords[dim] == 0), :, TILE * at + lane] = 1.0
                        if coords[dim] == 7:
                            small[MASK_AT + 7 * dim + at, :, lane] = 1.0
            slot += 1
    for node in range(NODES):
        count = sum(1 for c in coords_of(node) if c in (0, 7))
        small[MULT_AT + node // TILE, :, node % TILE] = count
    vander = np.zeros((288, NODES))
    for jx in range(6):
        for jy in range(6):
            for jz in range(6):
                for node in range(NODES):
                    a, b, c = coords_of(node)
                    vander[jx * 48 + jy * 8 + jz, node] = (
                        points[a] ** jx * points[b] ** jy * points[c] ** jz / 512.0
                    )
    for k in range(6):
        for a in range(6):
            if a >= k:
                small[k, a, :] = math.comb(a, k)
        for lane in range(108):
            ay, az = lane // 6 % 6, lane % 6
            if ay >= k:
                small[6 + k, :, lane] = math.comb(ay, k)
            if az >= k:
                small[12 + k, :, lane] = math.comb(az, k)
    for ax in range(6):
        for lane in range(108):
            small[18, ax, lane] = BOX_IN_ROOT ** (ax + lane // 6 % 6 + lane % 6)
    return diff, pick, spread, sides, vander, small, tail


BOX_CELLS = 2 ** ((3 * LMAX - 6) // 3)
FINEST = 1.0 / 2**LMAX
BOX_SIDE = BOX_CELLS * FINEST
BOX_SCALE = 0.5 * BOX_SIDE
BOX_IN_ROOT = BOX_SCALE / 0.5

(
    VEL_IN,
    PICK_IN,
    COUNTS_IN,
    NBR_IN,
    PRESS_IN,
    DIFF_IN,
    VISC_IN,
    SMALL_IN,
    LEVELS_IN,
    KEYS_IN,
    SPREAD_IN,
    SIDES_IN,
    VAND_IN,
) = range(13)
QUARTER = LEAVES // 4
HALF_BAND = BAND // 2
ROUNDS = 4
ORDERS = 288
BANDS_AT, LAST_AT, ROWS = 4 * LEAVES, 4 * LEAVES + 6 * BAND, 4 * LEAVES + 8 * BAND


def dot(a, b):
    return jnp.dot(a, b, preferred_element_type=F32)


def dot_nt(a, b):
    return lax.dot_general(a, b, (((1,), (1,)), ((), ())), preferred_element_type=F32)


def split(value):
    high = value.astype(BF16)
    return high, (value - high.astype(F32)).astype(BF16)


def flat_rows(packed, out_ref):
    lane = lax.broadcasted_iota(jnp.int32, (8, TILE), 1)
    sub = lax.broadcasted_iota(jnp.int32, (8, TILE), 0)
    first_tile = (sub < 3) | ((sub == 3) & (lane >= 108))
    valid = jnp.bitwise_and(lane - 36 * sub, TILE - 1) < 36
    turned = {0: packed}
    for by in range(-2, DEG + 1):
        if by:
            turned[by] = pltpu.roll(packed, 36 * by % TILE, 1)
    for comp in range(3):
        rows = turned[-comp]
        for ax in range(1, DEG + 1):
            rows = jnp.where(sub == ax, turned[ax - comp], rows)
        rows = jnp.where(valid & (sub < 6), rows, 0.0)
        near = jnp.sum(jnp.where(first_tile, rows, 0.0), axis=0, keepdims=True)
        far = jnp.sum(jnp.where(first_tile, 0.0, rows), axis=0, keepdims=True)
        out_ref[comp, :, 0:TILE] = near
        out_ref[comp, :, TILE:MOMENTS] = far[:, : MOMENTS - TILE]


def kernel(
    tail,
    vel_hbm,
    pick_hbm,
    counts_hbm,
    nbr_hbm,
    press_hbm,
    diff_hbm,
    visc_hbm,
    small_hbm,
    levels_hbm,
    keys_hbm,
    spread_hbm,
    sides_hbm,
    vand_hbm,
    force_out_ref,
    mass_out_ref,
    box_out_ref,
    root_out_ref,
    field,
    pick,
    counts,
    nbr_in,
    diff,
    visc,
    small,
    levels,
    keys,
    spread,
    sides,
    vand,
    tab,
    link_band,
    chip_band,
    grads,
    local,
    picked,
    force,
    mass,
    pos_sq,
    local_moments,
    across_live,
    mcat,
    part,
    recv_box,
    recv_a,
    recv_b,
    sum_b,
    flat,
    in_sem,
    out_sem,
    ring_send,
    ring_recv,
    fwd_send,
    fwd_recv,
    link_send,
    link_recv,
    relay_send,
    relay_recv,
    chip_send,
    chip_recv,
    box_send,
    box_recv,
    a_send,
    a_recv,
    b_send,
    b_recv,
    known,
):
    m = lax.axis_index("morton")
    s = lax.axis_index("sib")
    x_at = lax.div(m, ZC)
    zc_at = lax.rem(m, ZC)
    core = lax.rem(m, CORES)
    above = lax.rem(s + 1, SIBS)
    below = lax.rem(s + SIBS - 1, SIBS)
    m_chip = m + 1 - 2 * core
    m_link = lax.rem(m + MORTONS - 1 + 2 * core, MORTONS)

    def group_a(dx, dy):
        return (lax.rem(x_at + dx, X_SIZE) * ZC + zc_at, lax.rem(s + dy, SIBS))

    def group_b(dz):
        return (x_at * ZC + lax.rem(zc_at + dz, ZC), s)

    a_steps = [(dx, dy) for dx in range(X_SIZE) for dy in range(SIBS) if dx or dy]

    loads = [
        pltpu.make_async_copy(vel_hbm.at[0], field.at[0], in_sem.at[VEL_IN]),
        pltpu.make_async_copy(pick_hbm, pick, in_sem.at[PICK_IN]),
        pltpu.make_async_copy(counts_hbm, counts, in_sem.at[COUNTS_IN]),
        pltpu.make_async_copy(nbr_hbm, nbr_in, in_sem.at[NBR_IN]),
        pltpu.make_async_copy(press_hbm, field.at[3], in_sem.at[PRESS_IN]),
        pltpu.make_async_copy(diff_hbm, diff, in_sem.at[DIFF_IN]),
        pltpu.make_async_copy(visc_hbm, visc, in_sem.at[VISC_IN]),
        pltpu.make_async_copy(small_hbm, small, in_sem.at[SMALL_IN]),
        pltpu.make_async_copy(levels_hbm, levels, in_sem.at[LEVELS_IN]),
        pltpu.make_async_copy(keys_hbm, keys, in_sem.at[KEYS_IN]),
        pltpu.make_async_copy(spread_hbm, spread, in_sem.at[SPREAD_IN]),
        pltpu.make_async_copy(sides_hbm, sides, in_sem.at[SIDES_IN]),
        pltpu.make_async_copy(vand_hbm, vand, in_sem.at[VAND_IN]),
    ]
    more_velocity = [
        pltpu.make_async_copy(vel_hbm.at[k], field.at[k], in_sem.at[VAND_IN + k])
        for k in (1, 2)
    ]
    for copy in [loads[VEL_IN], loads[PICK_IN]] + more_velocity:
        copy.start()
    for which in (COUNTS_IN, NBR_IN):
        loads[which].start()

    near_groups = [group_a(1, 0), group_a(X_SIZE - 1, 0), group_b(1), group_b(ZC - 1)]
    near = [(m, above), (m, below), (m_link, s), (m_link, above), (m_link, below)] + near_groups
    barrier = pltpu.get_barrier_semaphore()
    for device in near:
        pl.semaphore_signal(barrier, inc=1, device_id=device, device_id_type=MESH)

    loads[VEL_IN].wait()
    for copy in more_velocity:
        copy.wait()
    loads[PICK_IN].wait()
    for which in range(PRESS_IN, len(loads)):
        loads[which].start()
    lane = lax.broadcasted_iota(jnp.int32, (LEAVES, TILE), 1)
    rest = dot(field[0:3].reshape(3 * LEAVES, NODES), pick[...])
    shared = jnp.zeros((LEAVES, TILE), F32)
    for comp in range(3):
        first = field[comp, :, 0:TILE].astype(F32)
        last = field[comp, :, NODES - TILE : NODES].astype(F32)
        tab[0:LEAVES, TILE * comp : TILE * (comp + 1)] = jnp.where(lane < 64, first, last).astype(BF16)
        rows = rest[LEAVES * comp : LEAVES * (comp + 1)]
        tab[0:LEAVES, TILE * (3 + comp) : TILE * (4 + comp)] = rows[:, 0:TILE].astype(BF16)
        piece = rows[:, TILE : 2 * TILE]
        if comp:
            piece = pltpu.roll(piece, tail * comp, 1)
        shared = shared + piece
    tab[0:LEAVES, TILE * 6 : TILE * 7] = shared.astype(BF16)

    pl.semaphore_wait(barrier, len(near))

    def send(src, dst, send_sem, recv_sem, device):
        return pltpu.make_async_remote_copy(
            src_ref=src,
            dst_ref=dst,
            send_sem=send_sem,
            recv_sem=recv_sem,
            device_id=device,
            device_id_type=MESH,
        )

    def quarters(block, q, count=1):
        return tab.at[pl.ds(LEAVES * block + QUARTER * q, QUARTER * count)]

    def link_rows(b, first=0, rows=BAND):
        return tab.at[pl.ds((LAST_AT if b == 3 else BANDS_AT + BAND * b) + first, rows)]

    def chip_rows(b):
        return tab.at[pl.ds(LAST_AT + BAND if b == 3 else BANDS_AT + BAND * (3 + b), BAND)]

    ups, downs = [], []
    for k, (q_up, q_down, count) in enumerate(((0, 2, 1), (1, 3, 1), (2, 0, 2))):
        ups.append(
            send(
                quarters(0, q_up, count),
                quarters(2, q_up, count),
                ring_send.at[0, k],
                ring_recv.at[0, k],
                (m, above),
            )
        )
        downs.append(
            send(
                quarters(0, q_down, count),
                quarters(1, q_down, count),
                ring_send.at[1, k],
                ring_recv.at[1, k],
                (m, below),
            )
        )
    forwards = [
        send(quarters(2, 0), quarters(3, 0), fwd_send.at[0], fwd_recv.at[0], (m, above)),
        send(quarters(1, 2), quarters(3, 2), fwd_send.at[1], fwd_recv.at[1], (m, below)),
        send(quarters(2, 1), quarters(3, 1), fwd_send.at[2], fwd_recv.at[2], (m, above)),
        send(quarters(1, 3), quarters(3, 3), fwd_send.at[3], fwd_recv.at[3], (m, below)),
    ]
    links = [
        send(link_band, link_rows(0), link_send.at[0], link_recv.at[0], (m_link, s)),
        send(link_band, link_rows(2), link_send.at[1], link_recv.at[1], (m_link, above)),
        send(link_band, link_rows(1), link_send.at[2], link_recv.at[2], (m_link, below)),
    ]
    relays = [
        send(
            link_rows(2, 0, HALF_BAND),
            link_rows(3, 0, HALF_BAND),
            relay_send.at[0],
            relay_recv.at[0],
            (m, above),
        ),
        send(
            link_rows(1, HALF_BAND, HALF_BAND),
            link_rows(3, HALF_BAND, HALF_BAND),
            relay_send.at[1],
            relay_recv.at[1],
            (m, below),
        ),
    ]
    chips = [
        send(chip_band.at[b], chip_rows(b), chip_send.at[b], chip_recv.at[b], (m_chip, s))
        for b in range(4)
    ]
    turn = [0, 1, 3, 2]
    band_row = lax.broadcasted_iota(jnp.int32, (BAND, LEAVES), 0)
    band_col = lax.broadcasted_iota(jnp.int32, (BAND, LEAVES), 1)

    def band(b, last):
        live = counts[m * SIBS + lax.rem(s + turn[b], SIBS)]
        chosen = jnp.where(band_col == band_row + last * (live - BAND), 1.0, 0.0).astype(BF16)
        return dot(chosen, tab[LEAVES * b : LEAVES * (b + 1)]).astype(BF16)

    def send_chip(b):
        chip_band[b] = band(b, 1 - core)
        chips[b].start()

    round_peers = []
    for k in range(ROUNDS):
        peers = [group_a(1, 0), group_a(X_SIZE - 1, 0), (m, above), (m, below)]
        if k < 3:
            peers += [group_b(2**k), group_b(ZC - 2**k)]
        round_peers.append(peers)

    def tell(k):
        for device in round_peers[k]:
            pl.semaphore_signal(known.at[k], inc=1, device_id=device, device_id_type=MESH)

    def hear(k):
        pl.semaphore_wait(known.at[k], len(round_peers[k]))

    ups[0].start()
    downs[0].start()
    ups[1].start()
    downs[1].start()
    loads[COUNTS_IN].wait()
    link_band[...] = band(0, core)
    links[0].start()
    loads[NBR_IN].wait()
    nbr = nbr_in[...]
    owner_sib = jnp.bitwise_and(jnp.right_shift(nbr, 7), 3)
    slot = jnp.bitwise_and(nbr, LEAVES - 1)
    step = jnp.right_shift(nbr, 9) - m
    offset = jnp.bitwise_and(owner_sib - s + SIBS, 3)
    block = jnp.where(offset == 2, 3, jnp.where(offset == 3, 2, offset))
    prior = lax.rem(m + MORTONS - 1, MORTONS) * SIBS
    prior_live = jnp.zeros_like(nbr)
    for k in range(SIBS):
        prior_live = jnp.where(owner_sib == k, counts[prior + k], prior_live)
    apart = jnp.where(block == 3, BAND, 3 * BAND)
    halo_row = jnp.where(block == 3, LAST_AT, BANDS_AT + block * BAND) + slot
    row = jnp.where(
        step == 0,
        block * LEAVES + slot,
        jnp.where(
            step == 1,
            halo_row + (1 - core) * apart,
            halo_row + core * apart - (prior_live - BAND),
        ),
    )
    row = jnp.where(nbr < 0, -1, row).astype(F32)
    pos_sq[...] = jnp.zeros_like(pos_sq)
    pos_sq[0:6, :] = row
    pos_sq[...] = pos_sq[...].T

    def gather(first, rows, fresh=False):
        col = lax.broadcasted_iota(jnp.int32, (LEAVES, rows), 1).astype(F32) + float(first)
        for dim in range(3):
            pair = []
            for face in (2 * dim, 2 * dim + 1):
                at = pos_sq[:, face : face + 1]
                pair.append(jnp.where(col == at, 1.0, 0.0))
            chosen = jnp.concatenate(pair, axis=0).astype(BF16)
            width = TILE * (3, 6, 7)[dim]
            got = dot(chosen, tab[first : first + rows, 0:width])
            for tile in range(width // TILE):
                lanes = slice(TILE * tile, TILE * (tile + 1))
                mask = small[MASK_AT + 7 * dim + tile, 0:1, :] > 0.5
                one = jnp.where(mask, got[0:LEAVES, lanes], got[LEAVES:, lanes]).astype(BF16)
                if fresh:
                    picked[dim, :, lanes] = one
                else:
                    picked[dim, :, lanes] += one

    links[1].start()
    links[2].start()
    send_chip(0)
    loads[SMALL_IN].wait()
    tell(0)
    gather(0, LEAVES, True)

    loads[PRESS_IN].wait()
    loads[DIFF_IN].wait()
    stacked = field[...].reshape(4 * LEAVES, NODES)
    for dim in range(3):
        grads[dim] = dot(stacked, diff[dim])
        if dim == 1:
            ups[2].start()
            downs[2].start()

    own_live = counts[m * SIBS + s]
    leaf_row = lax.broadcasted_iota(jnp.int32, (LEAVES, NODES), 0)
    live_rows = leaf_row < own_live

    def grad(comp, dim):
        return grads[dim, LEAVES * comp : LEAVES * (comp + 1), :]

    mass[...] = jnp.where(
        live_rows, -(grad(0, 0) + grad(1, 1) + grad(2, 2)) * mass_scale, 0.0
    )
    mass_out = pltpu.make_async_copy(mass, mass_out_ref, out_sem.at[0])
    mass_out.start()

    loads[VISC_IN].wait()
    stress = {}
    for i in range(3):
        for j in range(i, 3):
            stress[i, j] = (visc[...] * (grad(i, j) + grad(j, i))).astype(BF16)
    total = None
    for j in range(3):
        rows = jnp.concatenate([stress[min(i, j), max(i, j)] for i in range(3)], axis=0)
        term = dot(rows, diff[j])
        total = term if total is None else total + term
    mult = jnp.concatenate([small[MULT_AT + t, 0:1, :] for t in range(4)], axis=1)
    for comp in range(3):
        jump = field[comp].astype(F32) * mult
        value = (
            penalty * visc[...] * jump
            - total[LEAVES * comp : LEAVES * (comp + 1)]
            + grad(3, comp)
        ) * out_scale
        local[comp] = jnp.where(live_rows, value, 0.0)
    ups[0].wait_recv()
    forwards[0].start()
    downs[0].wait_recv()
    forwards[1].start()
    hear(0)
    tell(1)
    ups[1].wait_recv()
    forwards[2].start()
    downs[1].wait_recv()
    forwards[3].start()
    links[1].wait_recv()
    relays[0].start()
    links[2].wait_recv()
    relays[1].start()
    hear(1)
    tell(2)

    loads[LEVELS_IN].wait()
    loads[KEYS_IN].wait()
    level = levels[...]
    shift_bits = 3 * (LMAX - level)
    anchor = jnp.left_shift(jnp.right_shift(keys[...], shift_bits), shift_bits)
    span = jnp.left_shift(jnp.ones_like(level), LMAX - level).astype(F32)
    at_box = []
    box_center = []
    for dim, bit0 in enumerate((2, 1, 0)):
        cell = jnp.zeros_like(anchor)
        corner = 0
        for bit in range(LMAX):
            cell = cell + jnp.left_shift(
                jnp.bitwise_and(jnp.right_shift(anchor, 3 * bit + bit0), 1), bit
            )
            up_bit = 3 * bit + bit0 - (3 * LMAX - 6)
            if up_bit >= 0:
                corner = corner + lax.rem(lax.div(m, 2**up_bit), 2) * 2**bit
        center = corner.astype(F32) * FINEST + 0.5 * BOX_SIDE
        box_center.append(center)
        at_box.append(((cell.astype(F32) + 0.5 * span) * FINEST - center) / BOX_SCALE)
    half = 0.5 * span * FINEST / BOX_SCALE
    sub = lax.broadcasted_iota(jnp.int32, (8, TILE), 0)

    def power_rows(value):
        value = jnp.broadcast_to(value, (8, TILE))
        power = jnp.ones((8, TILE), F32)
        rows = power
        for k in range(1, DEG + 1):
            power = power * value
            rows = jnp.where(sub == k, power, rows)
        return rows

    half_rows = power_rows(half)
    half_wide = jnp.broadcast_to(half, (8, TILE))
    scales = [half_rows]
    for _ in range(DEG):
        scales.append(scales[-1] * half_wide)
    x_rows = power_rows(at_box[0])
    x_tiles = []
    half_power = jnp.ones((8, TILE), F32)
    for k in range(DEG + 1):
        turned = x_rows if k == 0 else pltpu.roll(x_rows, k, 0)
        x_tiles.append(small[k] * turned * half_power)
        half_power = half_power * half_wide
    x_table = jnp.concatenate(x_tiles, axis=1)
    x_high, x_low = split(x_table)
    y_wide = jnp.broadcast_to(at_box[1], (8, TILE))
    z_wide = jnp.broadcast_to(at_box[2], (8, TILE))
    z_coef = []
    z_power = jnp.ones((8, TILE), F32)
    for k in range(DEG + 1):
        z_coef.append(small[k] * z_power)
        z_power = z_power * z_wide

    loads[VAND_IN].wait()
    l_high, l_low = split(local[...].reshape(3 * LEAVES, NODES))
    by_high = dot_nt(vand[...].reshape(2 * ORDERS, NODES), l_high)
    local_moments[...] = by_high[0:ORDERS] + by_high[ORDERS:] + dot_nt(vand[0], l_low)
    downs[2].wait_recv()
    send_chip(1)
    ups[2].wait_recv()
    send_chip(2)
    gather(LEAVES, 2 * LEAVES)
    loads[SPREAD_IN].wait()
    hear(2)
    tell(3)
    for copy in [links[0]] + chips[:3]:
        copy.wait_recv()
    gather(BANDS_AT, 6 * BAND)
    for k in range(4):
        forwards[k].wait_recv()
    send_chip(3)
    gather(3 * LEAVES, LEAVES)
    hear(3)
    loads[SIDES_IN].wait()
    for copy in relays + [chips[3]]:
        copy.wait_recv()
    col = lax.broadcasted_iota(jnp.int32, (LEAVES, 2 * BAND), 1).astype(F32) + float(LAST_AT)
    near_sums = []
    for dim in range(3):
        width = TILE * (3, 6, 7)[dim]
        chosen = [
            jnp.where(col == pos_sq[:, face : face + 1], 1.0, 0.0)
            for face in (2 * dim, 2 * dim + 1)
        ]
        chosen = jnp.concatenate(chosen, axis=1).astype(BF16)
        late = tab[LAST_AT:ROWS, 0:width]
        side = [
            late * jnp.concatenate([sides[2 * dim + k, :, 0:width]] * 4, axis=0)
            for k in range(2)
        ]
        got = dot(chosen, jnp.concatenate(side, axis=0)).astype(BF16)
        near_sums.append(picked[dim, :, 0:width] + got)

    rows = []
    for comp in range(3):
        parts = []
        for dim in range(3):
            for tile in FACE_TILES[dim]:
                at = 6 if tile == 2 else 3 * tile + comp
                value = near_sums[dim][:, TILE * at : TILE * (at + 1)]
                if tile == 2:
                    mine = (lane >= tail * comp) & (lane < tail * (comp + 1))
                    value = jnp.where(mine, value.astype(F32), 0.0).astype(BF16)
                parts.append(value)
        rows.append(jnp.concatenate(parts, axis=1))
    across = dot(jnp.concatenate(rows, axis=0), spread[...])
    for comp in range(3):
        there = across[LEAVES * comp : LEAVES * (comp + 1)]
        near_part = jnp.where(live_rows, -(penalty * out_scale) * visc[...] * there, 0.0)
        across_live[LEAVES * comp : LEAVES * (comp + 1), :] = near_part.astype(BF16)
        force[comp] = local[comp] + near_part
    force_out = pltpu.make_async_copy(force, force_out_ref, out_sem.at[1])
    force_out.start()

    by_near = dot_nt(vand[...].reshape(2 * ORDERS, NODES), across_live[...])
    leaf_moments = local_moments[...] + by_near[0:ORDERS] + by_near[ORDERS:]
    for comp in range(3):
        for jx in range(6):
            columns = []
            for jy in range(6):
                first = jx * 48 + jy * 8
                base = leaf_moments[first : first + 8, TILE * comp : TILE * (comp + 1)] * scales[jy]
                moved = base * z_coef[0]
                for k in range(1, DEG + 1):
                    moved = moved + z_coef[k] * pltpu.roll(base, k, 0)
                columns.append(moved)
            for low in range(1, DEG + 1):
                for at in range(DEG, low - 1, -1):
                    columns[at] = columns[at] + y_wide * columns[at - 1]
            for jy in range(6):
                first = 36 * comp + 6 * jy
                mcat[first : first + 6, TILE * jx : TILE * (jx + 1)] = columns[jy][0:6]
    mcat[108:TILE, :] = jnp.zeros((TILE - 108, 6 * TILE), F32)
    c_high, c_low = split(mcat[...])
    own_box = dot_nt(x_high, c_high) + dot_nt(x_low, c_high) + dot_nt(x_high, c_low)

    shifted = own_box * small[18]
    shift_by = [(center - 0.5) / 0.5 for center in box_center]
    for dim, (axis, stride, base) in enumerate(((0, 1, 0), (1, 6, 6), (1, 1, 12))):
        moved = shifted
        power = 1.0
        for k in range(1, DEG + 1):
            power = power * shift_by[dim]
            moved = moved + small[base + k] * power * pltpu.roll(shifted, stride * k, axis)
        shifted = moved

    part[0] = own_box
    part[1] = shifted
    recv_box[s] = own_box
    box_copies = [
        send(
            part.at[0],
            recv_box.at[s],
            box_send.at[k],
            box_recv.at[k],
            (m, lax.rem(s + 1 + k, SIBS)),
        )
        for k in range(SIBS - 1)
    ]
    at_a = x_at * SIBS + s
    z_at = lax.div(zc_at, CORES)
    from_core = []
    for k in range(CORES):
        copies = []
        for n, (dx, dy) in enumerate(([(0, 0)] if k == 0 else []) + a_steps):
            to = (lax.rem(x_at + dx, X_SIZE) * ZC + zc_at + 1 - core, lax.rem(s + dy, SIBS))
            copies.append(
                send(part.at[1], recv_a.at[k, at_a], a_send.at[k, n], a_recv.at[k, n], to)
            )
        from_core.append(copies)
    b_steps = [CORES * k for k in range(1, Z_SIZE)] + [CORES * k + 1 for k in range(Z_SIZE)]
    b_copies = [
        send(
            sum_b,
            recv_b.at[z_at],
            b_send.at[k],
            b_recv.at[k],
            (x_at * ZC + lax.rem(CORES * z_at + 1 + step, ZC), s),
        )
        for k, step in enumerate(b_steps)
    ]
    to_core_1, to_core_0 = b_copies[: Z_SIZE - 1], b_copies[Z_SIZE - 1 :]

    @pl.when(core == 0)
    def _():
        for copy in from_core[0]:
            copy.start()

    @pl.when(core == 1)
    def _():
        recv_a[1, at_a] = shifted
        for copy in from_core[1]:
            copy.start()

    for copy in box_copies:
        copy.start()

    for copy in box_copies:
        copy.wait_recv()
    box = recv_box[0]
    for k in range(1, SIBS):
        box = box + recv_box[k]
    flat_rows(box, flat.at[0])
    box_out = pltpu.make_async_copy(flat.at[0], box_out_ref, out_sem.at[2])
    box_out.start()

    @pl.when(core == 1)
    def _():
        for copies in from_core:
            for copy in copies:
                copy.wait_recv()
        plane = recv_a[0, 0] + recv_a[1, 0]
        for k in range(1, X_SIZE * SIBS):
            plane = plane + (recv_a[0, k] + recv_a[1, k])
        sum_b[...] = plane
        recv_b[z_at] = plane
        for copy in b_copies:
            copy.start()
        for copy in to_core_1:
            copy.wait_recv()

    @pl.when(core == 0)
    def _():
        for copy in to_core_0:
            copy.wait_recv()

    total = recv_b[0]
    for k in range(1, Z_SIZE):
        total = total + recv_b[k]
    flat_rows(total, flat.at[1])
    root_out = pltpu.make_async_copy(flat.at[1], root_out_ref, out_sem.at[3])
    root_out.start()

    for copy in ups + downs + links + forwards + relays + chips + box_copies:
        copy.wait_send()

    @pl.when(core == 0)
    def _():
        for copy in from_core[0]:
            copy.wait_send()

    @pl.when(core == 1)
    def _():
        for copy in from_core[1] + b_copies:
            copy.wait_send()

    mass_out.wait()
    force_out.wait()
    box_out.wait()
    root_out.wait()


def finish(force, mass, box, root, force_out, mass_out, box_out, root_out, sem):
    pairs = [(force.at[k], force_out.at[k]) for k in range(3)]
    pairs += [(mass, mass_out), (box, box_out), (root, root_out)]
    copies = [pltpu.make_async_copy(a, b, sem.at[k]) for k, (a, b) in enumerate(pairs)]
    for copy in copies:
        copy.start()
    for copy in copies:
        copy.wait()


def on_device(velocity, pressure, viscosity, levels, morton_keys, counts, neighbors):
    diff, pick, spread, sides, vander, small, tail = tables()
    as_bf16 = lambda a: jnp.asarray(a.astype(np.float32)).astype(BF16)
    vander32 = vander.astype(np.float32)
    v_high = vander32.astype(jnp.bfloat16)
    v_low = (vander32 - v_high.astype(np.float32)).astype(jnp.bfloat16)
    vand = np.stack([v_high, v_low])
    dma = pltpu.SemaphoreType.DMA
    any_space = pl.BlockSpec(memory_space=pl.ANY)
    hbm = pl.BlockSpec(memory_space=pltpu.HBM)
    results = (
        jax.ShapeDtypeStruct((3, LEAVES, NODES), F32),
        jax.ShapeDtypeStruct((LEAVES, NODES), F32),
        jax.ShapeDtypeStruct((3, 1, MOMENTS), F32),
        jax.ShapeDtypeStruct((3, 1, MOMENTS), F32),
    )
    raw = pl.pallas_call(
        functools.partial(kernel, tail),
        out_shape=tuple(pltpu.VMEM(r.shape, r.dtype) for r in results),
        in_specs=[hbm] * 13,
        out_specs=(any_space,) * 4,
        scratch_shapes=[
            pltpu.VMEM((4, LEAVES, NODES), BF16),
            pltpu.VMEM((NODES, 2 * TILE), BF16),
            pltpu.SMEM((MORTONS * SIBS,), jnp.int32),
            pltpu.VMEM((6, LEAVES), jnp.int32),
            pltpu.VMEM((3, NODES, NODES), BF16),
            pltpu.VMEM((LEAVES, NODES), F32),
            pltpu.VMEM((MASK_AT + 21, 8, TILE), F32),
            pltpu.VMEM((1, LEAVES), jnp.int32),
            pltpu.VMEM((1, LEAVES), jnp.int32),
            pltpu.VMEM((6 * TILE, NODES), BF16),
            pltpu.VMEM((6, 16, LANES), BF16),
            pltpu.VMEM((2, ORDERS, NODES), BF16),
            pltpu.VMEM((ROWS, LANES), BF16),
            pltpu.VMEM((BAND, LANES), BF16),
            pltpu.VMEM((4, BAND, LANES), BF16),
            pltpu.VMEM((3, 4 * LEAVES, NODES), F32),
            pltpu.VMEM((3, LEAVES, NODES), F32),
            pltpu.VMEM((3, LEAVES, LANES), BF16),
            pltpu.VMEM((3, LEAVES, NODES), F32),
            pltpu.VMEM((LEAVES, NODES), F32),
            pltpu.VMEM((LEAVES, LEAVES), F32),
            pltpu.VMEM((ORDERS, 3 * LEAVES), F32),
            pltpu.VMEM((3 * LEAVES, NODES), BF16),
            pltpu.VMEM((TILE, 6 * TILE), F32),
            pltpu.VMEM((2, 8, TILE), F32),
            pltpu.VMEM((SIBS, 8, TILE), F32),
            pltpu.VMEM((CORES, X_SIZE * SIBS, 8, TILE), F32),
            pltpu.VMEM((Z_SIZE, 8, TILE), F32),
            pltpu.VMEM((8, TILE), F32),
            pltpu.VMEM((2, 3, 1, MOMENTS), F32),
            dma((15,)),
            dma((4,)),
            dma((2, 3)),
            dma((2, 3)),
            dma((4,)),
            dma((4,)),
            dma((3,)),
            dma((3,)),
            dma((2,)),
            dma((2,)),
            dma((4,)),
            dma((4,)),
            dma((3,)),
            dma((3,)),
            dma((CORES, 16)),
            dma((CORES, 16)),
            dma((15,)),
            dma((15,)),
            pltpu.SemaphoreType.REGULAR((ROUNDS,)),
        ],
        compiler_params=pltpu.CompilerParams(
            collective_id=0, has_side_effects=True, vmem_limit_bytes=60 * 2**20
        ),
    )(
        velocity.transpose(1, 0, 2),
        as_bf16(pick),
        counts,
        neighbors.T,
        pressure,
        as_bf16(diff),
        viscosity,
        jnp.asarray(small.astype(np.float32)),
        levels.reshape(1, LEAVES),
        morton_keys.reshape(1, LEAVES),
        as_bf16(spread),
        as_bf16(sides),
        jnp.asarray(vand),
    )
    force, mass, box, root = pl.pallas_call(
        finish,
        out_shape=results,
        in_specs=[any_space] * 4,
        out_specs=(any_space,) * 4,
        scratch_shapes=[dma((6,))],
    )(*[pltpu.with_memory_space_constraint(r, pltpu.VMEM) for r in raw])
    return (
        force.transpose(1, 0, 2),
        mass,
        box.transpose(1, 0, 2),
        root.transpose(1, 0, 2),
    )


def solution(mesh):
    in_specs = (
        P(("morton", "sib"), None, None),
        P(("morton", "sib"), None),
        P(("morton", "sib"), None),
        P(("morton", "sib")),
        P(("morton", "sib")),
        P(),
        P(("morton", "sib"), None),
    )
    out_specs = (
        P(("morton", "sib"), None, None),
        P(("morton", "sib"), None),
        P("morton", None, None),
        P("morton", None, None),
    )
    return jax.shard_map(
        on_device, mesh=mesh, in_specs=in_specs, out_specs=out_specs, check_vma=False
    )
```

```python
import functools
import math

import jax
import jax.numpy as jnp
import numpy as np
from jax import lax
from jax.experimental import pallas as pl
from jax.experimental.pallas import tpu as pltpu
from jax.sharding import PartitionSpec as P

DEG = 5
LMAX = 7
MOMENTS = 216
LEAVES = 128
NODES = 512
LANES = 896
BAND = 32
TILE = 128
MESH = pl.DeviceIdType.MESH
F32 = jnp.float32
BF16 = jnp.bfloat16

penalty = 256.0
out_scale = 1.0 / 1024.0
mass_scale = 1.0 / 32.0

X_SIZE, Z_SIZE, CORES, SIBS = 4, 8, 2, 4
ZC = Z_SIZE * CORES
MORTONS = X_SIZE * ZC


def cheb():
    points = -np.cos(np.pi * np.arange(8) / 7.0)
    weights = np.array([(-1.0) ** k for k in range(8)])
    weights[0] *= 0.5
    weights[7] *= 0.5
    derivative = np.zeros((8, 8))
    for row in range(8):
        for col in range(8):
            if row != col:
                derivative[row, col] = weights[col] / weights[row] / (points[row] - points[col])
        derivative[row, row] = -np.sum(derivative[row])
    return points, derivative


def node_of(coords):
    return 64 * coords[0] + 8 * coords[1] + coords[2]


def coords_of(node):
    return [node // 64, node // 8 % 8, node % 8]


def surface_lists():
    x_nodes = [node_of([7 * side, b, c]) for side in range(2) for b in range(8) for c in range(8)]
    inner = [n for n in range(NODES) if coords_of(n)[0] not in (0, 7)]
    on_y = [n for n in inner if coords_of(n)[1] in (0, 7)]
    only_z = [n for n in inner if n not in on_y and coords_of(n)[2] in (0, 7)]
    return x_nodes, on_y + only_z


FACE_TILES = ((0,), (0, 1), (0, 1, 2))
MULT_AT, MASK_AT = 6, 10


def tables():
    points, derivative = cheb()
    eye = np.eye(8)
    directional = [
        np.kron(np.kron(derivative, eye), eye),
        np.kron(np.kron(eye, derivative), eye),
        np.kron(np.kron(eye, eye), derivative),
    ]
    diff = np.stack([m.T for m in directional])
    x_nodes, rest = surface_lists()
    tail = len(rest) - TILE
    pick = np.zeros((NODES, 2 * TILE))
    for k, node in enumerate(rest):
        pick[node, k] = 1.0
    tiles = [list(x_nodes), list(rest[:TILE]), [-1] * TILE]
    for comp in range(3):
        for k in range(tail):
            tiles[2][tail * comp + k] = rest[TILE + k]
    spread = np.zeros((6 * TILE, NODES))
    small = np.zeros((MASK_AT + 21, 8, TILE))
    sides = np.zeros((6, 16, LANES))
    slot = 0
    for dim in range(3):
        for tile in FACE_TILES[dim]:
            for lane, node in enumerate(tiles[tile]):
                if node < 0:
                    continue
                coords = coords_of(node)
                if coords[dim] in (0, 7):
                    other = list(coords)
                    other[dim] = 7 - coords[dim]
                    spread[slot * TILE + lane, node_of(other)] = 1.0
                    for at in (6,) if tile == 2 else range(3 * tile, 3 * tile + 3):
                        sides[2 * dim + (coords[dim] == 0), :, TILE * at + lane] = 1.0
                        if coords[dim] == 7:
                            small[MASK_AT + 7 * dim + at, :, lane] = 1.0
            slot += 1
    for node in range(NODES):
        count = sum(1 for c in coords_of(node) if c in (0, 7))
        small[MULT_AT + node // TILE, :, node % TILE] = count
    vander = np.zeros((288, NODES))
    for jx in range(6):
        for jy in range(6):
            for jz in range(6):
                for node in range(NODES):
                    a, b, c = coords_of(node)
                    vander[jx * 48 + jy * 8 + jz, node] = (
                        points[a] ** jx * points[b] ** jy * points[c] ** jz / 512.0
                    )
    for k in range(6):
        for a in range(6):
            if a >= k:
                small[k, a, :] = math.comb(a, k)
    shift = np.zeros((3, TILE, TILE))
    for row in range(108):
        for col in range(108):
            jy, jz, ay, az = row // 6 % 6, row % 6, col // 6 % 6, col % 6
            if row // 36 == col // 36 and ay >= jy and az >= jz:
                shift[0, row, col] = (
                    math.comb(ay, jy) * math.comb(az, jz) * BOX_IN_ROOT ** (jy + jz)
                )
                shift[1, row, col] = ay - jy
                shift[2, row, col] = az - jz
    return diff, pick, spread, sides, shift, vander, small, tail


BOX_CELLS = 2 ** ((3 * LMAX - 6) // 3)
FINEST = 1.0 / 2**LMAX
BOX_SIDE = BOX_CELLS * FINEST
BOX_SCALE = 0.5 * BOX_SIDE
BOX_IN_ROOT = BOX_SCALE / 0.5

(
    VEL_IN,
    PICK_IN,
    COUNTS_IN,
    NBR_IN,
    PRESS_IN,
    DIFF_IN,
    VISC_IN,
    SMALL_IN,
    LEVELS_IN,
    KEYS_IN,
    SPREAD_IN,
    SIDES_IN,
    SHIFT_IN,
    VAND_IN,
) = range(14)
QUARTER = LEAVES // 4
HALF_BAND = BAND // 2
ROUNDS = 4
ORDERS = 288
BANDS_AT, LAST_AT, ROWS = 4 * LEAVES, 4 * LEAVES + 6 * BAND, 4 * LEAVES + 8 * BAND


def dot(a, b):
    return jnp.dot(a, b, preferred_element_type=F32)


def dot_nt(a, b):
    return lax.dot_general(a, b, (((1,), (1,)), ((), ())), preferred_element_type=F32)


def split(value):
    high = value.astype(BF16)
    return high, (value - high.astype(F32)).astype(BF16)


def flat_rows(packed, out_ref):
    lane = lax.broadcasted_iota(jnp.int32, (8, TILE), 1)
    sub = lax.broadcasted_iota(jnp.int32, (8, TILE), 0)
    first_tile = (sub < 3) | ((sub == 3) & (lane >= 108))
    valid = jnp.bitwise_and(lane - 36 * sub, TILE - 1) < 36
    turned = {0: packed}
    for by in range(-2, DEG + 1):
        if by:
            turned[by] = pltpu.roll(packed, 36 * by % TILE, 1)
    for comp in range(3):
        rows = turned[-comp]
        for ax in range(1, DEG + 1):
            rows = jnp.where(sub == ax, turned[ax - comp], rows)
        rows = jnp.where(valid & (sub < 6), rows, 0.0)
        near = jnp.sum(jnp.where(first_tile, rows, 0.0), axis=0, keepdims=True)
        far = jnp.sum(jnp.where(first_tile, 0.0, rows), axis=0, keepdims=True)
        out_ref[comp, :, 0:TILE] = near
        out_ref[comp, :, TILE:MOMENTS] = far[:, : MOMENTS - TILE]


def kernel(
    tail,
    vel_hbm,
    pick_hbm,
    counts_hbm,
    nbr_hbm,
    press_hbm,
    diff_hbm,
    visc_hbm,
    small_hbm,
    levels_hbm,
    keys_hbm,
    spread_hbm,
    sides_hbm,
    shift_hbm,
    vand_hbm,
    force_out_ref,
    mass_out_ref,
    box_out_ref,
    root_out_ref,
    field,
    pick,
    counts,
    nbr_in,
    diff,
    visc,
    small,
    levels,
    keys,
    spread,
    sides,
    shift_tab,
    vand,
    tab,
    link_band,
    chip_band,
    grads,
    local,
    picked,
    force,
    mass,
    pos_sq,
    force_high,
    force_low,
    x_tables,
    root_yz,
    mcat,
    part,
    recv_box,
    recv_a,
    recv_b,
    sum_b,
    tall,
    flat,
    in_sem,
    out_sem,
    ring_send,
    ring_recv,
    fwd_send,
    fwd_recv,
    link_send,
    link_recv,
    relay_send,
    relay_recv,
    chip_send,
    chip_recv,
    box_send,
    box_recv,
    a_send,
    a_recv,
    b_send,
    b_recv,
    known,
):
    m = lax.axis_index("morton")
    s = lax.axis_index("sib")
    x_at = lax.div(m, ZC)
    zc_at = lax.rem(m, ZC)
    core = lax.rem(m, CORES)
    above = lax.rem(s + 1, SIBS)
    below = lax.rem(s + SIBS - 1, SIBS)
    m_chip = m + 1 - 2 * core
    m_link = lax.rem(m + MORTONS - 1 + 2 * core, MORTONS)

    def group_a(dx, dy):
        return (lax.rem(x_at + dx, X_SIZE) * ZC + zc_at, lax.rem(s + dy, SIBS))

    def group_b(dz):
        return (x_at * ZC + lax.rem(zc_at + dz, ZC), s)

    a_steps = [(dx, dy) for dx in range(X_SIZE) for dy in range(SIBS) if dx or dy]

    loads = [
        pltpu.make_async_copy(
            vel_hbm.at[0, pl.ds(0, 64)], field.at[0, pl.ds(0, 64)], in_sem.at[VEL_IN]
        ),
        pltpu.make_async_copy(pick_hbm, pick, in_sem.at[PICK_IN]),
        pltpu.make_async_copy(counts_hbm, counts, in_sem.at[COUNTS_IN]),
        pltpu.make_async_copy(nbr_hbm, nbr_in, in_sem.at[NBR_IN]),
        pltpu.make_async_copy(press_hbm, field.at[3], in_sem.at[PRESS_IN]),
        pltpu.make_async_copy(diff_hbm, diff, in_sem.at[DIFF_IN]),
        pltpu.make_async_copy(visc_hbm, visc, in_sem.at[VISC_IN]),
        pltpu.make_async_copy(small_hbm, small, in_sem.at[SMALL_IN]),
        pltpu.make_async_copy(levels_hbm, levels, in_sem.at[LEVELS_IN]),
        pltpu.make_async_copy(keys_hbm, keys, in_sem.at[KEYS_IN]),
        pltpu.make_async_copy(spread_hbm, spread, in_sem.at[SPREAD_IN]),
        pltpu.make_async_copy(sides_hbm, sides, in_sem.at[SIDES_IN]),
        pltpu.make_async_copy(shift_hbm, shift_tab, in_sem.at[SHIFT_IN]),
        pltpu.make_async_copy(vand_hbm, vand, in_sem.at[VAND_IN]),
    ]
    more_velocity = [
        pltpu.make_async_copy(
            vel_hbm.at[k // 2, pl.ds(k % 2 * 64, 64)],
            field.at[k // 2, pl.ds(k % 2 * 64, 64)],
            in_sem.at[VAND_IN + k],
        )
        for k in range(1, 6)
    ]
    for copy in [loads[VEL_IN], loads[PICK_IN]] + more_velocity:
        copy.start()
    for which in (COUNTS_IN, NBR_IN):
        loads[which].start()

    near_groups = [group_a(1, 0), group_a(X_SIZE - 1, 0), group_b(1), group_b(ZC - 1)]
    near = [(m, above), (m, below), (m_link, s)] + near_groups
    barrier = pltpu.get_barrier_semaphore()
    for device in near:
        pl.semaphore_signal(barrier, inc=1, device_id=device, device_id_type=MESH)

    loads[VEL_IN].wait()
    for copy in more_velocity:
        copy.wait()
    loads[PICK_IN].wait()
    for which in range(PRESS_IN, len(loads)):
        loads[which].start()
    lane = lax.broadcasted_iota(jnp.int32, (LEAVES, TILE), 1)
    rest = dot(field[0:3].reshape(3 * LEAVES, NODES), pick[...])
    shared = jnp.zeros((LEAVES, TILE), F32)
    for comp in range(3):
        first = field[comp, :, 0:TILE].astype(F32)
        last = field[comp, :, NODES - TILE : NODES].astype(F32)
        tab[0:LEAVES, TILE * comp : TILE * (comp + 1)] = jnp.where(lane < 64, first, last).astype(BF16)
        rows = rest[LEAVES * comp : LEAVES * (comp + 1)]
        tab[0:LEAVES, TILE * (3 + comp) : TILE * (4 + comp)] = rows[:, 0:TILE].astype(BF16)
        piece = rows[:, TILE : 2 * TILE]
        if comp:
            piece = pltpu.roll(piece, tail * comp, 1)
        shared = shared + piece
    tab[0:LEAVES, TILE * 6 : TILE * 7] = shared.astype(BF16)

    pl.semaphore_wait(barrier, len(near))

    def send(src, dst, send_sem, recv_sem, device):
        return pltpu.make_async_remote_copy(
            src_ref=src,
            dst_ref=dst,
            send_sem=send_sem,
            recv_sem=recv_sem,
            device_id=device,
            device_id_type=MESH,
        )

    def quarters(block, q, count=1):
        return tab.at[pl.ds(LEAVES * block + QUARTER * q, QUARTER * count)]

    def link_rows(b, first=0, rows=BAND):
        return tab.at[pl.ds((LAST_AT if b == 3 else BANDS_AT + BAND * b) + first, rows)]

    def chip_rows(b):
        return tab.at[pl.ds(LAST_AT + BAND if b == 3 else BANDS_AT + BAND * (3 + b), BAND)]

    ups, downs = [], []
    for k, (q_up, q_down, count) in enumerate(((0, 2, 1), (1, 3, 1), (2, 0, 2))):
        ups.append(
            send(
                quarters(0, q_up, count),
                quarters(2, q_up, count),
                ring_send.at[0, k],
                ring_recv.at[0, k],
                (m, above),
            )
        )
        downs.append(
            send(
                quarters(0, q_down, count),
                quarters(1, q_down, count),
                ring_send.at[1, k],
                ring_recv.at[1, k],
                (m, below),
            )
        )
    forwards = [
        send(quarters(2, 0), quarters(3, 0), fwd_send.at[0], fwd_recv.at[0], (m, above)),
        send(quarters(1, 2), quarters(3, 2), fwd_send.at[1], fwd_recv.at[1], (m, below)),
        send(quarters(2, 1), quarters(3, 1), fwd_send.at[2], fwd_recv.at[2], (m, above)),
        send(quarters(1, 3), quarters(3, 3), fwd_send.at[3], fwd_recv.at[3], (m, below)),
    ]
    links = [
        send(link_band, link_rows(0), link_send.at[0], link_recv.at[0], (m_link, s)),
        send(link_band, link_rows(2), link_send.at[1], link_recv.at[1], (m_link, above)),
        send(link_band, link_rows(1), link_send.at[2], link_recv.at[2], (m_link, below)),
    ]
    relays = [
        send(
            link_rows(2, 0, HALF_BAND),
            link_rows(3, 0, HALF_BAND),
            relay_send.at[0],
            relay_recv.at[0],
            (m, above),
        ),
        send(
            link_rows(1, HALF_BAND, HALF_BAND),
            link_rows(3, HALF_BAND, HALF_BAND),
            relay_send.at[1],
            relay_recv.at[1],
            (m, below),
        ),
    ]
    chips = [
        send(chip_band.at[b], chip_rows(b), chip_send.at[b], chip_recv.at[b], (m_chip, s))
        for b in range(4)
    ]
    turn = [0, 1, 3, 2]
    band_row = lax.broadcasted_iota(jnp.int32, (BAND, LEAVES), 0)
    band_col = lax.broadcasted_iota(jnp.int32, (BAND, LEAVES), 1)

    def band(b, last):
        live = counts[m * SIBS + lax.rem(s + turn[b], SIBS)]
        chosen = jnp.where(band_col == band_row + last * (live - BAND), 1.0, 0.0).astype(BF16)
        return dot(chosen, tab[LEAVES * b : LEAVES * (b + 1)]).astype(BF16)

    def send_chip(b):
        chip_band[b] = band(b, 1 - core)
        chips[b].start()

    round_peers = []
    for k in range(ROUNDS):
        peers = [group_a(1, 0), group_a(X_SIZE - 1, 0), (m, above), (m, below)]
        if k < 3:
            peers += [group_b(2**k), group_b(ZC - 2**k)]
        round_peers.append(peers)

    def tell(k):
        for device in round_peers[k]:
            pl.semaphore_signal(known.at[k], inc=1, device_id=device, device_id_type=MESH)

    def hear(k):
        pl.semaphore_wait(known.at[k], len(round_peers[k]))

    ups[0].start()
    downs[0].start()
    ups[1].start()
    downs[1].start()
    tell(0)
    loads[COUNTS_IN].wait()
    link_band[...] = band(0, core)
    links[0].start()
    loads[NBR_IN].wait()
    nbr = nbr_in[...]
    owner_sib = jnp.bitwise_and(jnp.right_shift(nbr, 7), 3)
    slot = jnp.bitwise_and(nbr, LEAVES - 1)
    step = jnp.right_shift(nbr, 9) - m
    offset = jnp.bitwise_and(owner_sib - s + SIBS, 3)
    block = jnp.where(offset == 2, 3, jnp.where(offset == 3, 2, offset))
    prior = lax.rem(m + MORTONS - 1, MORTONS) * SIBS
    prior_live = jnp.zeros_like(nbr)
    for k in range(SIBS):
        prior_live = jnp.where(owner_sib == k, counts[prior + k], prior_live)
    apart = jnp.where(block == 3, BAND, 3 * BAND)
    halo_row = jnp.where(block == 3, LAST_AT, BANDS_AT + block * BAND) + slot
    row = jnp.where(
        step == 0,
        block * LEAVES + slot,
        jnp.where(
            step == 1,
            halo_row + (1 - core) * apart,
            halo_row + core * apart - (prior_live - BAND),
        ),
    )
    row = jnp.where(nbr < 0, -1, row).astype(F32)
    pos_sq[...] = jnp.zeros_like(pos_sq)
    pos_sq[0:6, :] = row
    pos_sq[...] = pos_sq[...].T

    def gather(first, rows, fresh=False):
        col = lax.broadcasted_iota(jnp.int32, (LEAVES, rows), 1).astype(F32) + float(first)
        for dim in range(3):
            pair = []
            for face in (2 * dim, 2 * dim + 1):
                at = pos_sq[:, face : face + 1]
                pair.append(jnp.where(col == at, 1.0, 0.0))
            chosen = jnp.concatenate(pair, axis=0).astype(BF16)
            width = TILE * (3, 6, 7)[dim]
            got = dot(chosen, tab[first : first + rows, 0:width])
            for tile in range(width // TILE):
                lanes = slice(TILE * tile, TILE * (tile + 1))
                mask = small[MASK_AT + 7 * dim + tile, 0:1, :] > 0.5
                one = jnp.where(mask, got[0:LEAVES, lanes], got[LEAVES:, lanes]).astype(BF16)
                if fresh:
                    picked[dim, :, lanes] = one
                else:
                    picked[dim, :, lanes] += one

    send_chip(0)
    loads[SMALL_IN].wait()
    gather(0, LEAVES, True)
    hear(0)
    links[1].start()
    links[2].start()
    tell(1)

    loads[PRESS_IN].wait()
    loads[DIFF_IN].wait()
    stacked = field[...].reshape(4 * LEAVES, NODES)
    for dim in range(3):
        grads[dim] = dot(stacked, diff[dim])
        if dim == 1:
            ups[2].start()
            downs[2].start()

    own_live = counts[m * SIBS + s]
    leaf_row = lax.broadcasted_iota(jnp.int32, (LEAVES, NODES), 0)
    live_rows = leaf_row < own_live

    def grad(comp, dim):
        return grads[dim, LEAVES * comp : LEAVES * (comp + 1), :]

    mass[...] = jnp.where(
        live_rows, -(grad(0, 0) + grad(1, 1) + grad(2, 2)) * mass_scale, 0.0
    )
    mass_out = pltpu.make_async_copy(mass, mass_out_ref, out_sem.at[0])
    mass_out.start()

    loads[VISC_IN].wait()
    stress = {}
    for i in range(3):
        for j in range(i, 3):
            stress[i, j] = (visc[...] * (grad(i, j) + grad(j, i))).astype(BF16)
    total = None
    for j in range(3):
        rows = jnp.concatenate([stress[min(i, j), max(i, j)] for i in range(3)], axis=0)
        term = dot(rows, diff[j])
        total = term if total is None else total + term
    mult = jnp.concatenate([small[MULT_AT + t, 0:1, :] for t in range(4)], axis=1)
    for comp in range(3):
        jump = field[comp].astype(F32) * mult
        value = (
            penalty * visc[...] * jump
            - total[LEAVES * comp : LEAVES * (comp + 1)]
            + grad(3, comp)
        ) * out_scale
        local[comp] = jnp.where(live_rows, value, 0.0)
    ups[0].wait_recv()
    forwards[0].start()
    downs[0].wait_recv()
    forwards[1].start()
    ups[1].wait_recv()
    forwards[2].start()
    downs[1].wait_recv()
    forwards[3].start()
    links[1].wait_recv()
    relays[0].start()
    links[2].wait_recv()
    relays[1].start()
    hear(1)
    tell(2)

    loads[LEVELS_IN].wait()
    loads[KEYS_IN].wait()
    level = levels[...]
    shift_bits = 3 * (LMAX - level)
    anchor = jnp.left_shift(jnp.right_shift(keys[...], shift_bits), shift_bits)
    span = jnp.left_shift(jnp.ones_like(level), LMAX - level).astype(F32)
    at_box = []
    box_center = []
    for dim, bit0 in enumerate((2, 1, 0)):
        cell = jnp.zeros_like(anchor)
        corner = 0
        for bit in range(LMAX):
            cell = cell + jnp.left_shift(
                jnp.bitwise_and(jnp.right_shift(anchor, 3 * bit + bit0), 1), bit
            )
            up_bit = 3 * bit + bit0 - (3 * LMAX - 6)
            if up_bit >= 0:
                corner = corner + lax.rem(lax.div(m, 2**up_bit), 2) * 2**bit
        center = corner.astype(F32) * FINEST + 0.5 * BOX_SIDE
        box_center.append(center)
        at_box.append(((cell.astype(F32) + 0.5 * span) * FINEST - center) / BOX_SCALE)
    half = 0.5 * span * FINEST / BOX_SCALE
    sub = lax.broadcasted_iota(jnp.int32, (8, TILE), 0)

    def power_rows(value):
        value = jnp.broadcast_to(value, (8, TILE))
        power = jnp.ones((8, TILE), F32)
        rows = power
        for k in range(1, DEG + 1):
            power = power * value
            rows = jnp.where(sub == k, power, rows)
        return rows

    loads[SHIFT_IN].wait()
    half_rows = power_rows(half)
    half_wide = jnp.broadcast_to(half, (8, TILE))
    scales = [half_rows]
    for _ in range(DEG):
        scales.append(scales[-1] * half_wide)

    def x_table(at, size):
        wide = jnp.broadcast_to(size, (8, TILE))
        rows = power_rows(at)
        size_power = jnp.ones((8, TILE), F32)
        tiles = []
        for k in range(DEG + 1):
            turned = rows if k == 0 else pltpu.roll(rows, k, 0)
            tiles.append(small[k] * turned * size_power)
            size_power = size_power * wide
        return split(jnp.concatenate(tiles, axis=1))

    at_root = (at_box[0] * BOX_SCALE + box_center[0] - 0.5) / 0.5
    box_high, box_low = x_table(at_box[0], half)
    root_high, root_low = x_table(at_root, half * BOX_IN_ROOT)
    x_tables[...] = jnp.concatenate([box_high, root_high, box_low, root_low], axis=0)
    moves = shift_tab[0]
    for dim, exponents in ((1, shift_tab[1]), (2, shift_tab[2])):
        by = (box_center[dim] - 0.5) / 0.5
        power = by
        factor = jnp.ones((TILE, TILE), F32)
        for k in range(1, DEG + 1):
            factor = jnp.where(exponents == float(k), power, factor)
            power = power * by
        moves = moves * factor
    move_high, move_low = split(moves)
    root_yz[0] = move_high
    root_yz[1] = move_low
    y_wide = jnp.broadcast_to(at_box[1], (8, TILE))
    z_wide = jnp.broadcast_to(at_box[2], (8, TILE))
    z_coef = []
    z_power = jnp.ones((8, TILE), F32)
    for k in range(DEG + 1):
        z_coef.append(small[k] * z_power)
        z_power = z_power * z_wide

    downs[2].wait_recv()
    send_chip(1)
    ups[2].wait_recv()
    send_chip(2)
    gather(LEAVES, 2 * LEAVES)
    loads[SPREAD_IN].wait()
    hear(2)
    tell(3)
    for copy in [links[0]] + chips[:3]:
        copy.wait_recv()
    gather(BANDS_AT, 6 * BAND)
    for k in range(4):
        forwards[k].wait_recv()
    send_chip(3)
    gather(3 * LEAVES, LEAVES)
    hear(3)
    loads[SIDES_IN].wait()
    loads[VAND_IN].wait()
    for copy in relays + [chips[3]]:
        copy.wait_recv()
    col = lax.broadcasted_iota(jnp.int32, (LEAVES, 2 * BAND), 1).astype(F32) + float(LAST_AT)
    near_sums = []
    for dim in range(3):
        width = TILE * (3, 6, 7)[dim]
        chosen = [
            jnp.where(col == pos_sq[:, face : face + 1], 1.0, 0.0)
            for face in (2 * dim, 2 * dim + 1)
        ]
        chosen = jnp.concatenate(chosen, axis=1).astype(BF16)
        late = tab[LAST_AT:ROWS, 0:width]
        side = [
            late * jnp.concatenate([sides[2 * dim + k, :, 0:width]] * 4, axis=0)
            for k in range(2)
        ]
        got = dot(chosen, jnp.concatenate(side, axis=0)).astype(BF16)
        near_sums.append(picked[dim, :, 0:width] + got)

    rows = []
    for comp in range(3):
        parts = []
        for dim in range(3):
            for tile in FACE_TILES[dim]:
                at = 6 if tile == 2 else 3 * tile + comp
                value = near_sums[dim][:, TILE * at : TILE * (at + 1)]
                if tile == 2:
                    mine = (lane >= tail * comp) & (lane < tail * (comp + 1))
                    value = jnp.where(mine, value.astype(F32), 0.0).astype(BF16)
                parts.append(value)
        rows.append(jnp.concatenate(parts, axis=1))
    across = dot(jnp.concatenate(rows, axis=0), spread[...])
    for comp in range(3):
        there = across[LEAVES * comp : LEAVES * (comp + 1)]
        value = local[comp] - (penalty * out_scale) * visc[...] * there
        value = jnp.where(live_rows, value, 0.0)
        force[comp] = value
        high, low = split(value)
        force_high[LEAVES * comp : LEAVES * (comp + 1), :] = high
        force_low[LEAVES * comp : LEAVES * (comp + 1), :] = low
    force_out = pltpu.make_async_copy(force, force_out_ref, out_sem.at[1])
    force_out.start()

    by_force = dot_nt(vand[...].reshape(2 * ORDERS, NODES), force_high[...])
    leaf_moments = by_force[0:ORDERS] + by_force[ORDERS:] + dot_nt(vand[0], force_low[...])
    for comp in range(3):
        for jx in range(6):
            columns = []
            for jy in range(6):
                first = jx * 48 + jy * 8
                base = leaf_moments[first : first + 8, TILE * comp : TILE * (comp + 1)] * scales[jy]
                moved = base * z_coef[0]
                for k in range(1, DEG + 1):
                    moved = moved + z_coef[k] * pltpu.roll(base, k, 0)
                columns.append(moved)
            for low in range(1, DEG + 1):
                for at in range(DEG, low - 1, -1):
                    columns[at] = columns[at] + y_wide * columns[at - 1]
            for jy in range(6):
                first = 36 * comp + 6 * jy
                mcat[first : first + 6, TILE * jx : TILE * (jx + 1)] = columns[jy][0:6]
    mcat[108:TILE, :] = jnp.zeros((TILE - 108, 6 * TILE), F32)
    c_high, c_low = split(mcat[...])
    by_parts = dot_nt(x_tables[...], c_high)
    both = by_parts[0:16] + by_parts[16:32] + dot_nt(x_tables[0:16], c_low)
    own_box = both[0:6]

    r_high, r_low = split(both[8:16])
    shifted = (
        dot(r_high, root_yz[0]) + dot(r_low, root_yz[0]) + dot(r_high, root_yz[1])
    )[0:6]

    part[0] = own_box
    part[1] = shifted
    recv_box[s] = own_box
    box_copies = [
        send(
            part.at[0],
            recv_box.at[s],
            box_send.at[k],
            box_recv.at[k],
            (m, lax.rem(s + 1 + k, SIBS)),
        )
        for k in range(SIBS - 1)
    ]
    at_a = x_at * SIBS + s
    z_at = lax.div(zc_at, CORES)
    from_core = []
    for k in range(CORES):
        copies = []
        for n, (dx, dy) in enumerate(([(0, 0)] if k == 0 else []) + a_steps):
            to = (lax.rem(x_at + dx, X_SIZE) * ZC + zc_at + 1 - core, lax.rem(s + dy, SIBS))
            copies.append(
                send(part.at[1], recv_a.at[k, at_a], a_send.at[k, n], a_recv.at[k, n], to)
            )
        from_core.append(copies)
    b_steps = [CORES * k for k in range(1, Z_SIZE)] + [CORES * k + 1 for k in range(Z_SIZE)]
    b_copies = [
        send(
            sum_b,
            recv_b.at[z_at],
            b_send.at[k],
            b_recv.at[k],
            (x_at * ZC + lax.rem(CORES * z_at + 1 + step, ZC), s),
        )
        for k, step in enumerate(b_steps)
    ]
    to_core_1, to_core_0 = b_copies[: Z_SIZE - 1], b_copies[Z_SIZE - 1 :]

    @pl.when(core == 0)
    def _():
        for copy in from_core[0]:
            copy.start()

    @pl.when(core == 1)
    def _():
        recv_a[1, at_a] = shifted
        for copy in from_core[1]:
            copy.start()

    for copy in box_copies:
        copy.start()

    for copy in box_copies:
        copy.wait_recv()
    box = recv_box[0]
    for k in range(1, SIBS):
        box = box + recv_box[k]
    tall[...] = jnp.zeros_like(tall)
    tall[0:6, :] = box
    flat_rows(tall[...], flat.at[0])
    box_out = pltpu.make_async_copy(flat.at[0], box_out_ref, out_sem.at[2])
    box_out.start()

    @pl.when(core == 1)
    def _():
        for copies in from_core:
            for copy in copies:
                copy.wait_recv()
        plane = recv_a[0, 0] + recv_a[1, 0]
        for k in range(1, X_SIZE * SIBS):
            plane = plane + (recv_a[0, k] + recv_a[1, k])
        sum_b[...] = plane
        recv_b[z_at] = plane
        for copy in b_copies:
            copy.start()
        for copy in to_core_1:
            copy.wait_recv()

    @pl.when(core == 0)
    def _():
        for copy in to_core_0:
            copy.wait_recv()

    total = recv_b[0]
    for k in range(1, Z_SIZE):
        total = total + recv_b[k]
    tall[0:6, :] = total
    flat_rows(tall[...], flat.at[1])
    root_out = pltpu.make_async_copy(flat.at[1], root_out_ref, out_sem.at[3])
    root_out.start()

    for copy in ups + downs + links + forwards + relays + chips + box_copies:
        copy.wait_send()

    @pl.when(core == 0)
    def _():
        for copy in from_core[0]:
            copy.wait_send()

    @pl.when(core == 1)
    def _():
        for copy in from_core[1] + b_copies:
            copy.wait_send()

    mass_out.wait()
    force_out.wait()
    box_out.wait()
    root_out.wait()


def finish(force, mass, box, root, force_out, mass_out, box_out, root_out, sem):
    pairs = [(force.at[k], force_out.at[k]) for k in range(3)]
    pairs += [(mass, mass_out), (box, box_out), (root, root_out)]
    copies = [pltpu.make_async_copy(a, b, sem.at[k]) for k, (a, b) in enumerate(pairs)]
    for copy in copies:
        copy.start()
    for copy in copies:
        copy.wait()


def on_device(velocity, pressure, viscosity, levels, morton_keys, counts, neighbors):
    diff, pick, spread, sides, shift, vander, small, tail = tables()
    as_bf16 = lambda a: jnp.asarray(a.astype(np.float32)).astype(BF16)
    vander32 = vander.astype(np.float32)
    v_high = vander32.astype(jnp.bfloat16)
    v_low = (vander32 - v_high.astype(np.float32)).astype(jnp.bfloat16)
    vand = np.stack([v_high, v_low])
    dma = pltpu.SemaphoreType.DMA
    any_space = pl.BlockSpec(memory_space=pl.ANY)
    hbm = pl.BlockSpec(memory_space=pltpu.HBM)
    results = (
        jax.ShapeDtypeStruct((3, LEAVES, NODES), F32),
        jax.ShapeDtypeStruct((LEAVES, NODES), F32),
        jax.ShapeDtypeStruct((3, 1, MOMENTS), F32),
        jax.ShapeDtypeStruct((3, 1, MOMENTS), F32),
    )
    raw = pl.pallas_call(
        functools.partial(kernel, tail),
        out_shape=tuple(pltpu.VMEM(r.shape, r.dtype) for r in results),
        in_specs=[hbm] * 14,
        out_specs=(any_space,) * 4,
        scratch_shapes=[
            pltpu.VMEM((4, LEAVES, NODES), BF16),
            pltpu.VMEM((NODES, 2 * TILE), BF16),
            pltpu.SMEM((MORTONS * SIBS,), jnp.int32),
            pltpu.VMEM((6, LEAVES), jnp.int32),
            pltpu.VMEM((3, NODES, NODES), BF16),
            pltpu.VMEM((LEAVES, NODES), F32),
            pltpu.VMEM((MASK_AT + 21, 8, TILE), F32),
            pltpu.VMEM((1, LEAVES), jnp.int32),
            pltpu.VMEM((1, LEAVES), jnp.int32),
            pltpu.VMEM((6 * TILE, NODES), BF16),
            pltpu.VMEM((6, 16, LANES), BF16),
            pltpu.VMEM((3, TILE, TILE), F32),
            pltpu.VMEM((2, ORDERS, NODES), BF16),
            pltpu.VMEM((ROWS, LANES), BF16),
            pltpu.VMEM((BAND, LANES), BF16),
            pltpu.VMEM((4, BAND, LANES), BF16),
            pltpu.VMEM((3, 4 * LEAVES, NODES), F32),
            pltpu.VMEM((3, LEAVES, NODES), F32),
            pltpu.VMEM((3, LEAVES, LANES), BF16),
            pltpu.VMEM((3, LEAVES, NODES), F32),
            pltpu.VMEM((LEAVES, NODES), F32),
            pltpu.VMEM((LEAVES, LEAVES), F32),
            pltpu.VMEM((3 * LEAVES, NODES), BF16),
            pltpu.VMEM((3 * LEAVES, NODES), BF16),
            pltpu.VMEM((32, 6 * TILE), BF16),
            pltpu.VMEM((2, TILE, TILE), BF16),
            pltpu.VMEM((TILE, 6 * TILE), F32),
            pltpu.VMEM((2, 6, TILE), F32),
            pltpu.VMEM((SIBS, 6, TILE), F32),
            pltpu.VMEM((CORES, X_SIZE * SIBS, 6, TILE), F32),
            pltpu.VMEM((Z_SIZE, 6, TILE), F32),
            pltpu.VMEM((6, TILE), F32),
            pltpu.VMEM((8, TILE), F32),
            pltpu.VMEM((2, 3, 1, MOMENTS), F32),
            dma((19,)),
            dma((4,)),
            dma((2, 3)),
            dma((2, 3)),
            dma((4,)),
            dma((4,)),
            dma((3,)),
            dma((3,)),
            dma((2,)),
            dma((2,)),
            dma((4,)),
            dma((4,)),
            dma((3,)),
            dma((3,)),
            dma((CORES, 16)),
            dma((CORES, 16)),
            dma((15,)),
            dma((15,)),
            pltpu.SemaphoreType.REGULAR((ROUNDS,)),
        ],
        compiler_params=pltpu.CompilerParams(
            collective_id=0, has_side_effects=True, vmem_limit_bytes=60 * 2**20
        ),
    )(
        velocity.transpose(1, 0, 2),
        as_bf16(pick),
        counts,
        neighbors.T,
        pressure,
        as_bf16(diff),
        viscosity,
        jnp.asarray(small.astype(np.float32)),
        levels.reshape(1, LEAVES),
        morton_keys.reshape(1, LEAVES),
        as_bf16(spread),
        as_bf16(sides),
        jnp.asarray(shift.astype(np.float32)),
        jnp.asarray(vand),
    )
    force, mass, box, root = pl.pallas_call(
        finish,
        out_shape=results,
        in_specs=[any_space] * 4,
        out_specs=(any_space,) * 4,
        scratch_shapes=[dma((6,))],
    )(*[pltpu.with_memory_space_constraint(r, pltpu.VMEM) for r in raw])
    return (
        force.transpose(1, 0, 2),
        mass,
        box.transpose(1, 0, 2),
        root.transpose(1, 0, 2),
    )


def solution(mesh):
    in_specs = (
        P(("morton", "sib"), None, None),
        P(("morton", "sib"), None),
        P(("morton", "sib"), None),
        P(("morton", "sib")),
        P(("morton", "sib")),
        P(),
        P(("morton", "sib"), None),
    )
    out_specs = (
        P(("morton", "sib"), None, None),
        P(("morton", "sib"), None),
        P("morton", None, None),
        P("morton", None, None),
    )
    return jax.shard_map(
        on_device, mesh=mesh, in_specs=in_specs, out_specs=out_specs, check_vma=False
    )
```

```python
import functools
import math

import jax
import jax.numpy as jnp
import numpy as np
from jax import lax
from jax.experimental import pallas as pl
from jax.experimental.pallas import tpu as pltpu
from jax.sharding import PartitionSpec as P

DEG = 5
LMAX = 7
MOMENTS = 216
LEAVES = 128
NODES = 512
LANES = 896
BAND = 32
TILE = 128
MESH = pl.DeviceIdType.MESH
F32 = jnp.float32
BF16 = jnp.bfloat16

penalty = 256.0
out_scale = 1.0 / 1024.0
mass_scale = 1.0 / 32.0

X_SIZE, Z_SIZE, CORES, SIBS = 4, 8, 2, 4
ZC = Z_SIZE * CORES
MORTONS = X_SIZE * ZC


def cheb():
    points = -np.cos(np.pi * np.arange(8) / 7.0)
    weights = np.array([(-1.0) ** k for k in range(8)])
    weights[0] *= 0.5
    weights[7] *= 0.5
    derivative = np.zeros((8, 8))
    for row in range(8):
        for col in range(8):
            if row != col:
                derivative[row, col] = weights[col] / weights[row] / (points[row] - points[col])
        derivative[row, row] = -np.sum(derivative[row])
    return points, derivative


def node_of(coords):
    return 64 * coords[0] + 8 * coords[1] + coords[2]


def coords_of(node):
    return [node // 64, node // 8 % 8, node % 8]


def surface_lists():
    x_nodes = [node_of([7 * side, b, c]) for side in range(2) for b in range(8) for c in range(8)]
    inner = [n for n in range(NODES) if coords_of(n)[0] not in (0, 7)]
    on_y = [n for n in inner if coords_of(n)[1] in (0, 7)]
    only_z = [n for n in inner if n not in on_y and coords_of(n)[2] in (0, 7)]
    return x_nodes, on_y + only_z


FACE_TILES = ((0,), (0, 1), (0, 1, 2))
MULT_AT, MASK_AT = 6, 10


def tables():
    points, derivative = cheb()
    eye = np.eye(8)
    directional = [
        np.kron(np.kron(derivative, eye), eye),
        np.kron(np.kron(eye, derivative), eye),
        np.kron(np.kron(eye, eye), derivative),
    ]
    diff = np.stack([m.T for m in directional])
    x_nodes, rest = surface_lists()
    tail = len(rest) - TILE
    pick = np.zeros((NODES, 2 * TILE))
    for k, node in enumerate(rest):
        pick[node, k] = 1.0
    tiles = [list(x_nodes), list(rest[:TILE]), [-1] * TILE]
    for comp in range(3):
        for k in range(tail):
            tiles[2][tail * comp + k] = rest[TILE + k]
    spread = np.zeros((6 * TILE, NODES))
    small = np.zeros((MASK_AT + 21, 8, TILE))
    sides = np.zeros((6, 16, LANES))
    slot = 0
    for dim in range(3):
        for tile in FACE_TILES[dim]:
            for lane, node in enumerate(tiles[tile]):
                if node < 0:
                    continue
                coords = coords_of(node)
                if coords[dim] in (0, 7):
                    other = list(coords)
                    other[dim] = 7 - coords[dim]
                    spread[slot * TILE + lane, node_of(other)] = 1.0
                    for at in (6,) if tile == 2 else range(3 * tile, 3 * tile + 3):
                        sides[2 * dim + (coords[dim] == 0), :, TILE * at + lane] = 1.0
                        if coords[dim] == 7:
                            small[MASK_AT + 7 * dim + at, :, lane] = 1.0
            slot += 1
    for node in range(NODES):
        count = sum(1 for c in coords_of(node) if c in (0, 7))
        small[MULT_AT + node // TILE, :, node % TILE] = count
    vander = np.zeros((288, NODES))
    for jx in range(6):
        for jy in range(6):
            for jz in range(6):
                for node in range(NODES):
                    a, b, c = coords_of(node)
                    vander[jx * 48 + jy * 8 + jz, node] = (
                        points[a] ** jx * points[b] ** jy * points[c] ** jz / 512.0
                    )
    for k in range(6):
        for a in range(6):
            if a >= k:
                small[k, a, :] = math.comb(a, k)
    shift = np.zeros((3, TILE, TILE))
    for row in range(108):
        for col in range(108):
            jy, jz, ay, az = row // 6 % 6, row % 6, col // 6 % 6, col % 6
            if row // 36 == col // 36 and ay >= jy and az >= jz:
                shift[0, row, col] = (
                    math.comb(ay, jy) * math.comb(az, jz) * BOX_IN_ROOT ** (jy + jz)
                )
                shift[1, row, col] = ay - jy
                shift[2, row, col] = az - jz
    return diff, pick, spread, sides, shift, vander, small, tail


BOX_CELLS = 2 ** ((3 * LMAX - 6) // 3)
FINEST = 1.0 / 2**LMAX
BOX_SIDE = BOX_CELLS * FINEST
BOX_SCALE = 0.5 * BOX_SIDE
BOX_IN_ROOT = BOX_SCALE / 0.5

(
    VEL_IN,
    PICK_IN,
    COUNTS_IN,
    NBR_IN,
    PRESS_IN,
    DIFF_IN,
    VISC_IN,
    SMALL_IN,
    LEVELS_IN,
    KEYS_IN,
    SPREAD_IN,
    SIDES_IN,
    SHIFT_IN,
    VAND_IN,
) = range(14)
QUARTER = LEAVES // 4
HALF_BAND = BAND // 2
ROUNDS = 4
ORDERS = 288
BANDS_AT, LAST_AT, ROWS = 4 * LEAVES, 4 * LEAVES + 6 * BAND, 4 * LEAVES + 8 * BAND


def dot(a, b):
    return jnp.dot(a, b, preferred_element_type=F32)


def dot_nt(a, b):
    return lax.dot_general(a, b, (((1,), (1,)), ((), ())), preferred_element_type=F32)


def split(value):
    high = value.astype(BF16)
    return high, (value - high.astype(F32)).astype(BF16)


def flat_rows(packed, out_ref):
    lane = lax.broadcasted_iota(jnp.int32, (8, TILE), 1)
    sub = lax.broadcasted_iota(jnp.int32, (8, TILE), 0)
    first_tile = (sub < 3) | ((sub == 3) & (lane >= 108))
    valid = jnp.bitwise_and(lane - 36 * sub, TILE - 1) < 36
    turned = {0: packed}
    for by in range(-2, DEG + 1):
        if by:
            turned[by] = pltpu.roll(packed, 36 * by % TILE, 1)
    for comp in range(3):
        rows = turned[-comp]
        for ax in range(1, DEG + 1):
            rows = jnp.where(sub == ax, turned[ax - comp], rows)
        rows = jnp.where(valid & (sub < 6), rows, 0.0)
        near = jnp.sum(jnp.where(first_tile, rows, 0.0), axis=0, keepdims=True)
        far = jnp.sum(jnp.where(first_tile, 0.0, rows), axis=0, keepdims=True)
        out_ref[comp, :, 0:TILE] = near
        out_ref[comp, :, TILE:MOMENTS] = far[:, : MOMENTS - TILE]


def kernel(
    tail,
    vel_hbm,
    pick_hbm,
    counts_hbm,
    nbr_hbm,
    press_hbm,
    diff_hbm,
    visc_hbm,
    small_hbm,
    levels_hbm,
    keys_hbm,
    spread_hbm,
    sides_hbm,
    shift_hbm,
    vand_hbm,
    force_out_ref,
    mass_out_ref,
    box_out_ref,
    root_out_ref,
    field,
    pick,
    counts,
    nbr_in,
    diff,
    visc,
    small,
    levels,
    keys,
    spread,
    sides,
    shift_tab,
    vand,
    tab,
    link_band,
    chip_band,
    grads,
    local,
    picked,
    force,
    mass,
    pos_sq,
    weight,
    force_high,
    force_low,
    x_tables,
    root_yz,
    mcat,
    part,
    recv_box,
    recv_a,
    recv_b,
    sum_b,
    tall,
    flat,
    in_sem,
    out_sem,
    ring_send,
    ring_recv,
    fwd_send,
    fwd_recv,
    link_send,
    link_recv,
    relay_send,
    relay_recv,
    hand_send,
    chip_send,
    chip_recv,
    box_send,
    box_recv,
    a_send,
    a_recv,
    b_send,
    b_recv,
    known,
):
    m = lax.axis_index("morton")
    s = lax.axis_index("sib")
    x_at = lax.div(m, ZC)
    zc_at = lax.rem(m, ZC)
    core = lax.rem(m, CORES)
    above = lax.rem(s + 1, SIBS)
    below = lax.rem(s + SIBS - 1, SIBS)
    m_chip = m + 1 - 2 * core
    m_link = lax.rem(m + MORTONS - 1 + 2 * core, MORTONS)

    linked = (m > 0) & (m < MORTONS - 1)

    def group_a(dx, dy):
        return (lax.rem(x_at + dx, X_SIZE) * ZC + zc_at, lax.rem(s + dy, SIBS))

    def group_b(dz):
        return (x_at * ZC + lax.rem(zc_at + dz, ZC), s)

    a_steps = [(dx, dy) for dx in range(X_SIZE) for dy in range(SIBS) if dx or dy]

    loads = [
        pltpu.make_async_copy(
            vel_hbm.at[0, pl.ds(0, 64)], field.at[0, pl.ds(0, 64)], in_sem.at[VEL_IN]
        ),
        pltpu.make_async_copy(pick_hbm, pick, in_sem.at[PICK_IN]),
        pltpu.make_async_copy(counts_hbm, counts, in_sem.at[COUNTS_IN]),
        pltpu.make_async_copy(nbr_hbm, nbr_in, in_sem.at[NBR_IN]),
        pltpu.make_async_copy(press_hbm, field.at[3], in_sem.at[PRESS_IN]),
        pltpu.make_async_copy(diff_hbm, diff, in_sem.at[DIFF_IN]),
        pltpu.make_async_copy(visc_hbm, visc, in_sem.at[VISC_IN]),
        pltpu.make_async_copy(small_hbm, small, in_sem.at[SMALL_IN]),
        pltpu.make_async_copy(levels_hbm, levels, in_sem.at[LEVELS_IN]),
        pltpu.make_async_copy(keys_hbm, keys, in_sem.at[KEYS_IN]),
        pltpu.make_async_copy(spread_hbm, spread, in_sem.at[SPREAD_IN]),
        pltpu.make_async_copy(sides_hbm, sides, in_sem.at[SIDES_IN]),
        pltpu.make_async_copy(shift_hbm, shift_tab, in_sem.at[SHIFT_IN]),
        pltpu.make_async_copy(vand_hbm, vand, in_sem.at[VAND_IN]),
    ]
    more_velocity = [
        pltpu.make_async_copy(
            vel_hbm.at[k // 2, pl.ds(k % 2 * 64, 64)],
            field.at[k // 2, pl.ds(k % 2 * 64, 64)],
            in_sem.at[VAND_IN + k],
        )
        for k in range(1, 6)
    ]
    for copy in [loads[VEL_IN], loads[PICK_IN]] + more_velocity:
        copy.start()
    for which in (COUNTS_IN, NBR_IN):
        loads[which].start()

    near_groups = [group_a(1, 0), group_a(X_SIZE - 1, 0), group_b(1), group_b(ZC - 1)]
    near = [(m, above), (m, below), (m_link, s)] + near_groups
    barrier = pltpu.get_barrier_semaphore()
    for device in near:
        pl.semaphore_signal(barrier, inc=1, device_id=device, device_id_type=MESH)

    loads[VEL_IN].wait()
    for copy in more_velocity:
        copy.wait()
    loads[PICK_IN].wait()
    for which in range(PRESS_IN, len(loads)):
        loads[which].start()
    lane = lax.broadcasted_iota(jnp.int32, (LEAVES, TILE), 1)
    rest = dot(field[0:3].reshape(3 * LEAVES, NODES), pick[...])
    shared = jnp.zeros((LEAVES, TILE), F32)
    for comp in range(3):
        first = field[comp, :, 0:TILE].astype(F32)
        last = field[comp, :, NODES - TILE : NODES].astype(F32)
        tab[0:LEAVES, TILE * comp : TILE * (comp + 1)] = jnp.where(lane < 64, first, last).astype(BF16)
        rows = rest[LEAVES * comp : LEAVES * (comp + 1)]
        tab[0:LEAVES, TILE * (3 + comp) : TILE * (4 + comp)] = rows[:, 0:TILE].astype(BF16)
        piece = rows[:, TILE : 2 * TILE]
        if comp:
            piece = pltpu.roll(piece, tail * comp, 1)
        shared = shared + piece
    tab[0:LEAVES, TILE * 6 : TILE * 7] = shared.astype(BF16)

    pl.semaphore_wait(barrier, len(near))

    def send(src, dst, send_sem, recv_sem, device):
        return pltpu.make_async_remote_copy(
            src_ref=src,
            dst_ref=dst,
            send_sem=send_sem,
            recv_sem=recv_sem,
            device_id=device,
            device_id_type=MESH,
        )

    def quarters(block, q, count=1):
        return tab.at[pl.ds(LEAVES * block + QUARTER * q, QUARTER * count)]

    def link_rows(b, first=0, rows=BAND):
        return tab.at[pl.ds((LAST_AT if b == 3 else BANDS_AT + BAND * b) + first, rows)]

    def chip_rows(b):
        return tab.at[pl.ds(LAST_AT + BAND if b == 3 else BANDS_AT + BAND * (3 + b), BAND)]

    def to_neighbour(way, k, q, count):
        block, device = ((2, (m, above)), (1, (m, below)))[way]
        return send(
            quarters(0, q, count),
            quarters(block, q, count),
            ring_send.at[way, k],
            ring_recv.at[way, k],
            device,
        )

    ups = [to_neighbour(0, k, *part) for k, part in enumerate(((0, 1), (1, 1), (2, 2)))]
    downs = [to_neighbour(1, k, q, 1) for k, q in enumerate((2, 3, 0, 1))]
    forwards = [
        send(quarters(2, 0), quarters(3, 0), fwd_send.at[0], fwd_recv.at[0], (m, above)),
        send(quarters(1, 2), quarters(3, 2), fwd_send.at[1], fwd_recv.at[1], (m, below)),
        send(quarters(2, 1), quarters(3, 1), fwd_send.at[2], fwd_recv.at[2], (m, above)),
        send(quarters(1, 3), quarters(3, 3), fwd_send.at[3], fwd_recv.at[3], (m, below)),
    ]
    links = [
        send(link_band, link_rows(0), link_send.at[0], link_recv.at[0], (m_link, s)),
        send(link_band, link_rows(2), link_send.at[1], link_recv.at[1], (m_link, above)),
        send(link_band, link_rows(1), link_send.at[2], link_recv.at[2], (m_link, below)),
    ]
    relays = [
        send(
            link_rows(2, 0, HALF_BAND),
            link_rows(3, 0, HALF_BAND),
            relay_send.at[0],
            relay_recv.at[0],
            (m, above),
        ),
        send(
            link_rows(1, HALF_BAND, HALF_BAND),
            link_rows(3, HALF_BAND, HALF_BAND),
            relay_send.at[1],
            relay_recv.at[1],
            (m, below),
        ),
    ]
    def hand_over(k, block, device, first):
        rows = pl.ds(LEAVES * block, BAND)
        part = pl.ds(LEAVES * block + first, HALF_BAND)
        return [
            send(tab.at[rows], link_rows(block), hand_send.at[k], link_recv.at[3 - block], (m_link, s)),
            send(
                tab.at[part],
                link_rows(3, first, HALF_BAND),
                hand_send.at[k + 1],
                relay_recv.at[k // 2],
                (m_link, device),
            ),
        ]

    from_up = hand_over(0, 2, above, 0)
    from_down = hand_over(2, 1, below, HALF_BAND)
    chips = [
        send(chip_band.at[b], chip_rows(b), chip_send.at[b], chip_recv.at[b], (m_chip, s))
        for b in range(4)
    ]
    turn = [0, 1, 3, 2]
    band_row = lax.broadcasted_iota(jnp.int32, (BAND, LEAVES), 0)
    band_col = lax.broadcasted_iota(jnp.int32, (BAND, LEAVES), 1)

    def band(b, last):
        live = counts[m * SIBS + lax.rem(s + turn[b], SIBS)]
        chosen = jnp.where(band_col == band_row + last * (live - BAND), 1.0, 0.0).astype(BF16)
        return dot(chosen, tab[LEAVES * b : LEAVES * (b + 1)]).astype(BF16)

    def send_chip(b):
        chip_band[b] = band(b, 1 - core)
        chips[b].start()

    round_peers = []
    for k in range(ROUNDS):
        peers = [group_a(1, 0), group_a(X_SIZE - 1, 0), (m, above), (m, below)]
        if k < 3:
            peers += [group_b(2**k), group_b(ZC - 2**k)]
        round_peers.append(peers)

    def tell(k):
        for device in round_peers[k]:
            pl.semaphore_signal(known.at[k], inc=1, device_id=device, device_id_type=MESH)

    def hear(k):
        pl.semaphore_wait(known.at[k], len(round_peers[k]))

    ups[0].start()
    downs[0].start()
    ups[1].start()
    downs[1].start()
    tell(0)
    loads[COUNTS_IN].wait()
    link_band[...] = band(0, core)

    @pl.when(linked)
    def _():
        links[0].start()

    @pl.when(jnp.logical_not(linked))
    def _():
        tab[BANDS_AT : BANDS_AT + 3 * BAND, :] = jnp.zeros((3 * BAND, LANES), BF16)
        tab[LAST_AT : LAST_AT + BAND, :] = jnp.zeros((BAND, LANES), BF16)

    loads[NBR_IN].wait()
    nbr = nbr_in[...]
    owner_sib = jnp.bitwise_and(jnp.right_shift(nbr, 7), 3)
    slot = jnp.bitwise_and(nbr, LEAVES - 1)
    step = jnp.right_shift(nbr, 9) - m
    offset = jnp.bitwise_and(owner_sib - s + SIBS, 3)
    block = jnp.where(offset == 2, 3, jnp.where(offset == 3, 2, offset))
    prior = lax.rem(m + MORTONS - 1, MORTONS) * SIBS
    prior_live = jnp.zeros_like(nbr)
    for k in range(SIBS):
        prior_live = jnp.where(owner_sib == k, counts[prior + k], prior_live)
    apart = jnp.where(block == 3, BAND, 3 * BAND)
    halo_row = jnp.where(block == 3, LAST_AT, BANDS_AT + block * BAND) + slot
    row = jnp.where(
        step == 0,
        block * LEAVES + slot,
        jnp.where(
            step == 1,
            halo_row + (1 - core) * apart,
            halo_row + core * apart - (prior_live - BAND),
        ),
    )
    row = jnp.where(nbr < 0, -1, row).astype(F32)
    pos_sq[...] = jnp.zeros_like(pos_sq)
    pos_sq[0:6, :] = row
    pos_sq[...] = pos_sq[...].T

    def gather(first, rows, fresh=False):
        col = lax.broadcasted_iota(jnp.int32, (LEAVES, rows), 1).astype(F32) + float(first)
        for dim in range(3):
            pair = []
            for face in (2 * dim, 2 * dim + 1):
                at = pos_sq[:, face : face + 1]
                pair.append(jnp.where(col == at, 1.0, 0.0))
            chosen = jnp.concatenate(pair, axis=0).astype(BF16)
            width = TILE * (3, 6, 7)[dim]
            got = dot(chosen, tab[first : first + rows, 0:width])
            for tile in range(width // TILE):
                lanes = slice(TILE * tile, TILE * (tile + 1))
                mask = small[MASK_AT + 7 * dim + tile, 0:1, :] > 0.5
                one = jnp.where(mask, got[0:LEAVES, lanes], got[LEAVES:, lanes]).astype(BF16)
                if fresh:
                    picked[dim, :, lanes] = one
                else:
                    picked[dim, :, lanes] += one

    send_chip(0)
    loads[SMALL_IN].wait()
    gather(0, LEAVES, True)
    hear(0)
    downs[2].start()

    @pl.when((core == 1) & linked)
    def _():
        links[1].start()
        links[2].start()

    tell(1)

    loads[PRESS_IN].wait()
    loads[DIFF_IN].wait()
    stacked = field[...].reshape(4 * LEAVES, NODES)
    for dim in range(3):
        grads[dim] = dot(stacked, diff[dim])
        if dim == 1:
            ups[2].start()
            downs[3].start()

    own_live = counts[m * SIBS + s]
    leaf_row = lax.broadcasted_iota(jnp.int32, (LEAVES, NODES), 0)
    live_rows = leaf_row < own_live

    def grad(comp, dim):
        return grads[dim, LEAVES * comp : LEAVES * (comp + 1), :]

    mass[...] = jnp.where(
        live_rows, -(grad(0, 0) + grad(1, 1) + grad(2, 2)) * mass_scale, 0.0
    )
    mass_out = pltpu.make_async_copy(mass, mass_out_ref, out_sem.at[0])
    mass_out.start()

    loads[VISC_IN].wait()
    stress = {}
    for i in range(3):
        for j in range(i, 3):
            stress[i, j] = (visc[...] * (grad(i, j) + grad(j, i))).astype(BF16)
    total = None
    for j in range(3):
        rows = jnp.concatenate([stress[min(i, j), max(i, j)] for i in range(3)], axis=0)
        term = dot(rows, diff[j])
        total = term if total is None else total + term
    mult = jnp.concatenate([small[MULT_AT + t, 0:1, :] for t in range(4)], axis=1)
    for comp in range(3):
        jump = field[comp].astype(F32) * mult
        value = (
            penalty * visc[...] * jump
            - total[LEAVES * comp : LEAVES * (comp + 1)]
            + grad(3, comp)
        ) * out_scale
        local[comp] = jnp.where(live_rows, value, 0.0)
    ups[0].wait_recv()
    forwards[0].start()

    @pl.when((core == 0) & linked)
    def _():
        for copy in from_up:
            copy.start()

    downs[0].wait_recv()
    forwards[1].start()
    ups[1].wait_recv()
    forwards[2].start()
    downs[1].wait_recv()
    forwards[3].start()
    downs[2].wait_recv()

    @pl.when((core == 0) & linked)
    def _():
        for copy in from_down:
            copy.start()
        links[1].wait_recv()
        relays[0].start()
        links[2].wait_recv()
        relays[1].start()

    hear(1)
    tell(2)

    weight[...] = jnp.where(live_rows, (penalty * out_scale) * visc[...], 0.0)
    loads[LEVELS_IN].wait()
    loads[KEYS_IN].wait()
    level = levels[...]
    shift_bits = 3 * (LMAX - level)
    anchor = jnp.left_shift(jnp.right_shift(keys[...], shift_bits), shift_bits)
    span = jnp.left_shift(jnp.ones_like(level), LMAX - level).astype(F32)
    at_box = []
    box_center = []
    for dim, bit0 in enumerate((2, 1, 0)):
        cell = jnp.zeros_like(anchor)
        corner = 0
        for bit in range(LMAX):
            cell = cell + jnp.left_shift(
                jnp.bitwise_and(jnp.right_shift(anchor, 3 * bit + bit0), 1), bit
            )
            up_bit = 3 * bit + bit0 - (3 * LMAX - 6)
            if up_bit >= 0:
                corner = corner + lax.rem(lax.div(m, 2**up_bit), 2) * 2**bit
        center = corner.astype(F32) * FINEST + 0.5 * BOX_SIDE
        box_center.append(center)
        at_box.append(((cell.astype(F32) + 0.5 * span) * FINEST - center) / BOX_SCALE)
    half = 0.5 * span * FINEST / BOX_SCALE
    sub = lax.broadcasted_iota(jnp.int32, (8, TILE), 0)

    def power_rows(value):
        value = jnp.broadcast_to(value, (8, TILE))
        power = jnp.ones((8, TILE), F32)
        rows = power
        for k in range(1, DEG + 1):
            power = power * value
            rows = jnp.where(sub == k, power, rows)
        return rows

    loads[SHIFT_IN].wait()
    half_rows = power_rows(half)
    half_wide = jnp.broadcast_to(half, (8, TILE))
    scales = [half_rows]
    for _ in range(DEG):
        scales.append(scales[-1] * half_wide)

    def x_table(at, size):
        wide = jnp.broadcast_to(size, (8, TILE))
        rows = power_rows(at)
        size_power = jnp.ones((8, TILE), F32)
        tiles = []
        for k in range(DEG + 1):
            turned = rows if k == 0 else pltpu.roll(rows, k, 0)
            tiles.append(small[k] * turned * size_power)
            size_power = size_power * wide
        return split(jnp.concatenate(tiles, axis=1))

    at_root = (at_box[0] * BOX_SCALE + box_center[0] - 0.5) / 0.5
    box_high, box_low = x_table(at_box[0], half)
    root_high, root_low = x_table(at_root, half * BOX_IN_ROOT)
    x_tables[...] = jnp.concatenate([box_high, root_high, box_low, root_low], axis=0)
    moves = shift_tab[0]
    for dim, exponents in ((1, shift_tab[1]), (2, shift_tab[2])):
        by = (box_center[dim] - 0.5) / 0.5
        power = by
        factor = jnp.ones((TILE, TILE), F32)
        for k in range(1, DEG + 1):
            factor = jnp.where(exponents == float(k), power, factor)
            power = power * by
        moves = moves * factor
    move_high, move_low = split(moves)
    root_yz[0] = move_high
    root_yz[1] = move_low
    y_wide = jnp.broadcast_to(at_box[1], (8, TILE))
    z_wide = jnp.broadcast_to(at_box[2], (8, TILE))
    z_coef = []
    z_power = jnp.ones((8, TILE), F32)
    for k in range(DEG + 1):
        z_coef.append(small[k] * z_power)
        z_power = z_power * z_wide

    downs[3].wait_recv()
    send_chip(1)
    ups[2].wait_recv()
    send_chip(2)
    gather(LEAVES, 2 * LEAVES)
    loads[SPREAD_IN].wait()
    hear(2)
    tell(3)
    for copy in chips[:3]:
        copy.wait_recv()

    @pl.when(linked)
    def _():
        links[0].wait_recv()

    @pl.when((core == 1) & linked)
    def _():
        links[1].wait_recv()
        links[2].wait_recv()

    gather(BANDS_AT, 6 * BAND)
    for k in range(4):
        forwards[k].wait_recv()
    send_chip(3)
    gather(3 * LEAVES, LEAVES)
    hear(3)
    loads[SIDES_IN].wait()
    loads[VAND_IN].wait()
    chips[3].wait_recv()

    @pl.when(linked)
    def _():
        for copy in relays:
            copy.wait_recv()

    col = lax.broadcasted_iota(jnp.int32, (LEAVES, 2 * BAND), 1).astype(F32) + float(LAST_AT)
    near_sums = []
    for dim in range(3):
        width = TILE * (3, 6, 7)[dim]
        chosen = [
            jnp.where(col == pos_sq[:, face : face + 1], 1.0, 0.0)
            for face in (2 * dim, 2 * dim + 1)
        ]
        chosen = jnp.concatenate(chosen, axis=1).astype(BF16)
        late = tab[LAST_AT:ROWS, 0:width]
        side = [
            late * jnp.concatenate([sides[2 * dim + k, :, 0:width]] * 4, axis=0)
            for k in range(2)
        ]
        got = dot(chosen, jnp.concatenate(side, axis=0)).astype(BF16)
        near_sums.append(picked[dim, :, 0:width] + got)

    rows = []
    for comp in range(3):
        parts = []
        for dim in range(3):
            for tile in FACE_TILES[dim]:
                at = 6 if tile == 2 else 3 * tile + comp
                value = near_sums[dim][:, TILE * at : TILE * (at + 1)]
                if tile == 2:
                    mine = (lane >= tail * comp) & (lane < tail * (comp + 1))
                    value = jnp.where(mine, value.astype(F32), 0.0).astype(BF16)
                parts.append(value)
        rows.append(jnp.concatenate(parts, axis=1))
    across = dot(jnp.concatenate(rows, axis=0), spread[...])
    for comp in range(3):
        there = across[LEAVES * comp : LEAVES * (comp + 1)]
        value = local[comp] - weight[...] * there
        force[comp] = value
        high, low = split(value)
        force_high[LEAVES * comp : LEAVES * (comp + 1), :] = high
        force_low[LEAVES * comp : LEAVES * (comp + 1), :] = low
    force_out = pltpu.make_async_copy(force, force_out_ref, out_sem.at[1])
    force_out.start()

    by_force = dot_nt(vand[...].reshape(2 * ORDERS, NODES), force_high[...])
    leaf_moments = by_force[0:ORDERS] + by_force[ORDERS:] + dot_nt(vand[0], force_low[...])
    for comp in range(3):
        for jx in range(6):
            columns = []
            for jy in range(6):
                first = jx * 48 + jy * 8
                base = leaf_moments[first : first + 8, TILE * comp : TILE * (comp + 1)] * scales[jy]
                moved = base * z_coef[0]
                for k in range(1, DEG + 1):
                    moved = moved + z_coef[k] * pltpu.roll(base, k, 0)
                columns.append(moved)
            for low in range(1, DEG + 1):
                for at in range(DEG, low - 1, -1):
                    columns[at] = columns[at] + y_wide * columns[at - 1]
            for jy in range(6):
                first = 36 * comp + 6 * jy
                mcat[first : first + 6, TILE * jx : TILE * (jx + 1)] = columns[jy][0:6]
    mcat[108:TILE, :] = jnp.zeros((TILE - 108, 6 * TILE), F32)
    c_high, c_low = split(mcat[...])
    by_parts = dot_nt(x_tables[...], c_high)
    both = by_parts[0:16] + by_parts[16:32] + dot_nt(x_tables[0:16], c_low)
    own_box = both[0:6]

    r_high, r_low = split(both[8:16])
    shifted = (
        dot(r_high, root_yz[0]) + dot(r_low, root_yz[0]) + dot(r_high, root_yz[1])
    )[0:6]

    part[0] = own_box
    part[1] = shifted
    recv_box[s] = own_box
    box_copies = [
        send(
            part.at[0],
            recv_box.at[s],
            box_send.at[k],
            box_recv.at[k],
            (m, lax.rem(s + 1 + k, SIBS)),
        )
        for k in range(SIBS - 1)
    ]
    at_a = x_at * SIBS + s
    z_at = lax.div(zc_at, CORES)
    from_core = []
    for k in range(CORES):
        copies = []
        for n, (dx, dy) in enumerate(([(0, 0)] if k == 0 else []) + a_steps):
            to = (lax.rem(x_at + dx, X_SIZE) * ZC + zc_at + 1 - core, lax.rem(s + dy, SIBS))
            copies.append(
                send(part.at[1], recv_a.at[k, at_a], a_send.at[k, n], a_recv.at[k, n], to)
            )
        from_core.append(copies)
    b_steps = [CORES * k for k in range(1, Z_SIZE)] + [CORES * k + 1 for k in range(Z_SIZE)]
    b_copies = [
        send(
            sum_b,
            recv_b.at[z_at],
            b_send.at[k],
            b_recv.at[k],
            (x_at * ZC + lax.rem(CORES * z_at + 1 + step, ZC), s),
        )
        for k, step in enumerate(b_steps)
    ]
    to_core_1, to_core_0 = b_copies[: Z_SIZE - 1], b_copies[Z_SIZE - 1 :]

    @pl.when(core == 0)
    def _():
        for copy in from_core[0]:
            copy.start()

    @pl.when(core == 1)
    def _():
        recv_a[1, at_a] = shifted
        for copy in from_core[1]:
            copy.start()

    for copy in box_copies:
        copy.start()

    for copy in box_copies:
        copy.wait_recv()
    box = recv_box[0]
    for k in range(1, SIBS):
        box = box + recv_box[k]
    tall[...] = jnp.zeros_like(tall)
    tall[0:6, :] = box
    flat_rows(tall[...], flat.at[0])
    box_out = pltpu.make_async_copy(flat.at[0], box_out_ref, out_sem.at[2])
    box_out.start()

    @pl.when(core == 1)
    def _():
        for copies in from_core:
            for copy in copies:
                copy.wait_recv()
        plane = recv_a[0, 0] + recv_a[1, 0]
        for k in range(1, X_SIZE * SIBS):
            plane = plane + (recv_a[0, k] + recv_a[1, k])
        sum_b[...] = plane
        recv_b[z_at] = plane
        for copy in b_copies:
            copy.start()
        for copy in to_core_1:
            copy.wait_recv()

    @pl.when(core == 0)
    def _():
        for copy in to_core_0:
            copy.wait_recv()

    total = recv_b[0]
    for k in range(1, Z_SIZE):
        total = total + recv_b[k]
    tall[0:6, :] = total
    flat_rows(tall[...], flat.at[1])
    root_out = pltpu.make_async_copy(flat.at[1], root_out_ref, out_sem.at[3])
    root_out.start()

    for copy in ups + downs + forwards + chips + box_copies:
        copy.wait_send()

    @pl.when(linked)
    def _():
        links[0].wait_send()

    @pl.when((core == 0) & linked)
    def _():
        for copy in relays + from_up + from_down:
            copy.wait_send()

    @pl.when((core == 1) & linked)
    def _():
        for copy in links[1:]:
            copy.wait_send()

    @pl.when(core == 0)
    def _():
        for copy in from_core[0]:
            copy.wait_send()

    @pl.when(core == 1)
    def _():
        for copy in from_core[1] + b_copies:
            copy.wait_send()

    mass_out.wait()
    force_out.wait()
    box_out.wait()
    root_out.wait()


def finish(force, mass, box, root, force_out, mass_out, box_out, root_out, sem):
    pairs = [(force.at[k], force_out.at[k]) for k in range(3)]
    pairs += [(mass, mass_out), (box, box_out), (root, root_out)]
    copies = [pltpu.make_async_copy(a, b, sem.at[k]) for k, (a, b) in enumerate(pairs)]
    for copy in copies:
        copy.start()
    for copy in copies:
        copy.wait()


def on_device(velocity, pressure, viscosity, levels, morton_keys, counts, neighbors):
    diff, pick, spread, sides, shift, vander, small, tail = tables()
    as_bf16 = lambda a: jnp.asarray(a.astype(np.float32)).astype(BF16)
    vander32 = vander.astype(np.float32)
    v_high = vander32.astype(jnp.bfloat16)
    v_low = (vander32 - v_high.astype(np.float32)).astype(jnp.bfloat16)
    vand = np.stack([v_high, v_low])
    dma = pltpu.SemaphoreType.DMA
    any_space = pl.BlockSpec(memory_space=pl.ANY)
    hbm = pl.BlockSpec(memory_space=pltpu.HBM)
    results = (
        jax.ShapeDtypeStruct((3, LEAVES, NODES), F32),
        jax.ShapeDtypeStruct((LEAVES, NODES), F32),
        jax.ShapeDtypeStruct((3, 1, MOMENTS), F32),
        jax.ShapeDtypeStruct((3, 1, MOMENTS), F32),
    )
    raw = pl.pallas_call(
        functools.partial(kernel, tail),
        out_shape=tuple(pltpu.VMEM(r.shape, r.dtype) for r in results),
        in_specs=[hbm] * 14,
        out_specs=(any_space,) * 4,
        scratch_shapes=[
            pltpu.VMEM((4, LEAVES, NODES), BF16),
            pltpu.VMEM((NODES, 2 * TILE), BF16),
            pltpu.SMEM((MORTONS * SIBS,), jnp.int32),
            pltpu.VMEM((6, LEAVES), jnp.int32),
            pltpu.VMEM((3, NODES, NODES), BF16),
            pltpu.VMEM((LEAVES, NODES), F32),
            pltpu.VMEM((MASK_AT + 21, 8, TILE), F32),
            pltpu.VMEM((1, LEAVES), jnp.int32),
            pltpu.VMEM((1, LEAVES), jnp.int32),
            pltpu.VMEM((6 * TILE, NODES), BF16),
            pltpu.VMEM((6, 16, LANES), BF16),
            pltpu.VMEM((3, TILE, TILE), F32),
            pltpu.VMEM((2, ORDERS, NODES), BF16),
            pltpu.VMEM((ROWS, LANES), BF16),
            pltpu.VMEM((BAND, LANES), BF16),
            pltpu.VMEM((4, BAND, LANES), BF16),
            pltpu.VMEM((3, 4 * LEAVES, NODES), F32),
            pltpu.VMEM((3, LEAVES, NODES), F32),
            pltpu.VMEM((3, LEAVES, LANES), BF16),
            pltpu.VMEM((3, LEAVES, NODES), F32),
            pltpu.VMEM((LEAVES, NODES), F32),
            pltpu.VMEM((LEAVES, LEAVES), F32),
            pltpu.VMEM((LEAVES, NODES), F32),
            pltpu.VMEM((3 * LEAVES, NODES), BF16),
            pltpu.VMEM((3 * LEAVES, NODES), BF16),
            pltpu.VMEM((32, 6 * TILE), BF16),
            pltpu.VMEM((2, TILE, TILE), BF16),
            pltpu.VMEM((TILE, 6 * TILE), F32),
            pltpu.VMEM((2, 6, TILE), F32),
            pltpu.VMEM((SIBS, 6, TILE), F32),
            pltpu.VMEM((CORES, X_SIZE * SIBS, 6, TILE), F32),
            pltpu.VMEM((Z_SIZE, 6, TILE), F32),
            pltpu.VMEM((6, TILE), F32),
            pltpu.VMEM((8, TILE), F32),
            pltpu.VMEM((2, 3, 1, MOMENTS), F32),
            dma((19,)),
            dma((4,)),
            dma((2, 4)),
            dma((2, 4)),
            dma((4,)),
            dma((4,)),
            dma((3,)),
            dma((3,)),
            dma((2,)),
            dma((2,)),
            dma((4,)),
            dma((4,)),
            dma((4,)),
            dma((3,)),
            dma((3,)),
            dma((CORES, 16)),
            dma((CORES, 16)),
            dma((15,)),
            dma((15,)),
            pltpu.SemaphoreType.REGULAR((ROUNDS,)),
        ],
        compiler_params=pltpu.CompilerParams(
            collective_id=0, has_side_effects=True, vmem_limit_bytes=60 * 2**20
        ),
    )(
        velocity.transpose(1, 0, 2),
        as_bf16(pick),
        counts,
        neighbors.T,
        pressure,
        as_bf16(diff),
        viscosity,
        jnp.asarray(small.astype(np.float32)),
        levels.reshape(1, LEAVES),
        morton_keys.reshape(1, LEAVES),
        as_bf16(spread),
        as_bf16(sides),
        jnp.asarray(shift.astype(np.float32)),
        jnp.asarray(vand),
    )
    force, mass, box, root = pl.pallas_call(
        finish,
        out_shape=results,
        in_specs=[any_space] * 4,
        out_specs=(any_space,) * 4,
        scratch_shapes=[dma((6,))],
    )(*[pltpu.with_memory_space_constraint(r, pltpu.VMEM) for r in raw])
    return (
        force.transpose(1, 0, 2),
        mass,
        box.transpose(1, 0, 2),
        root.transpose(1, 0, 2),
    )


def solution(mesh):
    in_specs = (
        P(("morton", "sib"), None, None),
        P(("morton", "sib"), None),
        P(("morton", "sib"), None),
        P(("morton", "sib")),
        P(("morton", "sib")),
        P(),
        P(("morton", "sib"), None),
    )
    out_specs = (
        P(("morton", "sib"), None, None),
        P(("morton", "sib"), None),
        P("morton", None, None),
        P("morton", None, None),
    )
    return jax.shard_map(
        on_device, mesh=mesh, in_specs=in_specs, out_specs=out_specs, check_vma=False
    )
```

```python
import functools
import math

import jax
import jax.numpy as jnp
import numpy as np
from jax import lax
from jax.experimental import pallas as pl
from jax.experimental.pallas import tpu as pltpu
from jax.sharding import PartitionSpec as P

DEG = 5
LMAX = 7
MOMENTS = 216
LEAVES = 128
NODES = 512
LANES = 896
BAND = 32
TILE = 128
MESH = pl.DeviceIdType.MESH
F32 = jnp.float32
BF16 = jnp.bfloat16

penalty = 256.0
out_scale = 1.0 / 1024.0
mass_scale = 1.0 / 32.0

X_SIZE, Z_SIZE, CORES, SIBS = 4, 8, 2, 4
ZC = Z_SIZE * CORES
MORTONS = X_SIZE * ZC


def cheb():
    points = -np.cos(np.pi * np.arange(8) / 7.0)
    weights = np.array([(-1.0) ** k for k in range(8)])
    weights[0] *= 0.5
    weights[7] *= 0.5
    derivative = np.zeros((8, 8))
    for row in range(8):
        for col in range(8):
            if row != col:
                derivative[row, col] = weights[col] / weights[row] / (points[row] - points[col])
        derivative[row, row] = -np.sum(derivative[row])
    return points, derivative


def node_of(coords):
    return 64 * coords[0] + 8 * coords[1] + coords[2]


def coords_of(node):
    return [node // 64, node // 8 % 8, node % 8]


def surface_lists():
    x_nodes = [node_of([7 * side, b, c]) for side in range(2) for b in range(8) for c in range(8)]
    inner = [n for n in range(NODES) if coords_of(n)[0] not in (0, 7)]
    on_y = [n for n in inner if coords_of(n)[1] in (0, 7)]
    only_z = [n for n in inner if n not in on_y and coords_of(n)[2] in (0, 7)]
    return x_nodes, on_y + only_z


FACE_TILES = ((0,), (0, 1), (0, 1, 2))
MULT_AT, MASK_AT = 6, 10


def tables():
    points, derivative = cheb()
    eye = np.eye(8)
    directional = [
        np.kron(np.kron(derivative, eye), eye),
        np.kron(np.kron(eye, derivative), eye),
        np.kron(np.kron(eye, eye), derivative),
    ]
    diff = np.stack([m.T for m in directional])
    x_nodes, rest = surface_lists()
    tail = len(rest) - TILE
    pick = np.zeros((NODES, 2 * TILE))
    for k, node in enumerate(rest):
        pick[node, k] = 1.0
    tiles = [list(x_nodes), list(rest[:TILE]), [-1] * TILE]
    for comp in range(3):
        for k in range(tail):
            tiles[2][tail * comp + k] = rest[TILE + k]
    spread = np.zeros((6 * TILE, NODES))
    small = np.zeros((MASK_AT + 21, 8, TILE))
    sides = np.zeros((6, 16, LANES))
    slot = 0
    for dim in range(3):
        for tile in FACE_TILES[dim]:
            for lane, node in enumerate(tiles[tile]):
                if node < 0:
                    continue
                coords = coords_of(node)
                if coords[dim] in (0, 7):
                    other = list(coords)
                    other[dim] = 7 - coords[dim]
                    spread[slot * TILE + lane, node_of(other)] = 1.0
                    for at in (6,) if tile == 2 else range(3 * tile, 3 * tile + 3):
                        sides[2 * dim + (coords[dim] == 0), :, TILE * at + lane] = 1.0
                        if coords[dim] == 7:
                            small[MASK_AT + 7 * dim + at, :, lane] = 1.0
            slot += 1
    for node in range(NODES):
        count = sum(1 for c in coords_of(node) if c in (0, 7))
        small[MULT_AT + node // TILE, :, node % TILE] = count
    vander = np.zeros((288, NODES))
    for jx in range(6):
        for jy in range(6):
            for jz in range(6):
                for node in range(NODES):
                    a, b, c = coords_of(node)
                    vander[jx * 48 + jy * 8 + jz, node] = (
                        points[a] ** jx * points[b] ** jy * points[c] ** jz / 512.0
                    )
    for k in range(6):
        for a in range(6):
            if a >= k:
                small[k, a, :] = math.comb(a, k)
    shift = np.zeros((3, TILE, TILE))
    for row in range(108):
        for col in range(108):
            jy, jz, ay, az = row // 6 % 6, row % 6, col // 6 % 6, col % 6
            if row // 36 == col // 36 and ay >= jy and az >= jz:
                shift[0, row, col] = (
                    math.comb(ay, jy) * math.comb(az, jz) * BOX_IN_ROOT ** (jy + jz)
                )
                shift[1, row, col] = ay - jy
                shift[2, row, col] = az - jz
    return diff, pick, spread, sides, shift, vander, small, tail


BOX_CELLS = 2 ** ((3 * LMAX - 6) // 3)
FINEST = 1.0 / 2**LMAX
BOX_SIDE = BOX_CELLS * FINEST
BOX_SCALE = 0.5 * BOX_SIDE
BOX_IN_ROOT = BOX_SCALE / 0.5

(
    VEL_IN,
    PICK_IN,
    COUNTS_IN,
    NBR_IN,
    PRESS_IN,
    DIFF_IN,
    VISC_IN,
    SMALL_IN,
    LEVELS_IN,
    KEYS_IN,
    SPREAD_IN,
    SIDES_IN,
    SHIFT_IN,
    VAND_IN,
) = range(14)
QUARTER = LEAVES // 4
HALF_BAND = BAND // 2
ROUNDS = 4
ORDERS = 288
BANDS_AT, LAST_AT, ROWS = 4 * LEAVES, 4 * LEAVES + 6 * BAND, 4 * LEAVES + 8 * BAND


def dot(a, b):
    return jnp.dot(a, b, preferred_element_type=F32)


def dot_nt(a, b):
    return lax.dot_general(a, b, (((1,), (1,)), ((), ())), preferred_element_type=F32)


def split(value):
    high = value.astype(BF16)
    return high, (value - high.astype(F32)).astype(BF16)


def flat_rows(packed, out_ref):
    lane = lax.broadcasted_iota(jnp.int32, (8, TILE), 1)
    sub = lax.broadcasted_iota(jnp.int32, (8, TILE), 0)
    first_tile = (sub < 3) | ((sub == 3) & (lane >= 108))
    valid = jnp.bitwise_and(lane - 36 * sub, TILE - 1) < 36
    turned = {0: packed}
    for by in range(-2, DEG + 1):
        if by:
            turned[by] = pltpu.roll(packed, 36 * by % TILE, 1)
    for comp in range(3):
        rows = turned[-comp]
        for ax in range(1, DEG + 1):
            rows = jnp.where(sub == ax, turned[ax - comp], rows)
        rows = jnp.where(valid & (sub < 6), rows, 0.0)
        near = jnp.sum(jnp.where(first_tile, rows, 0.0), axis=0, keepdims=True)
        far = jnp.sum(jnp.where(first_tile, 0.0, rows), axis=0, keepdims=True)
        out_ref[comp, :, 0:TILE] = near
        out_ref[comp, :, TILE:MOMENTS] = far[:, : MOMENTS - TILE]


def kernel(
    tail,
    vel_hbm,
    pick_hbm,
    counts_hbm,
    nbr_hbm,
    press_hbm,
    diff_hbm,
    visc_hbm,
    small_hbm,
    levels_hbm,
    keys_hbm,
    spread_hbm,
    sides_hbm,
    shift_hbm,
    vand_hbm,
    force_out_ref,
    mass_out_ref,
    box_out_ref,
    root_out_ref,
    field,
    pick,
    counts,
    nbr_in,
    diff,
    visc,
    small,
    levels,
    keys,
    spread,
    sides,
    shift_tab,
    vand,
    tab,
    link_band,
    chip_band,
    grads,
    local,
    picked,
    force,
    mass,
    pos_sq,
    weight,
    force_high,
    force_low,
    x_tables,
    root_yz,
    mcat,
    part,
    recv_box,
    recv_a,
    recv_b,
    sum_b,
    tall,
    flat,
    in_sem,
    out_sem,
    ring_send,
    ring_recv,
    fwd_send,
    fwd_recv,
    link_send,
    link_recv,
    relay_send,
    relay_recv,
    hand_send,
    chip_send,
    chip_recv,
    box_send,
    box_recv,
    a_send,
    a_recv,
    b_send,
    b_recv,
    known,
):
    m = lax.axis_index("morton")
    s = lax.axis_index("sib")
    x_at = lax.div(m, ZC)
    zc_at = lax.rem(m, ZC)
    core = lax.rem(m, CORES)
    above = lax.rem(s + 1, SIBS)
    below = lax.rem(s + SIBS - 1, SIBS)
    m_chip = m + 1 - 2 * core
    m_link = lax.rem(m + MORTONS - 1 + 2 * core, MORTONS)

    linked = (m > 0) & (m < MORTONS - 1)

    def group_a(dx, dy):
        return (lax.rem(x_at + dx, X_SIZE) * ZC + zc_at, lax.rem(s + dy, SIBS))

    def group_b(dz):
        return (x_at * ZC + lax.rem(zc_at + dz, ZC), s)

    a_steps = [(dx, dy) for dx in range(X_SIZE) for dy in range(SIBS) if dx or dy]

    loads = [
        pltpu.make_async_copy(
            vel_hbm.at[0, pl.ds(0, 64)], field.at[0, pl.ds(0, 64)], in_sem.at[VEL_IN]
        ),
        pltpu.make_async_copy(pick_hbm, pick, in_sem.at[PICK_IN]),
        pltpu.make_async_copy(counts_hbm, counts, in_sem.at[COUNTS_IN]),
        pltpu.make_async_copy(nbr_hbm, nbr_in, in_sem.at[NBR_IN]),
        pltpu.make_async_copy(press_hbm, field.at[3], in_sem.at[PRESS_IN]),
        pltpu.make_async_copy(diff_hbm, diff, in_sem.at[DIFF_IN]),
        pltpu.make_async_copy(visc_hbm, visc, in_sem.at[VISC_IN]),
        pltpu.make_async_copy(small_hbm, small, in_sem.at[SMALL_IN]),
        pltpu.make_async_copy(levels_hbm, levels, in_sem.at[LEVELS_IN]),
        pltpu.make_async_copy(keys_hbm, keys, in_sem.at[KEYS_IN]),
        pltpu.make_async_copy(spread_hbm, spread, in_sem.at[SPREAD_IN]),
        pltpu.make_async_copy(sides_hbm, sides, in_sem.at[SIDES_IN]),
        pltpu.make_async_copy(shift_hbm, shift_tab, in_sem.at[SHIFT_IN]),
        pltpu.make_async_copy(vand_hbm, vand, in_sem.at[VAND_IN]),
    ]
    more_velocity = [
        pltpu.make_async_copy(
            vel_hbm.at[k // 2, pl.ds(k % 2 * 64, 64)],
            field.at[k // 2, pl.ds(k % 2 * 64, 64)],
            in_sem.at[VAND_IN + k],
        )
        for k in range(1, 6)
    ]
    for copy in [loads[VEL_IN], loads[PICK_IN]] + more_velocity:
        copy.start()
    for which in (COUNTS_IN, NBR_IN):
        loads[which].start()

    near_groups = [group_a(1, 0), group_a(X_SIZE - 1, 0), group_b(1), group_b(ZC - 1)]
    near = [(m, above), (m, below), (m_link, s)] + near_groups
    barrier = pltpu.get_barrier_semaphore()
    for device in near:
        pl.semaphore_signal(barrier, inc=1, device_id=device, device_id_type=MESH)

    loads[VEL_IN].wait()
    for copy in more_velocity:
        copy.wait()
    loads[PICK_IN].wait()
    for which in range(PRESS_IN, len(loads)):
        loads[which].start()
    lane = lax.broadcasted_iota(jnp.int32, (LEAVES, TILE), 1)
    rest = dot(field[0:3].reshape(3 * LEAVES, NODES), pick[...])
    shared = jnp.zeros((LEAVES, TILE), F32)
    for comp in range(3):
        first = field[comp, :, 0:TILE].astype(F32)
        last = field[comp, :, NODES - TILE : NODES].astype(F32)
        tab[0:LEAVES, TILE * comp : TILE * (comp + 1)] = jnp.where(lane < 64, first, last).astype(BF16)
        rows = rest[LEAVES * comp : LEAVES * (comp + 1)]
        tab[0:LEAVES, TILE * (3 + comp) : TILE * (4 + comp)] = rows[:, 0:TILE].astype(BF16)
        piece = rows[:, TILE : 2 * TILE]
        if comp:
            piece = pltpu.roll(piece, tail * comp, 1)
        shared = shared + piece
    tab[0:LEAVES, TILE * 6 : TILE * 7] = shared.astype(BF16)

    pl.semaphore_wait(barrier, len(near))

    def send(src, dst, send_sem, recv_sem, device):
        return pltpu.make_async_remote_copy(
            src_ref=src,
            dst_ref=dst,
            send_sem=send_sem,
            recv_sem=recv_sem,
            device_id=device,
            device_id_type=MESH,
        )

    def quarters(block, q, count=1):
        return tab.at[pl.ds(LEAVES * block + QUARTER * q, QUARTER * count)]

    def link_rows(b, first=0, rows=BAND):
        return tab.at[pl.ds((LAST_AT if b == 3 else BANDS_AT + BAND * b) + first, rows)]

    def chip_rows(b):
        return tab.at[pl.ds(LAST_AT + BAND if b == 3 else BANDS_AT + BAND * (3 + b), BAND)]

    def to_neighbour(way, k, q, count):
        block, device = ((2, (m, above)), (1, (m, below)))[way]
        return send(
            quarters(0, q, count),
            quarters(block, q, count),
            ring_send.at[way, k],
            ring_recv.at[way, k],
            device,
        )

    ups = [to_neighbour(0, k, *part) for k, part in enumerate(((0, 1), (1, 1), (2, 2)))]
    downs = [to_neighbour(1, k, q, 1) for k, q in enumerate((2, 3, 0, 1))]
    forwards = [
        send(quarters(2, 0), quarters(3, 0), fwd_send.at[0], fwd_recv.at[0], (m, above)),
        send(quarters(1, 2), quarters(3, 2), fwd_send.at[1], fwd_recv.at[1], (m, below)),
        send(quarters(2, 1), quarters(3, 1), fwd_send.at[2], fwd_recv.at[2], (m, above)),
        send(quarters(1, 3), quarters(3, 3), fwd_send.at[3], fwd_recv.at[3], (m, below)),
    ]
    links = [
        send(link_band, link_rows(0), link_send.at[0], link_recv.at[0], (m_link, s)),
        send(link_band, link_rows(2), link_send.at[1], link_recv.at[1], (m_link, above)),
        send(link_band, link_rows(1), link_send.at[2], link_recv.at[2], (m_link, below)),
    ]
    relays = [
        send(
            link_rows(2, 0, HALF_BAND),
            link_rows(3, 0, HALF_BAND),
            relay_send.at[0],
            relay_recv.at[0],
            (m, above),
        ),
        send(
            link_rows(1, HALF_BAND, HALF_BAND),
            link_rows(3, HALF_BAND, HALF_BAND),
            relay_send.at[1],
            relay_recv.at[1],
            (m, below),
        ),
    ]
    def hand_over(k, block, device, first):
        rows = pl.ds(LEAVES * block, BAND)
        part = pl.ds(LEAVES * block + first, HALF_BAND)
        return [
            send(tab.at[rows], link_rows(block), hand_send.at[k], link_recv.at[3 - block], (m_link, s)),
            send(
                tab.at[part],
                link_rows(3, first, HALF_BAND),
                hand_send.at[k + 1],
                relay_recv.at[k // 2],
                (m_link, device),
            ),
        ]

    from_up = hand_over(0, 2, above, 0)
    from_down = hand_over(2, 1, below, HALF_BAND)
    chips = [
        send(chip_band.at[b], chip_rows(b), chip_send.at[b], chip_recv.at[b], (m_chip, s))
        for b in range(4)
    ]
    turn = [0, 1, 3, 2]
    band_row = lax.broadcasted_iota(jnp.int32, (BAND, LEAVES), 0)
    band_col = lax.broadcasted_iota(jnp.int32, (BAND, LEAVES), 1)

    def band(b, last):
        live = counts[m * SIBS + lax.rem(s + turn[b], SIBS)]
        chosen = jnp.where(band_col == band_row + last * (live - BAND), 1.0, 0.0).astype(BF16)
        return dot(chosen, tab[LEAVES * b : LEAVES * (b + 1)]).astype(BF16)

    def send_chip(b):
        chip_band[b] = band(b, 1 - core)
        chips[b].start()

    round_peers = []
    for k in range(ROUNDS):
        peers = [group_a(1, 0), group_a(X_SIZE - 1, 0), (m, above), (m, below)]
        if k < 3:
            peers += [group_b(2**k), group_b(ZC - 2**k)]
        round_peers.append(peers)

    def tell(k):
        for device in round_peers[k]:
            pl.semaphore_signal(known.at[k], inc=1, device_id=device, device_id_type=MESH)

    def hear(k):
        pl.semaphore_wait(known.at[k], len(round_peers[k]))

    ups[0].start()
    downs[0].start()
    ups[1].start()
    downs[1].start()
    tell(0)
    loads[COUNTS_IN].wait()
    link_band[...] = band(0, core)

    @pl.when(linked)
    def _():
        links[0].start()

    @pl.when(jnp.logical_not(linked))
    def _():
        tab[BANDS_AT : BANDS_AT + 3 * BAND, :] = jnp.zeros((3 * BAND, LANES), BF16)
        tab[LAST_AT : LAST_AT + BAND, :] = jnp.zeros((BAND, LANES), BF16)

    loads[NBR_IN].wait()
    nbr = nbr_in[...]
    owner_sib = jnp.bitwise_and(jnp.right_shift(nbr, 7), 3)
    slot = jnp.bitwise_and(nbr, LEAVES - 1)
    step = jnp.right_shift(nbr, 9) - m
    offset = jnp.bitwise_and(owner_sib - s + SIBS, 3)
    block = jnp.where(offset == 2, 3, jnp.where(offset == 3, 2, offset))
    prior = lax.rem(m + MORTONS - 1, MORTONS) * SIBS
    prior_live = jnp.zeros_like(nbr)
    for k in range(SIBS):
        prior_live = jnp.where(owner_sib == k, counts[prior + k], prior_live)
    apart = jnp.where(block == 3, BAND, 3 * BAND)
    halo_row = jnp.where(block == 3, LAST_AT, BANDS_AT + block * BAND) + slot
    row = jnp.where(
        step == 0,
        block * LEAVES + slot,
        jnp.where(
            step == 1,
            halo_row + (1 - core) * apart,
            halo_row + core * apart - (prior_live - BAND),
        ),
    )
    row = jnp.where(nbr < 0, -1, row).astype(F32)
    pos_sq[...] = jnp.zeros_like(pos_sq)
    pos_sq[0:6, :] = row
    pos_sq[...] = pos_sq[...].T

    def gather(first, rows, fresh=False):
        col = lax.broadcasted_iota(jnp.int32, (LEAVES, rows), 1).astype(F32) + float(first)
        for dim in range(3):
            pair = []
            for face in (2 * dim, 2 * dim + 1):
                at = pos_sq[:, face : face + 1]
                pair.append(jnp.where(col == at, 1.0, 0.0))
            chosen = jnp.concatenate(pair, axis=0).astype(BF16)
            width = TILE * (3, 6, 7)[dim]
            got = dot(chosen, tab[first : first + rows, 0:width])
            for tile in range(width // TILE):
                lanes = slice(TILE * tile, TILE * (tile + 1))
                mask = small[MASK_AT + 7 * dim + tile, 0:1, :] > 0.5
                one = jnp.where(mask, got[0:LEAVES, lanes], got[LEAVES:, lanes]).astype(BF16)
                if fresh:
                    picked[dim, :, lanes] = one
                else:
                    picked[dim, :, lanes] += one

    send_chip(0)
    loads[SMALL_IN].wait()
    downs[2].start()
    gather(0, LEAVES, True)
    hear(0)

    @pl.when((core == 1) & linked)
    def _():
        links[1].start()
        links[2].start()

    tell(1)

    loads[PRESS_IN].wait()
    loads[DIFF_IN].wait()
    stacked = field[...].reshape(4 * LEAVES, NODES)
    for dim in range(3):
        grads[dim] = dot(stacked, diff[dim])
        if dim == 0:
            ups[2].start()
            downs[3].start()

    own_live = counts[m * SIBS + s]
    leaf_row = lax.broadcasted_iota(jnp.int32, (LEAVES, NODES), 0)
    live_rows = leaf_row < own_live

    def grad(comp, dim):
        return grads[dim, LEAVES * comp : LEAVES * (comp + 1), :]

    mass[...] = jnp.where(
        live_rows, -(grad(0, 0) + grad(1, 1) + grad(2, 2)) * mass_scale, 0.0
    )
    mass_out = pltpu.make_async_copy(mass, mass_out_ref, out_sem.at[0])
    mass_out.start()

    loads[VISC_IN].wait()
    stress = {}
    for i in range(3):
        for j in range(i, 3):
            stress[i, j] = (visc[...] * (grad(i, j) + grad(j, i))).astype(BF16)
    total = None
    for j in range(3):
        rows = jnp.concatenate([stress[min(i, j), max(i, j)] for i in range(3)], axis=0)
        term = dot(rows, diff[j])
        total = term if total is None else total + term
    mult = jnp.concatenate([small[MULT_AT + t, 0:1, :] for t in range(4)], axis=1)
    for comp in range(3):
        jump = field[comp].astype(F32) * mult
        value = (
            penalty * visc[...] * jump
            - total[LEAVES * comp : LEAVES * (comp + 1)]
            + grad(3, comp)
        ) * out_scale
        local[comp] = jnp.where(live_rows, value, 0.0)
    ups[0].wait_recv()
    forwards[0].start()

    @pl.when((core == 0) & linked)
    def _():
        for copy in from_up:
            copy.start()

    downs[0].wait_recv()
    forwards[1].start()
    ups[1].wait_recv()
    forwards[2].start()
    downs[1].wait_recv()
    forwards[3].start()
    downs[2].wait_recv()

    @pl.when((core == 0) & linked)
    def _():
        for copy in from_down:
            copy.start()
        links[1].wait_recv()
        relays[0].start()
        links[2].wait_recv()
        relays[1].start()

    hear(1)
    tell(2)

    weight[...] = jnp.where(live_rows, (penalty * out_scale) * visc[...], 0.0)
    loads[LEVELS_IN].wait()
    loads[KEYS_IN].wait()
    level = levels[...]
    shift_bits = 3 * (LMAX - level)
    anchor = jnp.left_shift(jnp.right_shift(keys[...], shift_bits), shift_bits)
    span = jnp.left_shift(jnp.ones_like(level), LMAX - level).astype(F32)
    at_box = []
    box_center = []
    for dim, bit0 in enumerate((2, 1, 0)):
        cell = jnp.zeros_like(anchor)
        corner = 0
        for bit in range(LMAX):
            cell = cell + jnp.left_shift(
                jnp.bitwise_and(jnp.right_shift(anchor, 3 * bit + bit0), 1), bit
            )
            up_bit = 3 * bit + bit0 - (3 * LMAX - 6)
            if up_bit >= 0:
                corner = corner + lax.rem(lax.div(m, 2**up_bit), 2) * 2**bit
        center = corner.astype(F32) * FINEST + 0.5 * BOX_SIDE
        box_center.append(center)
        at_box.append(((cell.astype(F32) + 0.5 * span) * FINEST - center) / BOX_SCALE)
    half = 0.5 * span * FINEST / BOX_SCALE
    sub = lax.broadcasted_iota(jnp.int32, (8, TILE), 0)

    def power_rows(value):
        value = jnp.broadcast_to(value, (8, TILE))
        power = jnp.ones((8, TILE), F32)
        rows = power
        for k in range(1, DEG + 1):
            power = power * value
            rows = jnp.where(sub == k, power, rows)
        return rows

    loads[SHIFT_IN].wait()
    half_rows = power_rows(half)
    half_wide = jnp.broadcast_to(half, (8, TILE))
    scales = [half_rows]
    for _ in range(DEG):
        scales.append(scales[-1] * half_wide)

    def x_table(at, size):
        wide = jnp.broadcast_to(size, (8, TILE))
        rows = power_rows(at)
        size_power = jnp.ones((8, TILE), F32)
        tiles = []
        for k in range(DEG + 1):
            turned = rows if k == 0 else pltpu.roll(rows, k, 0)
            tiles.append(small[k] * turned * size_power)
            size_power = size_power * wide
        return split(jnp.concatenate(tiles, axis=1))

    at_root = (at_box[0] * BOX_SCALE + box_center[0] - 0.5) / 0.5
    box_high, box_low = x_table(at_box[0], half)
    root_high, root_low = x_table(at_root, half * BOX_IN_ROOT)
    x_tables[...] = jnp.concatenate([box_high, root_high, box_low, root_low], axis=0)
    moves = shift_tab[0]
    for dim, exponents in ((1, shift_tab[1]), (2, shift_tab[2])):
        by = (box_center[dim] - 0.5) / 0.5
        power = by
        factor = jnp.ones((TILE, TILE), F32)
        for k in range(1, DEG + 1):
            factor = jnp.where(exponents == float(k), power, factor)
            power = power * by
        moves = moves * factor
    move_high, move_low = split(moves)
    root_yz[0] = move_high
    root_yz[1] = move_low
    y_wide = jnp.broadcast_to(at_box[1], (8, TILE))
    z_wide = jnp.broadcast_to(at_box[2], (8, TILE))
    z_coef = []
    z_power = jnp.ones((8, TILE), F32)
    for k in range(DEG + 1):
        z_coef.append(small[k] * z_power)
        z_power = z_power * z_wide

    downs[3].wait_recv()
    send_chip(1)
    ups[2].wait_recv()
    send_chip(2)
    gather(LEAVES, 2 * LEAVES)
    loads[SPREAD_IN].wait()
    hear(2)
    tell(3)
    for copy in chips[:3]:
        copy.wait_recv()

    @pl.when(linked)
    def _():
        links[0].wait_recv()

    @pl.when((core == 1) & linked)
    def _():
        links[1].wait_recv()
        links[2].wait_recv()

    gather(BANDS_AT, 6 * BAND)
    for k in range(4):
        forwards[k].wait_recv()
    send_chip(3)
    gather(3 * LEAVES, LEAVES)
    hear(3)
    loads[SIDES_IN].wait()
    loads[VAND_IN].wait()
    chips[3].wait_recv()

    @pl.when(linked)
    def _():
        for copy in relays:
            copy.wait_recv()

    col = lax.broadcasted_iota(jnp.int32, (LEAVES, 2 * BAND), 1).astype(F32) + float(LAST_AT)
    near_sums = []
    for dim in range(3):
        width = TILE * (3, 6, 7)[dim]
        chosen = [
            jnp.where(col == pos_sq[:, face : face + 1], 1.0, 0.0)
            for face in (2 * dim, 2 * dim + 1)
        ]
        chosen = jnp.concatenate(chosen, axis=1).astype(BF16)
        late = tab[LAST_AT:ROWS, 0:width]
        side = [
            late * jnp.concatenate([sides[2 * dim + k, :, 0:width]] * 4, axis=0)
            for k in range(2)
        ]
        got = dot(chosen, jnp.concatenate(side, axis=0)).astype(BF16)
        near_sums.append(picked[dim, :, 0:width] + got)

    rows = []
    for comp in range(3):
        parts = []
        for dim in range(3):
            for tile in FACE_TILES[dim]:
                at = 6 if tile == 2 else 3 * tile + comp
                value = near_sums[dim][:, TILE * at : TILE * (at + 1)]
                if tile == 2:
                    mine = (lane >= tail * comp) & (lane < tail * (comp + 1))
                    value = jnp.where(mine, value.astype(F32), 0.0).astype(BF16)
                parts.append(value)
        rows.append(jnp.concatenate(parts, axis=1))
    across = dot(jnp.concatenate(rows, axis=0), spread[...])
    for comp in range(3):
        there = across[LEAVES * comp : LEAVES * (comp + 1)]
        value = local[comp] - weight[...] * there
        force[comp] = value
        high, low = split(value)
        force_high[LEAVES * comp : LEAVES * (comp + 1), :] = high
        force_low[LEAVES * comp : LEAVES * (comp + 1), :] = low
    force_out = pltpu.make_async_copy(force, force_out_ref, out_sem.at[1])
    force_out.start()

    by_force = dot_nt(vand[...].reshape(2 * ORDERS, NODES), force_high[...])
    leaf_moments = by_force[0:ORDERS] + by_force[ORDERS:] + dot_nt(vand[0], force_low[...])
    for comp in range(3):
        for jx in range(6):
            columns = []
            for jy in range(6):
                first = jx * 48 + jy * 8
                base = leaf_moments[first : first + 8, TILE * comp : TILE * (comp + 1)] * scales[jy]
                moved = base * z_coef[0]
                for k in range(1, DEG + 1):
                    moved = moved + z_coef[k] * pltpu.roll(base, k, 0)
                columns.append(moved)
            for low in range(1, DEG + 1):
                for at in range(DEG, low - 1, -1):
                    columns[at] = columns[at] + y_wide * columns[at - 1]
            for jy in range(6):
                first = 36 * comp + 6 * jy
                mcat[first : first + 6, TILE * jx : TILE * (jx + 1)] = columns[jy][0:6]
    mcat[108:TILE, :] = jnp.zeros((TILE - 108, 6 * TILE), F32)
    c_high, c_low = split(mcat[...])
    by_parts = dot_nt(x_tables[...], c_high)
    both = by_parts[0:16] + by_parts[16:32] + dot_nt(x_tables[0:16], c_low)
    own_box = both[0:6]

    r_high, r_low = split(both[8:16])
    shifted = (
        dot(r_high, root_yz[0]) + dot(r_low, root_yz[0]) + dot(r_high, root_yz[1])
    )[0:6]

    part[0] = own_box
    part[1] = shifted
    recv_box[s] = own_box
    box_copies = [
        send(
            part.at[0],
            recv_box.at[s],
            box_send.at[k],
            box_recv.at[k],
            (m, lax.rem(s + 1 + k, SIBS)),
        )
        for k in range(SIBS - 1)
    ]
    at_a = x_at * SIBS + s
    z_at = lax.div(zc_at, CORES)
    from_core = []
    for k in range(CORES):
        copies = []
        for n, (dx, dy) in enumerate(([(0, 0)] if k == 0 else []) + a_steps):
            to = (lax.rem(x_at + dx, X_SIZE) * ZC + zc_at + 1 - core, lax.rem(s + dy, SIBS))
            copies.append(
                send(part.at[1], recv_a.at[k, at_a], a_send.at[k, n], a_recv.at[k, n], to)
            )
        from_core.append(copies)
    b_steps = [CORES * k for k in range(1, Z_SIZE)] + [CORES * k + 1 for k in range(Z_SIZE)]
    b_copies = [
        send(
            sum_b,
            recv_b.at[z_at],
            b_send.at[k],
            b_recv.at[k],
            (x_at * ZC + lax.rem(CORES * z_at + 1 + step, ZC), s),
        )
        for k, step in enumerate(b_steps)
    ]
    to_core_1, to_core_0 = b_copies[: Z_SIZE - 1], b_copies[Z_SIZE - 1 :]

    @pl.when(core == 0)
    def _():
        for copy in from_core[0]:
            copy.start()

    @pl.when(core == 1)
    def _():
        recv_a[1, at_a] = shifted
        for copy in from_core[1]:
            copy.start()

    for copy in box_copies:
        copy.start()

    for copy in box_copies:
        copy.wait_recv()
    box = recv_box[0]
    for k in range(1, SIBS):
        box = box + recv_box[k]
    tall[...] = jnp.zeros_like(tall)
    tall[0:6, :] = box
    flat_rows(tall[...], flat.at[0])
    box_out = pltpu.make_async_copy(flat.at[0], box_out_ref, out_sem.at[2])
    box_out.start()

    @pl.when(core == 1)
    def _():
        for copies in from_core:
            for copy in copies:
                copy.wait_recv()
        plane = recv_a[0, 0] + recv_a[1, 0]
        for k in range(1, X_SIZE * SIBS):
            plane = plane + (recv_a[0, k] + recv_a[1, k])
        sum_b[...] = plane
        recv_b[z_at] = plane
        for copy in b_copies:
            copy.start()
        for copy in to_core_1:
            copy.wait_recv()

    @pl.when(core == 0)
    def _():
        for copy in to_core_0:
            copy.wait_recv()

    total = recv_b[0]
    for k in range(1, Z_SIZE):
        total = total + recv_b[k]
    tall[0:6, :] = total
    flat_rows(tall[...], flat.at[1])
    root_out = pltpu.make_async_copy(flat.at[1], root_out_ref, out_sem.at[3])
    root_out.start()

    for copy in ups + downs + forwards + chips + box_copies:
        copy.wait_send()

    @pl.when(linked)
    def _():
        links[0].wait_send()

    @pl.when((core == 0) & linked)
    def _():
        for copy in relays + from_up + from_down:
            copy.wait_send()

    @pl.when((core == 1) & linked)
    def _():
        for copy in links[1:]:
            copy.wait_send()

    @pl.when(core == 0)
    def _():
        for copy in from_core[0]:
            copy.wait_send()

    @pl.when(core == 1)
    def _():
        for copy in from_core[1] + b_copies:
            copy.wait_send()

    mass_out.wait()
    force_out.wait()
    box_out.wait()
    root_out.wait()


def finish(force, mass, box, root, force_out, mass_out, box_out, root_out, sem):
    pairs = [(force.at[k], force_out.at[k]) for k in range(3)]
    pairs += [(mass, mass_out), (box, box_out), (root, root_out)]
    copies = [pltpu.make_async_copy(a, b, sem.at[k]) for k, (a, b) in enumerate(pairs)]
    for copy in copies:
        copy.start()
    for copy in copies:
        copy.wait()


def on_device(velocity, pressure, viscosity, levels, morton_keys, counts, neighbors):
    diff, pick, spread, sides, shift, vander, small, tail = tables()
    as_bf16 = lambda a: jnp.asarray(a.astype(np.float32)).astype(BF16)
    vander32 = vander.astype(np.float32)
    v_high = vander32.astype(jnp.bfloat16)
    v_low = (vander32 - v_high.astype(np.float32)).astype(jnp.bfloat16)
    vand = np.stack([v_high, v_low])
    dma = pltpu.SemaphoreType.DMA
    any_space = pl.BlockSpec(memory_space=pl.ANY)
    hbm = pl.BlockSpec(memory_space=pltpu.HBM)
    results = (
        jax.ShapeDtypeStruct((3, LEAVES, NODES), F32),
        jax.ShapeDtypeStruct((LEAVES, NODES), F32),
        jax.ShapeDtypeStruct((3, 1, MOMENTS), F32),
        jax.ShapeDtypeStruct((3, 1, MOMENTS), F32),
    )
    raw = pl.pallas_call(
        functools.partial(kernel, tail),
        out_shape=tuple(pltpu.VMEM(r.shape, r.dtype) for r in results),
        in_specs=[hbm] * 14,
        out_specs=(any_space,) * 4,
        scratch_shapes=[
            pltpu.VMEM((4, LEAVES, NODES), BF16),
            pltpu.VMEM((NODES, 2 * TILE), BF16),
            pltpu.SMEM((MORTONS * SIBS,), jnp.int32),
            pltpu.VMEM((6, LEAVES), jnp.int32),
            pltpu.VMEM((3, NODES, NODES), BF16),
            pltpu.VMEM((LEAVES, NODES), F32),
            pltpu.VMEM((MASK_AT + 21, 8, TILE), F32),
            pltpu.VMEM((1, LEAVES), jnp.int32),
            pltpu.VMEM((1, LEAVES), jnp.int32),
            pltpu.VMEM((6 * TILE, NODES), BF16),
            pltpu.VMEM((6, 16, LANES), BF16),
            pltpu.VMEM((3, TILE, TILE), F32),
            pltpu.VMEM((2, ORDERS, NODES), BF16),
            pltpu.VMEM((ROWS, LANES), BF16),
            pltpu.VMEM((BAND, LANES), BF16),
            pltpu.VMEM((4, BAND, LANES), BF16),
            pltpu.VMEM((3, 4 * LEAVES, NODES), F32),
            pltpu.VMEM((3, LEAVES, NODES), F32),
            pltpu.VMEM((3, LEAVES, LANES), BF16),
            pltpu.VMEM((3, LEAVES, NODES), F32),
            pltpu.VMEM((LEAVES, NODES), F32),
            pltpu.VMEM((LEAVES, LEAVES), F32),
            pltpu.VMEM((LEAVES, NODES), F32),
            pltpu.VMEM((3 * LEAVES, NODES), BF16),
            pltpu.VMEM((3 * LEAVES, NODES), BF16),
            pltpu.VMEM((32, 6 * TILE), BF16),
            pltpu.VMEM((2, TILE, TILE), BF16),
            pltpu.VMEM((TILE, 6 * TILE), F32),
            pltpu.VMEM((2, 6, TILE), F32),
            pltpu.VMEM((SIBS, 6, TILE), F32),
            pltpu.VMEM((CORES, X_SIZE * SIBS, 6, TILE), F32),
            pltpu.VMEM((Z_SIZE, 6, TILE), F32),
            pltpu.VMEM((6, TILE), F32),
            pltpu.VMEM((8, TILE), F32),
            pltpu.VMEM((2, 3, 1, MOMENTS), F32),
            dma((19,)),
            dma((4,)),
            dma((2, 4)),
            dma((2, 4)),
            dma((4,)),
            dma((4,)),
            dma((3,)),
            dma((3,)),
            dma((2,)),
            dma((2,)),
            dma((4,)),
            dma((4,)),
            dma((4,)),
            dma((3,)),
            dma((3,)),
            dma((CORES, 16)),
            dma((CORES, 16)),
            dma((15,)),
            dma((15,)),
            pltpu.SemaphoreType.REGULAR((ROUNDS,)),
        ],
        compiler_params=pltpu.CompilerParams(
            collective_id=0, has_side_effects=True, vmem_limit_bytes=60 * 2**20
        ),
    )(
        velocity.transpose(1, 0, 2),
        as_bf16(pick),
        counts,
        neighbors.T,
        pressure,
        as_bf16(diff),
        viscosity,
        jnp.asarray(small.astype(np.float32)),
        levels.reshape(1, LEAVES),
        morton_keys.reshape(1, LEAVES),
        as_bf16(spread),
        as_bf16(sides),
        jnp.asarray(shift.astype(np.float32)),
        jnp.asarray(vand),
    )
    force, mass, box, root = pl.pallas_call(
        finish,
        out_shape=results,
        in_specs=[any_space] * 4,
        out_specs=(any_space,) * 4,
        scratch_shapes=[dma((6,))],
    )(*[pltpu.with_memory_space_constraint(r, pltpu.VMEM) for r in raw])
    return (
        force.transpose(1, 0, 2),
        mass,
        box.transpose(1, 0, 2),
        root.transpose(1, 0, 2),
    )


def solution(mesh):
    in_specs = (
        P(("morton", "sib"), None, None),
        P(("morton", "sib"), None),
        P(("morton", "sib"), None),
        P(("morton", "sib")),
        P(("morton", "sib")),
        P(),
        P(("morton", "sib"), None),
    )
    out_specs = (
        P(("morton", "sib"), None, None),
        P(("morton", "sib"), None),
        P("morton", None, None),
        P("morton", None, None),
    )
    return jax.shard_map(
        on_device, mesh=mesh, in_specs=in_specs, out_specs=out_specs, check_vma=False
    )
```

```python
import functools
import math

import jax
import jax.numpy as jnp
import numpy as np
from jax import lax
from jax.experimental import pallas as pl
from jax.experimental.pallas import tpu as pltpu
from jax.sharding import PartitionSpec as P

DEG = 5
LMAX = 7
MOMENTS = 216
LEAVES = 128
NODES = 512
LANES = 896
BAND = 32
TILE = 128
MESH = pl.DeviceIdType.MESH
F32 = jnp.float32
BF16 = jnp.bfloat16

penalty = 256.0
out_scale = 1.0 / 1024.0
mass_scale = 1.0 / 32.0

X_SIZE, Z_SIZE, CORES, SIBS = 4, 8, 2, 4
ZC = Z_SIZE * CORES
MORTONS = X_SIZE * ZC


def cheb():
    points = -np.cos(np.pi * np.arange(8) / 7.0)
    weights = np.array([(-1.0) ** k for k in range(8)])
    weights[0] *= 0.5
    weights[7] *= 0.5
    derivative = np.zeros((8, 8))
    for row in range(8):
        for col in range(8):
            if row != col:
                derivative[row, col] = weights[col] / weights[row] / (points[row] - points[col])
        derivative[row, row] = -np.sum(derivative[row])
    return points, derivative


def node_of(coords):
    return 64 * coords[0] + 8 * coords[1] + coords[2]


def coords_of(node):
    return [node // 64, node // 8 % 8, node % 8]


def surface_lists():
    x_nodes = [node_of([7 * side, b, c]) for side in range(2) for b in range(8) for c in range(8)]
    inner = [n for n in range(NODES) if coords_of(n)[0] not in (0, 7)]
    on_y = [n for n in inner if coords_of(n)[1] in (0, 7)]
    only_z = [n for n in inner if n not in on_y and coords_of(n)[2] in (0, 7)]
    return x_nodes, on_y + only_z


FACE_TILES = ((0,), (0, 1), (0, 1, 2))
MULT_AT, MASK_AT = 6, 10


def tables():
    points, derivative = cheb()
    eye = np.eye(8)
    directional = [
        np.kron(np.kron(derivative, eye), eye),
        np.kron(np.kron(eye, derivative), eye),
        np.kron(np.kron(eye, eye), derivative),
    ]
    diff = np.stack([m.T for m in directional])
    x_nodes, rest = surface_lists()
    tail = len(rest) - TILE
    pick = np.zeros((NODES, 2 * TILE))
    for k, node in enumerate(rest):
        pick[node, k] = 1.0
    tiles = [list(x_nodes), list(rest[:TILE]), [-1] * TILE]
    for comp in range(3):
        for k in range(tail):
            tiles[2][tail * comp + k] = rest[TILE + k]
    spread = np.zeros((6 * TILE, NODES))
    small = np.zeros((MASK_AT + 21, 8, TILE))
    sides = np.zeros((6, 16, LANES))
    slot = 0
    for dim in range(3):
        for tile in FACE_TILES[dim]:
            for lane, node in enumerate(tiles[tile]):
                if node < 0:
                    continue
                coords = coords_of(node)
                if coords[dim] in (0, 7):
                    other = list(coords)
                    other[dim] = 7 - coords[dim]
                    spread[slot * TILE + lane, node_of(other)] = 1.0
                    for at in (6,) if tile == 2 else range(3 * tile, 3 * tile + 3):
                        sides[2 * dim + (coords[dim] == 0), :, TILE * at + lane] = 1.0
                        if coords[dim] == 7:
                            small[MASK_AT + 7 * dim + at, :, lane] = 1.0
            slot += 1
    for node in range(NODES):
        count = sum(1 for c in coords_of(node) if c in (0, 7))
        small[MULT_AT + node // TILE, :, node % TILE] = count
    vander = np.zeros((288, NODES))
    for jx in range(6):
        for jy in range(6):
            for jz in range(6):
                for node in range(NODES):
                    a, b, c = coords_of(node)
                    vander[jx * 48 + jy * 8 + jz, node] = (
                        points[a] ** jx * points[b] ** jy * points[c] ** jz / 512.0
                    )
    for k in range(6):
        for a in range(6):
            if a >= k:
                small[k, a, :] = math.comb(a, k)
    shift = np.zeros((3, TILE, TILE))
    for row in range(108):
        for col in range(108):
            jy, jz, ay, az = row // 6 % 6, row % 6, col // 6 % 6, col % 6
            if row // 36 == col // 36 and ay >= jy and az >= jz:
                shift[0, row, col] = (
                    math.comb(ay, jy) * math.comb(az, jz) * BOX_IN_ROOT ** (jy + jz)
                )
                shift[1, row, col] = ay - jy
                shift[2, row, col] = az - jz
    return diff, pick, spread, sides, shift, vander, small, tail


BOX_CELLS = 2 ** ((3 * LMAX - 6) // 3)
FINEST = 1.0 / 2**LMAX
BOX_SIDE = BOX_CELLS * FINEST
BOX_SCALE = 0.5 * BOX_SIDE
BOX_IN_ROOT = BOX_SCALE / 0.5

(
    VEL_IN,
    PICK_IN,
    COUNTS_IN,
    NBR_IN,
    PRESS_IN,
    DIFF_IN,
    VISC_IN,
    SMALL_IN,
    LEVELS_IN,
    KEYS_IN,
    SPREAD_IN,
    SIDES_IN,
    SHIFT_IN,
    VAND_IN,
) = range(14)
QUARTER = LEAVES // 4
HALF_BAND = BAND // 2
ROUNDS = 4
ORDERS = 288
BANDS_AT, LAST_AT, ROWS = 4 * LEAVES, 4 * LEAVES + 6 * BAND, 4 * LEAVES + 8 * BAND


def dot(a, b):
    return jnp.dot(a, b, preferred_element_type=F32)


def dot_nt(a, b):
    return lax.dot_general(a, b, (((1,), (1,)), ((), ())), preferred_element_type=F32)


def split(value):
    high = value.astype(BF16)
    return high, (value - high.astype(F32)).astype(BF16)


def flat_rows(packed, out_ref):
    lane = lax.broadcasted_iota(jnp.int32, (8, TILE), 1)
    sub = lax.broadcasted_iota(jnp.int32, (8, TILE), 0)
    first_tile = (sub < 3) | ((sub == 3) & (lane >= 108))
    valid = jnp.bitwise_and(lane - 36 * sub, TILE - 1) < 36
    turned = {0: packed}
    for by in range(-2, DEG + 1):
        if by:
            turned[by] = pltpu.roll(packed, 36 * by % TILE, 1)
    for comp in range(3):
        rows = turned[-comp]
        for ax in range(1, DEG + 1):
            rows = jnp.where(sub == ax, turned[ax - comp], rows)
        rows = jnp.where(valid & (sub < 6), rows, 0.0)
        near = jnp.sum(jnp.where(first_tile, rows, 0.0), axis=0, keepdims=True)
        far = jnp.sum(jnp.where(first_tile, 0.0, rows), axis=0, keepdims=True)
        out_ref[comp, :, 0:TILE] = near
        out_ref[comp, :, TILE:MOMENTS] = far[:, : MOMENTS - TILE]


def kernel(
    tail,
    vel_hbm,
    pick_hbm,
    counts_hbm,
    nbr_hbm,
    press_hbm,
    diff_hbm,
    visc_hbm,
    small_hbm,
    levels_hbm,
    keys_hbm,
    spread_hbm,
    sides_hbm,
    shift_hbm,
    vand_hbm,
    force_out_ref,
    mass_out_ref,
    box_out_ref,
    root_out_ref,
    field,
    pick,
    counts,
    nbr_in,
    diff,
    visc,
    small,
    levels,
    keys,
    spread,
    sides,
    shift_tab,
    vand,
    tab,
    link_band,
    chip_band,
    grads,
    local,
    picked,
    force,
    mass,
    pos_sq,
    weight,
    force_high,
    force_low,
    x_tables,
    root_yz,
    mcat,
    part,
    recv_box,
    recv_a,
    recv_b,
    sum_b,
    tall,
    flat,
    in_sem,
    out_sem,
    ring_send,
    ring_recv,
    fwd_send,
    fwd_recv,
    link_send,
    link_recv,
    relay_send,
    relay_recv,
    hand_send,
    chip_send,
    chip_recv,
    box_send,
    box_recv,
    a_send,
    a_recv,
    b_send,
    b_recv,
    known,
):
    m = lax.axis_index("morton")
    s = lax.axis_index("sib")
    x_at = lax.div(m, ZC)
    zc_at = lax.rem(m, ZC)
    core = lax.rem(m, CORES)
    above = lax.rem(s + 1, SIBS)
    below = lax.rem(s + SIBS - 1, SIBS)
    m_chip = m + 1 - 2 * core
    m_link = lax.rem(m + MORTONS - 1 + 2 * core, MORTONS)

    linked = (m > 0) & (m < MORTONS - 1)

    def group_a(dx, dy):
        return (lax.rem(x_at + dx, X_SIZE) * ZC + zc_at, lax.rem(s + dy, SIBS))

    def group_b(dz):
        return (x_at * ZC + lax.rem(zc_at + dz, ZC), s)

    a_steps = [(dx, dy) for dx in range(X_SIZE) for dy in range(SIBS) if dx or dy]

    loads = [
        pltpu.make_async_copy(
            vel_hbm.at[0, pl.ds(0, 64)], field.at[0, pl.ds(0, 64)], in_sem.at[VEL_IN]
        ),
        pltpu.make_async_copy(pick_hbm, pick, in_sem.at[PICK_IN]),
        pltpu.make_async_copy(counts_hbm, counts, in_sem.at[COUNTS_IN]),
        pltpu.make_async_copy(nbr_hbm, nbr_in, in_sem.at[NBR_IN]),
        pltpu.make_async_copy(press_hbm, field.at[3], in_sem.at[PRESS_IN]),
        pltpu.make_async_copy(diff_hbm, diff, in_sem.at[DIFF_IN]),
        pltpu.make_async_copy(visc_hbm, visc, in_sem.at[VISC_IN]),
        pltpu.make_async_copy(small_hbm, small, in_sem.at[SMALL_IN]),
        pltpu.make_async_copy(levels_hbm, levels, in_sem.at[LEVELS_IN]),
        pltpu.make_async_copy(keys_hbm, keys, in_sem.at[KEYS_IN]),
        pltpu.make_async_copy(spread_hbm, spread, in_sem.at[SPREAD_IN]),
        pltpu.make_async_copy(sides_hbm, sides, in_sem.at[SIDES_IN]),
        pltpu.make_async_copy(shift_hbm, shift_tab, in_sem.at[SHIFT_IN]),
        pltpu.make_async_copy(vand_hbm, vand, in_sem.at[VAND_IN]),
    ]
    more_velocity = [
        pltpu.make_async_copy(
            vel_hbm.at[k // 2, pl.ds(k % 2 * 64, 64)],
            field.at[k // 2, pl.ds(k % 2 * 64, 64)],
            in_sem.at[VAND_IN + k],
        )
        for k in range(1, 6)
    ]
    for copy in [loads[VEL_IN], loads[PICK_IN]] + more_velocity:
        copy.start()
    for which in (COUNTS_IN, NBR_IN):
        loads[which].start()

    near_groups = [group_a(1, 0), group_a(X_SIZE - 1, 0), group_b(1), group_b(ZC - 1)]
    near = [(m, above), (m, below), (m_link, s)] + near_groups
    barrier = pltpu.get_barrier_semaphore()
    for device in near:
        pl.semaphore_signal(barrier, inc=1, device_id=device, device_id_type=MESH)

    loads[VEL_IN].wait()
    for copy in more_velocity:
        copy.wait()
    loads[PICK_IN].wait()
    for which in range(PRESS_IN, len(loads)):
        loads[which].start()
    lane = lax.broadcasted_iota(jnp.int32, (LEAVES, TILE), 1)
    rest = dot(field[0:3].reshape(3 * LEAVES, NODES), pick[...])
    shared = jnp.zeros((LEAVES, TILE), F32)
    for comp in range(3):
        first = field[comp, :, 0:TILE].astype(F32)
        last = field[comp, :, NODES - TILE : NODES].astype(F32)
        tab[0:LEAVES, TILE * comp : TILE * (comp + 1)] = jnp.where(lane < 64, first, last).astype(BF16)
        rows = rest[LEAVES * comp : LEAVES * (comp + 1)]
        tab[0:LEAVES, TILE * (3 + comp) : TILE * (4 + comp)] = rows[:, 0:TILE].astype(BF16)
        piece = rows[:, TILE : 2 * TILE]
        if comp:
            piece = pltpu.roll(piece, tail * comp, 1)
        shared = shared + piece
    tab[0:LEAVES, TILE * 6 : TILE * 7] = shared.astype(BF16)

    pl.semaphore_wait(barrier, len(near))

    def send(src, dst, send_sem, recv_sem, device):
        return pltpu.make_async_remote_copy(
            src_ref=src,
            dst_ref=dst,
            send_sem=send_sem,
            recv_sem=recv_sem,
            device_id=device,
            device_id_type=MESH,
        )

    def quarters(block, q, count=1):
        return tab.at[pl.ds(LEAVES * block + QUARTER * q, QUARTER * count)]

    def link_rows(b, first=0, rows=BAND):
        return tab.at[pl.ds((LAST_AT if b == 3 else BANDS_AT + BAND * b) + first, rows)]

    def chip_rows(b):
        return tab.at[pl.ds(LAST_AT + BAND if b == 3 else BANDS_AT + BAND * (3 + b), BAND)]

    def to_neighbour(way, k, q, count):
        block, device = ((2, (m, above)), (1, (m, below)))[way]
        return send(
            quarters(0, q, count),
            quarters(block, q, count),
            ring_send.at[way, k],
            ring_recv.at[way, k],
            device,
        )

    ups = [to_neighbour(0, k, *part) for k, part in enumerate(((0, 1), (1, 1), (2, 2)))]
    downs = [to_neighbour(1, k, q, 1) for k, q in enumerate((2, 3, 0, 1))]
    forwards = [
        send(quarters(2, 0), quarters(3, 0), fwd_send.at[0], fwd_recv.at[0], (m, above)),
        send(quarters(1, 2), quarters(3, 2), fwd_send.at[1], fwd_recv.at[1], (m, below)),
        send(quarters(2, 1), quarters(3, 1), fwd_send.at[2], fwd_recv.at[2], (m, above)),
        send(quarters(1, 3), quarters(3, 3), fwd_send.at[3], fwd_recv.at[3], (m, below)),
    ]
    links = [
        send(link_band, link_rows(0), link_send.at[0], link_recv.at[0], (m_link, s)),
        send(link_band, link_rows(2), link_send.at[1], link_recv.at[1], (m_link, above)),
        send(link_band, link_rows(1), link_send.at[2], link_recv.at[2], (m_link, below)),
    ]
    relays = [
        send(
            link_rows(2, 0, HALF_BAND),
            link_rows(3, 0, HALF_BAND),
            relay_send.at[0],
            relay_recv.at[0],
            (m, above),
        ),
        send(
            link_rows(1, HALF_BAND, HALF_BAND),
            link_rows(3, HALF_BAND, HALF_BAND),
            relay_send.at[1],
            relay_recv.at[1],
            (m, below),
        ),
    ]
    def hand_over(k, block, device, first):
        rows = pl.ds(LEAVES * block, BAND)
        part = pl.ds(LEAVES * block + first, HALF_BAND)
        return [
            send(tab.at[rows], link_rows(block), hand_send.at[k], link_recv.at[3 - block], (m_link, s)),
            send(
                tab.at[part],
                link_rows(3, first, HALF_BAND),
                hand_send.at[k + 1],
                relay_recv.at[k // 2],
                (m_link, device),
            ),
        ]

    from_up = hand_over(0, 2, above, 0)
    from_down = hand_over(2, 1, below, HALF_BAND)
    chips = [
        send(chip_band.at[b], chip_rows(b), chip_send.at[b], chip_recv.at[b], (m_chip, s))
        for b in range(4)
    ]
    turn = [0, 1, 3, 2]
    band_row = lax.broadcasted_iota(jnp.int32, (BAND, LEAVES), 0)
    band_col = lax.broadcasted_iota(jnp.int32, (BAND, LEAVES), 1)

    def band(b, last):
        live = counts[m * SIBS + lax.rem(s + turn[b], SIBS)]
        chosen = jnp.where(band_col == band_row + last * (live - BAND), 1.0, 0.0).astype(BF16)
        return dot(chosen, tab[LEAVES * b : LEAVES * (b + 1)]).astype(BF16)

    def send_chip(b):
        chip_band[b] = band(b, 1 - core)
        chips[b].start()

    round_peers = []
    for k in range(ROUNDS):
        peers = [group_a(1, 0), group_a(X_SIZE - 1, 0), (m, above), (m, below)]
        if k < 3:
            peers += [group_b(2**k), group_b(ZC - 2**k)]
        round_peers.append(peers)

    def tell(k):
        for device in round_peers[k]:
            pl.semaphore_signal(known.at[k], inc=1, device_id=device, device_id_type=MESH)

    def hear(k):
        pl.semaphore_wait(known.at[k], len(round_peers[k]))

    ups[0].start()
    downs[0].start()
    ups[1].start()
    downs[1].start()
    tell(0)
    loads[COUNTS_IN].wait()
    link_band[...] = band(0, core)

    @pl.when(linked)
    def _():
        links[0].start()

    @pl.when(jnp.logical_not(linked))
    def _():
        tab[BANDS_AT : BANDS_AT + 3 * BAND, :] = jnp.zeros((3 * BAND, LANES), BF16)
        tab[LAST_AT : LAST_AT + BAND, :] = jnp.zeros((BAND, LANES), BF16)

    loads[NBR_IN].wait()
    nbr = nbr_in[...]
    owner_sib = jnp.bitwise_and(jnp.right_shift(nbr, 7), 3)
    slot = jnp.bitwise_and(nbr, LEAVES - 1)
    step = jnp.right_shift(nbr, 9) - m
    offset = jnp.bitwise_and(owner_sib - s + SIBS, 3)
    block = jnp.where(offset == 2, 3, jnp.where(offset == 3, 2, offset))
    prior = lax.rem(m + MORTONS - 1, MORTONS) * SIBS
    prior_live = jnp.zeros_like(nbr)
    for k in range(SIBS):
        prior_live = jnp.where(owner_sib == k, counts[prior + k], prior_live)
    apart = jnp.where(block == 3, BAND, 3 * BAND)
    halo_row = jnp.where(block == 3, LAST_AT, BANDS_AT + block * BAND) + slot
    row = jnp.where(
        step == 0,
        block * LEAVES + slot,
        jnp.where(
            step == 1,
            halo_row + (1 - core) * apart,
            halo_row + core * apart - (prior_live - BAND),
        ),
    )
    row = jnp.where(nbr < 0, -1, row).astype(F32)
    pos_sq[...] = jnp.zeros_like(pos_sq)
    pos_sq[0:6, :] = row
    pos_sq[...] = pos_sq[...].T

    def gather(first, rows, fresh=False):
        col = lax.broadcasted_iota(jnp.int32, (LEAVES, rows), 1).astype(F32) + float(first)
        for dim in range(3):
            pair = []
            for face in (2 * dim, 2 * dim + 1):
                at = pos_sq[:, face : face + 1]
                pair.append(jnp.where(col == at, 1.0, 0.0))
            chosen = jnp.concatenate(pair, axis=0).astype(BF16)
            width = TILE * (3, 6, 7)[dim]
            got = dot(chosen, tab[first : first + rows, 0:width])
            for tile in range(width // TILE):
                lanes = slice(TILE * tile, TILE * (tile + 1))
                mask = small[MASK_AT + 7 * dim + tile, 0:1, :] > 0.5
                one = jnp.where(mask, got[0:LEAVES, lanes], got[LEAVES:, lanes]).astype(BF16)
                if fresh:
                    picked[dim, :, lanes] = one
                else:
                    picked[dim, :, lanes] += one

    send_chip(0)
    loads[SMALL_IN].wait()
    gather(0, LEAVES, True)
    hear(0)
    downs[2].start()

    @pl.when((core == 1) & linked)
    def _():
        links[1].start()
        links[2].start()

    tell(1)

    loads[PRESS_IN].wait()
    loads[DIFF_IN].wait()
    stacked = field[...].reshape(4 * LEAVES, NODES)
    for dim in range(3):
        grads[dim] = dot(stacked, diff[dim])
        if dim == 1:
            ups[2].start()
            downs[3].start()

    own_live = counts[m * SIBS + s]
    leaf_row = lax.broadcasted_iota(jnp.int32, (LEAVES, NODES), 0)
    live_rows = leaf_row < own_live

    def grad(comp, dim):
        return grads[dim, LEAVES * comp : LEAVES * (comp + 1), :]

    mass[...] = jnp.where(
        live_rows, -(grad(0, 0) + grad(1, 1) + grad(2, 2)) * mass_scale, 0.0
    )
    mass_out = pltpu.make_async_copy(mass, mass_out_ref, out_sem.at[0])
    mass_out.start()

    loads[VISC_IN].wait()
    stress = {}
    for i in range(3):
        for j in range(i, 3):
            stress[i, j] = (visc[...] * (grad(i, j) + grad(j, i))).astype(BF16)
    total = None
    for j in range(3):
        rows = jnp.concatenate([stress[min(i, j), max(i, j)] for i in range(3)], axis=0)
        term = dot(rows, diff[j])
        total = term if total is None else total + term
    mult = jnp.concatenate([small[MULT_AT + t, 0:1, :] for t in range(4)], axis=1)
    for comp in range(3):
        jump = field[comp].astype(F32) * mult
        value = (
            penalty * visc[...] * jump
            - total[LEAVES * comp : LEAVES * (comp + 1)]
            + grad(3, comp)
        ) * out_scale
        local[comp] = jnp.where(live_rows, value, 0.0)
    ups[0].wait_recv()
    forwards[0].start()

    @pl.when((core == 0) & linked)
    def _():
        for copy in from_up:
            copy.start()

    downs[0].wait_recv()
    forwards[1].start()
    ups[1].wait_recv()
    forwards[2].start()
    downs[1].wait_recv()
    forwards[3].start()
    downs[2].wait_recv()

    @pl.when((core == 0) & linked)
    def _():
        for copy in from_down:
            copy.start()
        links[1].wait_recv()
        relays[0].start()
        links[2].wait_recv()
        relays[1].start()

    hear(1)
    tell(2)

    weight[...] = jnp.where(live_rows, (penalty * out_scale) * visc[...], 0.0)
    loads[LEVELS_IN].wait()
    loads[KEYS_IN].wait()
    level = levels[...]
    shift_bits = 3 * (LMAX - level)
    anchor = jnp.left_shift(jnp.right_shift(keys[...], shift_bits), shift_bits)
    span = jnp.left_shift(jnp.ones_like(level), LMAX - level).astype(F32)
    at_box = []
    box_center = []
    for dim, bit0 in enumerate((2, 1, 0)):
        cell = jnp.zeros_like(anchor)
        corner = 0
        for bit in range(LMAX):
            cell = cell + jnp.left_shift(
                jnp.bitwise_and(jnp.right_shift(anchor, 3 * bit + bit0), 1), bit
            )
            up_bit = 3 * bit + bit0 - (3 * LMAX - 6)
            if up_bit >= 0:
                corner = corner + lax.rem(lax.div(m, 2**up_bit), 2) * 2**bit
        center = corner.astype(F32) * FINEST + 0.5 * BOX_SIDE
        box_center.append(center)
        at_box.append(((cell.astype(F32) + 0.5 * span) * FINEST - center) / BOX_SCALE)
    half = 0.5 * span * FINEST / BOX_SCALE
    sub = lax.broadcasted_iota(jnp.int32, (8, TILE), 0)

    def power_rows(value):
        value = jnp.broadcast_to(value, (8, TILE))
        power = jnp.ones((8, TILE), F32)
        rows = power
        for k in range(1, DEG + 1):
            power = power * value
            rows = jnp.where(sub == k, power, rows)
        return rows

    loads[SHIFT_IN].wait()
    half_rows = power_rows(half)
    half_wide = jnp.broadcast_to(half, (8, TILE))
    scales = [half_rows]
    for _ in range(DEG):
        scales.append(scales[-1] * half_wide)

    def x_table(at, size):
        wide = jnp.broadcast_to(size, (8, TILE))
        rows = power_rows(at)
        size_power = jnp.ones((8, TILE), F32)
        tiles = []
        for k in range(DEG + 1):
            turned = rows if k == 0 else pltpu.roll(rows, k, 0)
            tiles.append(small[k] * turned * size_power)
            size_power = size_power * wide
        return split(jnp.concatenate(tiles, axis=1))

    at_root = (at_box[0] * BOX_SCALE + box_center[0] - 0.5) / 0.5
    box_high, box_low = x_table(at_box[0], half)
    root_high, root_low = x_table(at_root, half * BOX_IN_ROOT)
    x_tables[...] = jnp.concatenate([box_high, root_high, box_low, root_low], axis=0)
    moves = shift_tab[0]
    for dim, exponents in ((1, shift_tab[1]), (2, shift_tab[2])):
        by = (box_center[dim] - 0.5) / 0.5
        power = by
        factor = jnp.ones((TILE, TILE), F32)
        for k in range(1, DEG + 1):
            factor = jnp.where(exponents == float(k), power, factor)
            power = power * by
        moves = moves * factor
    move_high, move_low = split(moves)
    root_yz[0] = move_high
    root_yz[1] = move_low
    y_wide = jnp.broadcast_to(at_box[1], (8, TILE))
    z_wide = jnp.broadcast_to(at_box[2], (8, TILE))
    z_coef = []
    z_power = jnp.ones((8, TILE), F32)
    for k in range(DEG + 1):
        z_coef.append(small[k] * z_power)
        z_power = z_power * z_wide

    downs[3].wait_recv()
    send_chip(1)
    ups[2].wait_recv()
    send_chip(2)
    gather(LEAVES, 2 * LEAVES)
    loads[SPREAD_IN].wait()
    hear(2)
    tell(3)
    for copy in chips[:3]:
        copy.wait_recv()

    @pl.when(linked)
    def _():
        links[0].wait_recv()

    @pl.when((core == 1) & linked)
    def _():
        links[1].wait_recv()
        links[2].wait_recv()

    gather(BANDS_AT, 6 * BAND)
    first_quarter = send(
        tab.at[pl.ds(3 * LEAVES, BAND)],
        chip_rows(3),
        chip_send.at[3],
        chip_recv.at[3],
        (m_chip, s),
    )
    forwards[0].wait_recv()

    @pl.when(core == 1)
    def _():
        first_quarter.start()

    for k in range(1, 4):
        forwards[k].wait_recv()

    @pl.when(core == 0)
    def _():
        send_chip(3)

    gather(3 * LEAVES, LEAVES)
    hear(3)
    loads[SIDES_IN].wait()
    loads[VAND_IN].wait()
    chips[3].wait_recv()

    @pl.when(linked)
    def _():
        for copy in relays:
            copy.wait_recv()

    col = lax.broadcasted_iota(jnp.int32, (LEAVES, 2 * BAND), 1).astype(F32) + float(LAST_AT)
    near_sums = []
    for dim in range(3):
        width = TILE * (3, 6, 7)[dim]
        chosen = [
            jnp.where(col == pos_sq[:, face : face + 1], 1.0, 0.0)
            for face in (2 * dim, 2 * dim + 1)
        ]
        chosen = jnp.concatenate(chosen, axis=1).astype(BF16)
        late = tab[LAST_AT:ROWS, 0:width]
        side = [
            late * jnp.concatenate([sides[2 * dim + k, :, 0:width]] * 4, axis=0)
            for k in range(2)
        ]
        got = dot(chosen, jnp.concatenate(side, axis=0)).astype(BF16)
        near_sums.append(picked[dim, :, 0:width] + got)

    rows = []
    for comp in range(3):
        parts = []
        for dim in range(3):
            for tile in FACE_TILES[dim]:
                at = 6 if tile == 2 else 3 * tile + comp
                value = near_sums[dim][:, TILE * at : TILE * (at + 1)]
                if tile == 2:
                    mine = (lane >= tail * comp) & (lane < tail * (comp + 1))
                    value = jnp.where(mine, value.astype(F32), 0.0).astype(BF16)
                parts.append(value)
        rows.append(jnp.concatenate(parts, axis=1))
    across = dot(jnp.concatenate(rows, axis=0), spread[...])
    for comp in range(3):
        there = across[LEAVES * comp : LEAVES * (comp + 1)]
        value = local[comp] - weight[...] * there
        force[comp] = value
        high, low = split(value)
        force_high[LEAVES * comp : LEAVES * (comp + 1), :] = high
        force_low[LEAVES * comp : LEAVES * (comp + 1), :] = low
    force_out = pltpu.make_async_copy(force, force_out_ref, out_sem.at[1])
    force_out.start()

    by_force = dot_nt(vand[...].reshape(2 * ORDERS, NODES), force_high[...])
    leaf_moments = by_force[0:ORDERS] + by_force[ORDERS:] + dot_nt(vand[0], force_low[...])
    for comp in range(3):
        for jx in range(6):
            columns = []
            for jy in range(6):
                first = jx * 48 + jy * 8
                base = leaf_moments[first : first + 8, TILE * comp : TILE * (comp + 1)] * scales[jy]
                moved = base * z_coef[0]
                for k in range(1, DEG + 1):
                    moved = moved + z_coef[k] * pltpu.roll(base, k, 0)
                columns.append(moved)
            for low in range(1, DEG + 1):
                for at in range(DEG, low - 1, -1):
                    columns[at] = columns[at] + y_wide * columns[at - 1]
            for jy in range(6):
                first = 36 * comp + 6 * jy
                mcat[first : first + 6, TILE * jx : TILE * (jx + 1)] = columns[jy][0:6]
    mcat[108:TILE, :] = jnp.zeros((TILE - 108, 6 * TILE), F32)
    c_high, c_low = split(mcat[...])
    by_parts = dot_nt(x_tables[...], c_high)
    both = by_parts[0:16] + by_parts[16:32] + dot_nt(x_tables[0:16], c_low)
    own_box = both[0:6]

    r_high, r_low = split(both[8:16])
    shifted = (
        dot(r_high, root_yz[0]) + dot(r_low, root_yz[0]) + dot(r_high, root_yz[1])
    )[0:6]

    part[0] = own_box
    part[1] = shifted
    recv_box[s] = own_box
    box_copies = [
        send(
            part.at[0],
            recv_box.at[s],
            box_send.at[k],
            box_recv.at[k],
            (m, lax.rem(s + 1 + k, SIBS)),
        )
        for k in range(SIBS - 1)
    ]
    at_a = x_at * SIBS + s
    z_at = lax.div(zc_at, CORES)
    from_core = []
    for k in range(CORES):
        copies = []
        for n, (dx, dy) in enumerate(([(0, 0)] if k == 0 else []) + a_steps):
            to = (lax.rem(x_at + dx, X_SIZE) * ZC + zc_at + 1 - core, lax.rem(s + dy, SIBS))
            copies.append(
                send(part.at[1], recv_a.at[k, at_a], a_send.at[k, n], a_recv.at[k, n], to)
            )
        from_core.append(copies)
    b_steps = [CORES * k for k in range(1, Z_SIZE)] + [CORES * k + 1 for k in range(Z_SIZE)]
    b_copies = [
        send(
            sum_b,
            recv_b.at[z_at],
            b_send.at[k],
            b_recv.at[k],
            (x_at * ZC + lax.rem(CORES * z_at + 1 + step, ZC), s),
        )
        for k, step in enumerate(b_steps)
    ]
    to_core_1, to_core_0 = b_copies[: Z_SIZE - 1], b_copies[Z_SIZE - 1 :]

    @pl.when(core == 0)
    def _():
        for copy in from_core[0]:
            copy.start()

    @pl.when(core == 1)
    def _():
        recv_a[1, at_a] = shifted
        for copy in from_core[1]:
            copy.start()

    for copy in box_copies:
        copy.start()

    for copy in box_copies:
        copy.wait_recv()
    box = recv_box[0]
    for k in range(1, SIBS):
        box = box + recv_box[k]
    tall[...] = jnp.zeros_like(tall)
    tall[0:6, :] = box
    flat_rows(tall[...], flat.at[0])
    box_out = pltpu.make_async_copy(flat.at[0], box_out_ref, out_sem.at[2])
    box_out.start()

    @pl.when(core == 1)
    def _():
        for copies in from_core:
            for copy in copies:
                copy.wait_recv()
        plane = recv_a[0, 0] + recv_a[1, 0]
        for k in range(1, X_SIZE * SIBS):
            plane = plane + (recv_a[0, k] + recv_a[1, k])
        sum_b[...] = plane
        recv_b[z_at] = plane
        for copy in b_copies:
            copy.start()
        for copy in to_core_1:
            copy.wait_recv()

    @pl.when(core == 0)
    def _():
        for copy in to_core_0:
            copy.wait_recv()

    total = recv_b[0]
    for k in range(1, Z_SIZE):
        total = total + recv_b[k]
    tall[0:6, :] = total
    flat_rows(tall[...], flat.at[1])
    root_out = pltpu.make_async_copy(flat.at[1], root_out_ref, out_sem.at[3])
    root_out.start()

    for copy in ups + downs + forwards + chips + box_copies:
        copy.wait_send()

    @pl.when(linked)
    def _():
        links[0].wait_send()

    @pl.when((core == 0) & linked)
    def _():
        for copy in relays + from_up + from_down:
            copy.wait_send()

    @pl.when((core == 1) & linked)
    def _():
        for copy in links[1:]:
            copy.wait_send()

    @pl.when(core == 0)
    def _():
        for copy in from_core[0]:
            copy.wait_send()

    @pl.when(core == 1)
    def _():
        for copy in from_core[1] + b_copies:
            copy.wait_send()

    mass_out.wait()
    force_out.wait()
    box_out.wait()
    root_out.wait()


def finish(force, mass, box, root, force_out, mass_out, box_out, root_out, sem):
    pairs = [(force.at[k], force_out.at[k]) for k in range(3)]
    pairs += [(mass, mass_out), (box, box_out), (root, root_out)]
    copies = [pltpu.make_async_copy(a, b, sem.at[k]) for k, (a, b) in enumerate(pairs)]
    for copy in copies:
        copy.start()
    for copy in copies:
        copy.wait()


def on_device(velocity, pressure, viscosity, levels, morton_keys, counts, neighbors):
    diff, pick, spread, sides, shift, vander, small, tail = tables()
    as_bf16 = lambda a: jnp.asarray(a.astype(np.float32)).astype(BF16)
    vander32 = vander.astype(np.float32)
    v_high = vander32.astype(jnp.bfloat16)
    v_low = (vander32 - v_high.astype(np.float32)).astype(jnp.bfloat16)
    vand = np.stack([v_high, v_low])
    dma = pltpu.SemaphoreType.DMA
    any_space = pl.BlockSpec(memory_space=pl.ANY)
    hbm = pl.BlockSpec(memory_space=pltpu.HBM)
    results = (
        jax.ShapeDtypeStruct((3, LEAVES, NODES), F32),
        jax.ShapeDtypeStruct((LEAVES, NODES), F32),
        jax.ShapeDtypeStruct((3, 1, MOMENTS), F32),
        jax.ShapeDtypeStruct((3, 1, MOMENTS), F32),
    )
    raw = pl.pallas_call(
        functools.partial(kernel, tail),
        out_shape=tuple(pltpu.VMEM(r.shape, r.dtype) for r in results),
        in_specs=[hbm] * 14,
        out_specs=(any_space,) * 4,
        scratch_shapes=[
            pltpu.VMEM((4, LEAVES, NODES), BF16),
            pltpu.VMEM((NODES, 2 * TILE), BF16),
            pltpu.SMEM((MORTONS * SIBS,), jnp.int32),
            pltpu.VMEM((6, LEAVES), jnp.int32),
            pltpu.VMEM((3, NODES, NODES), BF16),
            pltpu.VMEM((LEAVES, NODES), F32),
            pltpu.VMEM((MASK_AT + 21, 8, TILE), F32),
            pltpu.VMEM((1, LEAVES), jnp.int32),
            pltpu.VMEM((1, LEAVES), jnp.int32),
            pltpu.VMEM((6 * TILE, NODES), BF16),
            pltpu.VMEM((6, 16, LANES), BF16),
            pltpu.VMEM((3, TILE, TILE), F32),
            pltpu.VMEM((2, ORDERS, NODES), BF16),
            pltpu.VMEM((ROWS, LANES), BF16),
            pltpu.VMEM((BAND, LANES), BF16),
            pltpu.VMEM((4, BAND, LANES), BF16),
            pltpu.VMEM((3, 4 * LEAVES, NODES), F32),
            pltpu.VMEM((3, LEAVES, NODES), F32),
            pltpu.VMEM((3, LEAVES, LANES), BF16),
            pltpu.VMEM((3, LEAVES, NODES), F32),
            pltpu.VMEM((LEAVES, NODES), F32),
            pltpu.VMEM((LEAVES, LEAVES), F32),
            pltpu.VMEM((LEAVES, NODES), F32),
            pltpu.VMEM((3 * LEAVES, NODES), BF16),
            pltpu.VMEM((3 * LEAVES, NODES), BF16),
            pltpu.VMEM((32, 6 * TILE), BF16),
            pltpu.VMEM((2, TILE, TILE), BF16),
            pltpu.VMEM((TILE, 6 * TILE), F32),
            pltpu.VMEM((2, 6, TILE), F32),
            pltpu.VMEM((SIBS, 6, TILE), F32),
            pltpu.VMEM((CORES, X_SIZE * SIBS, 6, TILE), F32),
            pltpu.VMEM((Z_SIZE, 6, TILE), F32),
            pltpu.VMEM((6, TILE), F32),
            pltpu.VMEM((8, TILE), F32),
            pltpu.VMEM((2, 3, 1, MOMENTS), F32),
            dma((19,)),
            dma((4,)),
            dma((2, 4)),
            dma((2, 4)),
            dma((4,)),
            dma((4,)),
            dma((3,)),
            dma((3,)),
            dma((2,)),
            dma((2,)),
            dma((4,)),
            dma((4,)),
            dma((4,)),
            dma((3,)),
            dma((3,)),
            dma((CORES, 16)),
            dma((CORES, 16)),
            dma((15,)),
            dma((15,)),
            pltpu.SemaphoreType.REGULAR((ROUNDS,)),
        ],
        compiler_params=pltpu.CompilerParams(
            collective_id=0, has_side_effects=True, vmem_limit_bytes=60 * 2**20
        ),
    )(
        velocity.transpose(1, 0, 2),
        as_bf16(pick),
        counts,
        neighbors.T,
        pressure,
        as_bf16(diff),
        viscosity,
        jnp.asarray(small.astype(np.float32)),
        levels.reshape(1, LEAVES),
        morton_keys.reshape(1, LEAVES),
        as_bf16(spread),
        as_bf16(sides),
        jnp.asarray(shift.astype(np.float32)),
        jnp.asarray(vand),
    )
    force, mass, box, root = pl.pallas_call(
        finish,
        out_shape=results,
        in_specs=[any_space] * 4,
        out_specs=(any_space,) * 4,
        scratch_shapes=[dma((6,))],
    )(*[pltpu.with_memory_space_constraint(r, pltpu.VMEM) for r in raw])
    return (
        force.transpose(1, 0, 2),
        mass,
        box.transpose(1, 0, 2),
        root.transpose(1, 0, 2),
    )


def solution(mesh):
    in_specs = (
        P(("morton", "sib"), None, None),
        P(("morton", "sib"), None),
        P(("morton", "sib"), None),
        P(("morton", "sib")),
        P(("morton", "sib")),
        P(),
        P(("morton", "sib"), None),
    )
    out_specs = (
        P(("morton", "sib"), None, None),
        P(("morton", "sib"), None),
        P("morton", None, None),
        P("morton", None, None),
    )
    return jax.shard_map(
        on_device, mesh=mesh, in_specs=in_specs, out_specs=out_specs, check_vma=False
    )
```
